32 devices in a mesh: dp: 8 (over y, x, core), tensor: 4 (over z).
Axes of the slice: x: 2, y: 2, z: 4, core: 2. Of those that a mesh axis runs over, the one named last changes fastest.
Arguments:
- tokens: bfloat16 [8192, 2048], P('dp', 'tensor'), may hold values from -36 to 36
- norm_one_gain: bfloat16 [2048], P('tensor'), may hold values from 0.25 to 1.75
- norm_one_shift: bfloat16 [2048], P('tensor'), may hold values from -4 to 4
- project_weight: bfloat16 [2048, 3, 2048], P(None, None, 'tensor'), may hold values from -0.125 to 0.125
- project_bias: bfloat16 [3, 2048], P(None, 'tensor'), may hold values from -6 to 6
- output_weight: bfloat16 [2048, 2048], P('tensor'), may hold values from -0.5 to 0.5
- norm_two_gain: bfloat16 [2048], P('tensor'), may hold values from 0.25 to 1.75
- norm_two_shift: bfloat16 [2048], P('tensor'), may hold values from -4 to 4
- gate_up_weight: bfloat16 [2048, 2, 5632], P(None, None, 'tensor'), may hold values from -0.125 to 0.125
- down_weight: bfloat16 [5632, 2048], P('tensor'), may hold values from -0.078125 to 0.078125
- cotangent: bfloat16 [8192, 2048], P('dp', 'tensor'), may hold values from -6 to 6
Outputs:
- result: bfloat16 [8192, 2048], P('dp', 'tensor')
- tokens_grad: float32 [8192, 2048], P('dp', 'tensor')
- norm_one_gain_grad: float32 [2048], P('tensor')
- norm_one_shift_grad: float32 [2048], P('tensor')
- project_weight_grad: float32 [2048, 3, 2048], P(None, None, 'tensor')
- project_bias_grad: float32 [3, 2048], P(None, 'tensor')
- output_weight_grad: float32 [2048, 2048], P('tensor')
- norm_two_gain_grad: float32 [2048], P('tensor')
- norm_two_shift_grad: float32 [2048], P('tensor')
- gate_up_weight_grad: float32 [2048, 2, 5632], P(None, None, 'tensor')
- down_weight_grad: float32 [5632, 2048], P('tensor')
The draws below stay inside these ranges and needn't reach their ends.
All inputs are finite; a program needn't handle non-finite values.
Results may differ from the reference program's by a relative error of at most 0.013.
Values may be sent and summed in bfloat16 or wider, within the bound.
No kernel may reach another device: no remote copies, remote signals or barrier semaphores. Data moves between devices by JAX's collectives and lax.ppermute only.
A program may use at most 320 MiB of HBM per device.

```python
import math
import jax
import jax.numpy as jnp
from jax import lax

D = 2048
HEADS = 32
FF = 5632
HEAD_DIM = 64
ROT = 16
SEQ = 1024
TOKENS = 8192


def draw_tokens(key, part):
    key = jax.random.fold_in(key, 11)
    row_key, column_key, value_key = jax.random.split(key, 3)
    row_scale = jnp.exp(jax.random.uniform(row_key, (TOKENS, 1), jnp.float32, math.log(0.3), math.log(3.0)))
    column_scale = jnp.exp(jax.random.uniform(column_key, (1, D), jnp.float32, math.log(0.3), math.log(3.0)))
    base_values = jax.random.truncated_normal(value_key, -4.0, 4.0, (TOKENS, D), jnp.float32)
    return (base_values * row_scale * column_scale).astype(jnp.bfloat16)


def level_of(own_key, shape, pieces, low, high):
    def one(position, parts):
        draws = jax.random.uniform(jax.random.fold_in(jax.random.fold_in(own_key, 6), position), (parts,), jnp.float32, low / len(pieces), high / len(pieces))
        return jnp.repeat(jnp.exp(draws), shape[position] // parts).reshape((-1,) + (1,) * (len(shape) - position - 1))

    gain = one(*pieces[0])
    for cut in pieces[1:]:
        gain = gain * one(*cut)
    return gain


def normal_values(key, extent, width, reach, cuts=(), kind=jnp.bfloat16):
    factor_of = level_of(key, extent, cuts, -0.22, 0.18) if cuts else 1.0
    entries = jax.random.normal(key, extent, jnp.float32) * width * factor_of
    return jnp.minimum(jnp.maximum(entries, -reach), reach).astype(kind)


def setup_inputs(seed: int = 0) -> dict:
    keys = jax.random.split(jax.random.key(seed), 12)
    return {
        "tokens": draw_tokens(jax.random.fold_in(keys[11], 71), 0),
        "norm_one_gain": jnp.clip(1.0 + 0.15 * jax.random.normal(keys[1], (D,), jnp.float32), 0.25, 1.75).astype(jnp.bfloat16),
        "norm_one_shift": normal_values(keys[2], (D,), 0.3, 4.0, ((0, 4),)),
        "project_weight": normal_values(keys[3], (D, 3, D), D ** -0.5, 0.125, ((2, 4),)),
        "project_bias": normal_values(keys[4], (3, D), 0.5, 6.0, ((1, 4),)),
        "output_weight": normal_values(keys[5], (D, D), (D // 16) ** -0.5, 0.5, ((0, 4),)),
        "norm_two_gain": jnp.clip(1.0 + 0.15 * jax.random.normal(keys[6], (D,), jnp.float32), 0.25, 1.75).astype(jnp.bfloat16),
        "norm_two_shift": normal_values(keys[7], (D,), 0.3, 4.0, ((0, 4),)),
        "gate_up_weight": normal_values(keys[8], (D, 2, FF), D ** -0.5, 0.125, ((2, 4),)),
        "down_weight": normal_values(keys[9], (FF, D), FF ** -0.5, 0.078125, ((0, 4),)),
        "cotangent": normal_values(keys[10], (TOKENS, D), 1.0, 6.0, ((0, 8), (1, 4))),
    }


@jax.custom_vjp
def low(v):
    return lax.optimization_barrier(v.astype(jnp.bfloat16)).astype(jnp.float32)

@jax.custom_vjp
def low_back(v):
    return v

def low_keep(v):
    return (low(v), None)

def low_pass(kept, grad):
    return (grad,)

def back_keep(v):
    return (v, None)

def back_low(kept, grad):
    return (low(grad),)
low.defvjp(low_keep, low_pass)
low_back.defvjp(back_keep, back_low)
EPSILON = 1e-05
ROPE_BASE = 10000.0
HIGHEST_PRECISION = lax.Precision.HIGHEST

def layer_norm(values, gain_full, shift_full):
    row_mean = lax.optimization_barrier(jnp.mean(values, axis=-1, keepdims=True))
    centered = values - row_mean
    inverse = lax.rsqrt(lax.optimization_barrier(jnp.mean(centered * centered, axis=-1, keepdims=True)) + EPSILON)
    return centered * inverse * gain_full + shift_full

def rotary_tables(length):
    half_rot = ROT // 2
    positions = jnp.arange(length, dtype=jnp.float32)[:, None]
    exponent = jnp.arange(half_rot, dtype=jnp.float32)[None, :] * (2.0 / ROT)
    angles = positions * ROPE_BASE ** (-exponent)
    return (jnp.cos(angles)[:, None, :], jnp.sin(angles)[:, None, :])

def rotate(heads_in, cosine_table, sine_table):
    half_rot = ROT // 2
    first_half = heads_in[..., :half_rot]
    second = heads_in[..., half_rot:ROT]
    return jnp.concatenate([first_half * cosine_table - second * sine_table, second * cosine_table + first_half * sine_table, heads_in[..., ROT:]], axis=-1)

def attention(query_heads, key_heads, value_heads):
    block_rows = min(512, SEQ)
    score_scale = HEAD_DIM ** (-0.5)

    def one_block(number):
        start_row = number * block_rows
        query_block = lax.dynamic_slice_in_dim(query_heads, start_row, block_rows, 0)
        scores = low_back(jnp.einsum('qhc,khc->hqk', query_block, key_heads, precision=HIGHEST_PRECISION) * score_scale)
        row_index = start_row + jnp.arange(block_rows, dtype=jnp.int32)[:, None]
        column_index = jnp.arange(SEQ, dtype=jnp.int32)[None, :]
        scores = jnp.where(column_index <= row_index, scores, -1000000000.0)
        maximum = lax.optimization_barrier(jnp.max(scores, axis=-1, keepdims=True))
        raised = jnp.exp(scores - maximum)
        weights = raised / lax.optimization_barrier(jnp.sum(raised, axis=-1, keepdims=True))
        return jnp.einsum('hqk,khc->qhc', low(weights), value_heads, precision=HIGHEST_PRECISION)
    blocks = lax.map(jax.checkpoint(one_block), jnp.arange(SEQ // block_rows, dtype=jnp.int32))
    return blocks.reshape(SEQ, HEADS, HEAD_DIM)

def forward(inputs, norm_one_gain, norm_one_shift, project_weight, project_bias, output_weight, norm_two_gain, norm_two_shift, gate_up_weight, down_weight):
    normed_one = low(layer_norm(inputs, norm_one_gain, norm_one_shift))
    project = low_back(jnp.einsum('td,dkc->tkc', normed_one, project_weight, precision=HIGHEST_PRECISION) + project_bias)
    project = project.reshape(SEQ, 3, HEADS, HEAD_DIM)
    cosine_table, sine_table = rotary_tables(SEQ)
    query_heads = low(rotate(project[:, 0], cosine_table, sine_table))
    key_heads = low(rotate(project[:, 1], cosine_table, sine_table))
    value_heads = low(project[:, 2])
    context = attention(query_heads, key_heads, value_heads).reshape(SEQ, D)
    context = low(low_back(context))
    branch = low_back(jnp.dot(context, output_weight, precision=HIGHEST_PRECISION))
    middle = inputs + branch
    normed_two = low(layer_norm(middle, norm_two_gain, norm_two_shift))
    gate_up = low_back(jnp.einsum('td,dkf->tkf', normed_two, gate_up_weight, precision=HIGHEST_PRECISION))
    gate_pre = gate_up[:, 0]
    hidden = low(gate_pre * jax.nn.sigmoid(gate_pre) * gate_up[:, 1])
    return middle + jnp.dot(hidden, down_weight, precision=HIGHEST_PRECISION)

def reference(tokens, norm_one_gain, norm_one_shift, project_weight, project_bias, output_weight, norm_two_gain, norm_two_shift, gate_up_weight, down_weight, cotangent):
    weights = tuple((item.astype(jnp.float32) for item in (norm_one_gain, norm_one_shift, project_weight, project_bias, output_weight, norm_two_gain, norm_two_shift, gate_up_weight, down_weight)))
    token_seqs = tokens.astype(jnp.float32).reshape(TOKENS // SEQ, SEQ, D)
    upstream_seqs = cotangent.astype(jnp.float32).reshape(TOKENS // SEQ, SEQ, D)

    def one_sequence(totals, pair):
        outcome, pullback = jax.vjp(forward, pair[0], *weights)
        gradients = pullback(pair[1])
        new_totals = tuple((total_item + new_item for total_item, new_item in zip(totals, gradients[1:])))
        return (new_totals, (outcome.astype(jnp.bfloat16), gradients[0]))
    zeros_start = tuple((jnp.zeros_like(item) for item in weights))
    totals, (outcomes, input_grads) = lax.scan(one_sequence, zeros_start, (token_seqs, upstream_seqs))
    return (outcomes.reshape(TOKENS, D), input_grads.reshape(TOKENS, D), totals[0], totals[1], totals[2], totals[3], totals[4], totals[5], totals[6], totals[7], totals[8])
```

```python
import functools

import jax
import jax.numpy as jnp
from jax import lax
from jax.experimental import pallas as pl
from jax.experimental.pallas import tpu as pltpu
from jax.sharding import PartitionSpec as P

D = 2048
HEAD_DIM = 64
ROT = 16
SEQ = 1024
PAIR = 2 * HEAD_DIM
CHUNKS = 1
SUB = 256
LIGHT = 64
EXTRA = 16

EPSILON = 1e-05
ROPE_BASE = 10000.0
BF = jnp.bfloat16
F32 = jnp.float32
NT = (((1,), (1,)), ((), ()))
TN = (((0,), (0,)), ((), ()))
ANY = pl.BlockSpec(memory_space=pl.ANY)


def dot(a, b, dims=(((1,), (0,)), ((), ()))):
    return lax.dot_general(a, b, dims, preferred_element_type=F32)


def params(mib):
    return pltpu.CompilerParams(vmem_limit_bytes=mib << 20)


def cost(flops, nbytes):
    return pl.CostEstimate(flops=int(flops) // LIGHT, bytes_accessed=int(nbytes) // LIGHT, transcendentals=0)


def after(value, *others):
    return lax.optimization_barrier((value, *others))[0]


def kernel_call(body, grid, ins, in_specs, outs, out_specs, previous=(), scratch=(), mib=56, flops=0, name=None, weight=1):
    given = len(ins)
    previous = dict(previous)
    aliases = {given + i: out for i, out in enumerate(previous)}

    def run(*refs):
        body(*refs[:given], *refs[given + len(previous) :])

    nbytes = sum(a.size * a.dtype.itemsize for a in ins) + sum(o.size * o.dtype.itemsize for o in outs)
    return pl.pallas_call(
        run,
        grid=grid,
        in_specs=list(in_specs) + [ANY] * len(previous),
        out_specs=list(out_specs),
        out_shape=list(outs),
        input_output_aliases=aliases,
        scratch_shapes=list(scratch),
        compiler_params=params(mib),
        cost_estimate=cost(weight * flops, nbytes),
        name=name,
    )(*ins, *previous.values())


def still(block, index):
    return pl.BlockSpec(block, index, pipeline_mode=pl.Buffered(1))


def sds(shape, dtype):
    return jax.ShapeDtypeStruct(shape, dtype)


def prefetched(body, scalars, grid, ins, in_specs, outs, out_specs, mib=56, flops=0, name=None):
    nbytes = sum(a.size * a.dtype.itemsize for a in ins) + sum(o.size * o.dtype.itemsize for o in outs)
    return pl.pallas_call(
        body,
        grid_spec=pltpu.PrefetchScalarGridSpec(
            num_scalar_prefetch=1, grid=grid, in_specs=in_specs, out_specs=out_specs
        ),
        out_shape=outs,
        compiler_params=params(mib),
        cost_estimate=cost(flops, nbytes),
        name=name,
    )(jnp.stack(scalars).astype(jnp.int32), *ins)


def norm_rows(x_ref, gain, shift, normed_ref, stats_ref, rows=64):
    def step(i, carry):
        at = pl.ds(pl.multiple_of(i * rows, rows), rows)
        x = x_ref[at, :].astype(F32)
        mean = jnp.mean(x, axis=-1, keepdims=True)
        centered = x - mean
        inverse = lax.rsqrt(jnp.mean(centered * centered, axis=-1, keepdims=True) + EPSILON)
        normed_ref[at, :] = (centered * inverse * gain + shift).astype(BF)
        lane = lax.broadcasted_iota(jnp.int32, (rows, 128), 1)
        stats_ref[at, :] = jnp.where(lane == 0, mean, inverse)
        return carry

    lax.fori_loop(0, x_ref.shape[0] // rows, step, 0)


def rope_tables():
    lane = jnp.arange(PAIR, dtype=jnp.int32)[None, :] % HEAD_DIM
    half = ROT // 2
    index = (lane % half).astype(F32)
    angles = jnp.arange(SEQ, dtype=F32)[:, None] * ROPE_BASE ** (-(index * (2.0 / ROT)))
    turned = lane < ROT
    cosine = jnp.where(turned, jnp.cos(angles), 1.0)
    low = jnp.where(turned & (lane >= half), jnp.sin(angles), 0.0)
    high = jnp.where(lane < half, -jnp.sin(angles), 0.0)
    return jnp.stack([cosine, low, high])


def turn(values, table):
    half = ROT // 2
    return (
        values * table[0]
        + pltpu.roll(values, half, 1) * table[1]
        + pltpu.roll(values, values.shape[1] - half, 1) * table[2]
    )


def turn_back(values, table):
    half = ROT // 2
    return (
        values * table[0]
        - pltpu.roll(values, half, 1) * table[1]
        - pltpu.roll(values, values.shape[1] - half, 1) * table[2]
    )


def project_body(x_ref, small_ref, weight_ref, bias_ref, table_ref, normed_ref, stats_ref, heads_ref):
    part = pl.program_id(0)

    @pl.when(part == 0)
    def _():
        gain, shift = (small_ref[k : k + 1, :].astype(F32) for k in (0, 1))
        norm_rows(x_ref, gain, shift, normed_ref, stats_ref)

    out = dot(normed_ref[...], weight_ref[0]) + bias_ref[0]
    width = out.shape[1]

    @pl.when(part < 2)
    def _():
        table = table_ref[...]
        for p in range(width // PAIR):
            heads_ref[0, :, p * PAIR : (p + 1) * PAIR] = turn(out[:, p * PAIR : (p + 1) * PAIR], table).astype(BF)

    @pl.when(part == 2)
    def _():
        heads_ref[0] = out.astype(BF)


def project(c, x, weight, bias, tables, previous):
    t, width = x.shape[0] - EXTRA, weight.shape[2]
    total = t * CHUNKS
    one = lambda k: (0, 0)
    return kernel_call(
        project_body,
        (3,),
        [x, x, weight, bias, tables],
        [
            still((t, D), one),
            pl.BlockSpec((EXTRA, D), lambda k: (t // EXTRA, 0)),
            pl.BlockSpec((1, D, width), lambda k: (k, 0, 0)),
            pl.BlockSpec((1, 1, width), lambda k: (k, 0, 0)),
            still((3, t, PAIR), lambda k: (0, c, 0)),
        ],
        [sds((total, D), BF), sds((total, 128), F32), sds((3, total, width), BF)],
        [
            pl.BlockSpec((t, D), lambda k: (c, 0)),
            pl.BlockSpec((t, 128), lambda k: (c, 0)),
            pl.BlockSpec((1, t, width), lambda k: (k, c, 0)),
        ],
        previous,
        mib=34,
        flops=2 * t * D * 3 * width,
        name="project",
    )


def lane_of(rows):
    return lax.broadcasted_iota(jnp.int32, (rows, PAIR), 1) < HEAD_DIM


def attend_body(c, owners_ref, q_ref, k_ref, v_ref, out_weight_ref, first_ref, rest_ref, ctx_ref, lse_ref):
    pair = pl.program_id(0)
    t = q_ref.shape[1]
    scale = HEAD_DIM ** (-0.5)
    low = lane_of(SUB)
    for r in range(t // SUB):
        start = c * t + r * SUB
        extent = start + SUB
        q = q_ref[0, r * SUB : (r + 1) * SUB, :].astype(F32) * scale
        keys = k_ref[0, :extent, :]
        values = v_ref[0, :extent, :]
        row = start + lax.broadcasted_iota(jnp.int32, (SUB, extent), 0)
        seen = lax.broadcasted_iota(jnp.int32, (SUB, extent), 1) <= row
        contexts, sums = [], []
        for h in range(2):
            own = jnp.where(low if h == 0 else ~low, q, 0.0).astype(BF)
            scores = jnp.where(seen, dot(own, keys, NT), -1000000000.0)
            top = jnp.max(scores, axis=-1, keepdims=True)
            raised = jnp.exp(scores - top)
            total = jnp.sum(raised, axis=-1, keepdims=True)
            contexts.append(dot(raised.astype(BF), values) / total)
            sums.append(top + jnp.log(total))
        at = pl.ds(pl.multiple_of(pair * PAIR, PAIR), PAIR)
        ctx_ref[r * SUB : (r + 1) * SUB, at] = jnp.where(low, contexts[0], contexts[1]).astype(BF)
        lse_ref[r * SUB : (r + 1) * SUB, :] = jnp.where(low, sums[0], sums[1])

    @pl.when(pair == pl.num_programs(0) - 1)
    def _():
        wide = first_ref.shape[1]
        for j in range(D // wide):
            at = pl.ds(pl.multiple_of(owners_ref[j] * wide, wide), wide)
            out = dot(ctx_ref[...], out_weight_ref[:, at]).astype(BF)
            if j == 0:
                first_ref[...] = out
            else:
                rest_ref[:, (j - 1) * wide : j * wide] = out


def attend(owners, heads, out_weight):
    t, width = heads.shape[1], heads.shape[2]
    here = lambda p, owners: (0, p)
    fixed = lambda p, owners: (0, 0)
    return prefetched(
        functools.partial(attend_body, 0),
        owners,
        (width // PAIR,),
        [heads, heads, heads, out_weight],
        [pl.BlockSpec((1, t, PAIR), lambda p, owners, k=k: (k, 0, p)) for k in range(3)]
        + [still((width, D), fixed)],
        [sds((t, width), BF), sds((t, D - width), BF), sds((t, width), BF), sds((t, width), F32)],
        [
            pl.BlockSpec((t, width), fixed),
            pl.BlockSpec((t, D - width), fixed),
            pl.BlockSpec((t, width), fixed),
            pl.BlockSpec((t, PAIR), here),
        ],
        mib=30,
        flops=(8 * t * t * width + 2 * t * width * D) * 4 * LIGHT,
        name="attend",
    )


def attend_back_body(c, *refs):
    q_ref, k_ref, v_ref, lse_ref, ctx_ref, dctx_ref, table_ref, with_ref, dq_ref, dk_ref, dv_ref, sums_ref, dk_sum, dv_sum = refs
    t = q_ref.shape[1]

    @pl.when(pl.program_id(0) == 0)
    def _():
        sums_ref[...] = jnp.zeros_like(sums_ref)

    def row_sums(k, gradient, values, at):
        first = gradient * with_ref[0, k : k + 1, :]
        second = gradient * (values - with_ref[1, k : k + 1, :])
        sums_ref[0:1, at] += jnp.sum(first.T, axis=0, keepdims=True)
        sums_ref[1:2, at] += jnp.sum(second.T, axis=0, keepdims=True)

    scale = HEAD_DIM ** (-0.5)
    low = lane_of(SUB)
    dk_sum[...] = jnp.zeros_like(dk_sum)
    dv_sum[...] = jnp.zeros_like(dv_sum)
    for r in range(t // SUB):
        here = slice(r * SUB, (r + 1) * SUB)
        start = c * t + r * SUB
        extent = start + SUB
        q = q_ref[0, here, :].astype(F32) * scale
        keys = k_ref[0, :extent, :]
        values = v_ref[0, :extent, :]
        dctx = dctx_ref[here, :]
        lse_t = lse_ref[here, :].T
        product_t = (ctx_ref[here, :].astype(F32) * dctx.astype(F32)).T
        low_keys = lane_of(extent)
        column = start + lax.broadcasted_iota(jnp.int32, (extent, SUB), 1)
        seen = lax.broadcasted_iota(jnp.int32, (extent, SUB), 0) <= column
        dq = jnp.zeros((SUB, PAIR), F32)
        for h in range(2):
            own = low if h == 0 else ~low
            q_own = jnp.where(own, q, 0.0).astype(BF)
            dctx_own = jnp.where(own, dctx, jnp.zeros_like(dctx))
            rows = slice(h * HEAD_DIM, (h + 1) * HEAD_DIM)
            row_dot = jnp.sum(product_t[rows, :], axis=0, keepdims=True)
            scores = dot(keys, q_own, NT) - lse_t[h * HEAD_DIM : h * HEAD_DIM + 1, :]
            probs = jnp.where(seen, jnp.exp(scores), 0.0)
            delta_probs = dot(values, dctx_own, NT)
            delta_scores = (probs * (delta_probs - row_dot)).astype(BF)
            dv_sum[:extent, :] += dot(probs.astype(BF), dctx_own)
            dk_sum[:extent, :] += dot(delta_scores, q_own)
            keys_own = jnp.where(low_keys if h == 0 else ~low_keys, keys, jnp.zeros_like(keys))
            dq = dq + dot(delta_scores, keys_own, TN)
        table = table_ref[:, start:extent, :]
        dq = turn_back(dq * scale, table)
        dq_ref[here, :] = dq.astype(BF)
        row_sums(0, dq, turn_back(q_ref[0, here, :].astype(F32), table), here)
    for r in range(t // SUB):
        here = slice(r * SUB, (r + 1) * SUB)
        table = table_ref[:, here, :]
        dk = turn_back(dk_sum[here, :], table)
        dk_ref[here, :] = dk.astype(BF)
        row_sums(1, dk, turn_back(k_ref[0, here, :].astype(F32), table), here)
        dv = dv_sum[here, :]
        dv_ref[here, :] = dv.astype(BF)
        row_sums(2, dv, v_ref[0, here, :].astype(F32), here)


def attend_back(heads, lse, ctx, dctx, tables, with_rows):
    t, width = heads.shape[1], heads.shape[2]
    own = pl.BlockSpec((t, PAIR), lambda p: (0, p))
    return kernel_call(
        functools.partial(attend_back_body, 0),
        (width // PAIR,),
        [heads, heads, heads, lse, ctx, dctx, tables, with_rows],
        [pl.BlockSpec((1, t, PAIR), lambda p, k=k: (k, 0, p)) for k in range(3)]
        + [own, own, own, still((3, t, PAIR), lambda p: (0, 0, 0)), pl.BlockSpec((2, 3, PAIR), lambda p: (0, 0, p))],
        [sds((t, width), BF)] * 3 + [sds((8, t), F32)],
        [own, own, own, pl.BlockSpec((8, t), lambda p: (0, 0))],
        scratch=[pltpu.VMEM((t, PAIR), F32)] * 2,
        mib=28,
        flops=20 * t * t * width,
        name="attend_back",
        weight=4 * LIGHT,
    )


def mlp_body(mid_ref, up_ref, gain_ref, shift_ref, gate_w_ref, up_w_ref, down_w_ref, normed_ref, stats_ref, hidden_ref, dgate_ref, dup_ref):
    @pl.when(pl.program_id(0) == 0)
    def _():
        norm_rows(mid_ref, gain_ref[...], shift_ref[...], normed_ref, stats_ref)

    normed = normed_ref[...]
    gate = dot(normed, gate_w_ref[...])
    upward = dot(normed, up_w_ref[...])
    delta_hidden = dot(up_ref[...], down_w_ref[...], NT)
    sigmoid = jax.nn.sigmoid(gate)
    silu = gate * sigmoid
    hidden_ref[...] = (silu * upward).astype(BF)
    dgate_ref[...] = (delta_hidden * upward * (sigmoid + silu * (1.0 - sigmoid))).astype(BF)
    dup_ref[...] = (delta_hidden * silu).astype(BF)


def mlp(c, mid, upstream, gain, shift, gate_w, up_w, down_w, previous):
    t, units = mid.shape[0], gate_w.shape[1]
    total = t * CHUNKS
    tile = 256
    one = lambda j: (0, 0)
    own = lambda j: (c, 0)
    column = pl.BlockSpec((t, tile), lambda j: (c, j))
    return kernel_call(
        mlp_body,
        (pl.cdiv(units, tile),),
        [mid, upstream, gain, shift, gate_w, up_w, down_w],
        [
            still((t, D), one),
            still((t, D), own),
            pl.BlockSpec((1, D), one),
            pl.BlockSpec((1, D), one),
            pl.BlockSpec((D, tile), lambda j: (0, j)),
            pl.BlockSpec((D, tile), lambda j: (0, j)),
            pl.BlockSpec((tile, D), lambda j: (j, 0)),
        ],
        [sds((total, D), BF), sds((total, 128), F32)] + [sds((total, units), BF)] * 3,
        [pl.BlockSpec((t, D), own), pl.BlockSpec((t, 128), own), column, column, column],
        previous,
        mib=46,
        flops=6 * t * D * units,
        name="mlp",
    )


def mlp_back_body(owners_ref, dgate_ref, dup_ref, gate_w_ref, up_w_ref, out_ref):
    out_ref[...] = (dot(dgate_ref[...], gate_w_ref[...], NT) + dot(dup_ref[...], up_w_ref[...], NT)).astype(BF)


def mlp_back(owners, width, dgate, dup, gate_w, up_w):
    t, units = dgate.shape
    whole = still((t, units), lambda j, owners: (0, 0))
    weight = pl.BlockSpec((width, units), lambda j, owners: (owners[j], 0))
    return prefetched(
        mlp_back_body,
        owners,
        (len(owners),),
        [dgate, dup, gate_w, up_w],
        [whole, whole, weight, weight],
        [sds((t, len(owners) * width), BF)],
        [pl.BlockSpec((t, width), lambda j, owners: (0, j))],
        mib=28,
        flops=4 * t * D * units,
        name="mlp_back",
    )[0]


def branch_back_body(e_ref, mid_ref, stats_ref, up_ref, weight_ref, means_ref, dbranch_ref, dctx_ref):
    rows = 64

    def step(i, carry):
        at = pl.ds(pl.multiple_of(i * rows, rows), rows)
        e = e_ref[at, :].astype(F32)
        mean, inverse = stats_ref[at, 0:1], stats_ref[at, 1:2]
        unit = (mid_ref[at, :].astype(F32) - mean) * inverse
        first = jnp.mean(e, axis=-1, keepdims=True)
        second = jnp.mean(e * unit, axis=-1, keepdims=True)
        dbranch_ref[at, :] = (up_ref[at, :].astype(F32) + inverse * (e - first - unit * second)).astype(BF)
        lane = lax.broadcasted_iota(jnp.int32, (rows, 128), 1)
        means_ref[at, :] = jnp.where(lane == 0, first, second)
        return carry

    lax.fori_loop(0, e_ref.shape[0] // rows, step, 0)
    dctx_ref[...] = dot(dbranch_ref[...], weight_ref[...], NT).astype(BF)


def branch_back(e, mid, stats, upstream, weight):
    t, width = e.shape[0], weight.shape[0]
    tile = SUB
    row = lambda i: (i, 0)
    return kernel_call(
        branch_back_body,
        (t // tile,),
        [e, mid, stats, upstream, weight],
        [
            pl.BlockSpec((tile, D), row),
            pl.BlockSpec((tile, D), row),
            pl.BlockSpec((tile, 128), row),
            pl.BlockSpec((tile, D), row),
            still((width, D), lambda i: (0, 0)),
        ],
        [sds((t, 128), F32), sds((t, D), BF), sds((t, width), BF)],
        [pl.BlockSpec((tile, 128), row), pl.BlockSpec((tile, D), row), pl.BlockSpec((tile, width), row)],
        mib=24,
        flops=2 * t * D * width,
        name="branch_back",
    )


def project_back_body(owners_ref, dq_ref, dk_ref, dv_ref, weight_ref, x_ref, stats_ref, below_ref, out_ref):
    n = dot(dq_ref[...], weight_ref[0], NT) + dot(dk_ref[...], weight_ref[1], NT) + dot(dv_ref[...], weight_ref[2], NT)
    out_ref[: n.shape[0], :] = n.astype(BF)
    unit = (x_ref[...].astype(F32) - stats_ref[:, 0:1]) * stats_ref[:, 1:2]
    with_unit = n * unit
    row = lax.broadcasted_iota(jnp.int32, (EXTRA, n.shape[1]), 0)
    gain_grad = jnp.sum(with_unit, axis=0, keepdims=True)
    shift_grad = jnp.sum(n, axis=0, keepdims=True)
    out_ref[n.shape[0] :, :] = jnp.where(row == 0, gain_grad, jnp.where(row == 1, shift_grad, below_ref[...])).astype(BF)


def project_back(owners, dq, dk, dv, weight, x, stats, below):
    t, width = dq.shape
    count = len(owners)
    whole = still((t, width), lambda j, owners: (0, 0))
    return prefetched(
        project_back_body,
        owners,
        (count,),
        [dq, dk, dv, weight, x, stats, below],
        [
            whole,
            whole,
            whole,
            pl.BlockSpec((3, width, width), lambda j, owners: (0, owners[j], 0)),
            pl.BlockSpec((t, width), lambda j, owners: (0, owners[j])),
            still((t, 128), lambda j, owners: (0, 0)),
            still((EXTRA, width), lambda j, owners: (0, 0)),
        ],
        [sds((t + EXTRA, count * width), BF)],
        [pl.BlockSpec((t + EXTRA, width), lambda j, owners: (0, j))],
        mib=34,
        flops=6 * t * D * width,
        name="project_back",
    )[0]


def add(a, b):
    return (a.astype(F32) + b.astype(F32)).astype(BF)


class Order:
    def __init__(self):
        self.before = ()

    def __call__(self, value):
        return after(value, *self.before) if self.before else value

    def done(self, *values):
        self.before = tuple(values)


class Gather:
    def __init__(self, share):
        self.n = lax.axis_size("tensor")
        self.pieces = [share]
        self.held = {(i, i): 0 for i in range(self.n)}
        self.steps = 0

    def send(self, piece, pairs, order):
        self.pieces.append(lax.ppermute(order(self.pieces[piece]), "tensor", pairs))

    def step(self, order):
        n, s = self.n, self.steps
        self.steps += 1
        before = len(self.pieces)
        if n == 4:
            outer, inner, out = [(0, 1), (1, 0), (2, 3), (3, 2)], [(1, 2), (2, 1)], [(1, 0), (2, 3)]
            for piece, pairs in (((0, outer), (0, inner)), ((2, out), (1, inner)), ((4, out),))[s]:
                self.send(piece, pairs, order)
            owners = ((1, None, 2, None, 3), (0, 2, None, 3, None), (3, 1, None, 0, None), (2, None, 1, None, 0))
            self.held = {(i, i): 0 for i in range(n)} | {
                (i, owner): 1 + k for i, row in enumerate(owners) for k, owner in enumerate(row) if owner is not None
            }
        else:
            up, down = (0, 0) if s == 0 else (before - 2, before - 1)
            self.held.update({(i + 1, i - s): before for i in range(s, n - 1)})
            self.held.update({(i, i + 1 + s): before + 1 for i in range(n - 1 - s)})
            self.send(up, [(i, i + 1) for i in range(s, n - 1)], order)
            self.send(down, [(i + 1, i) for i in range(n - 1 - s)], order)
        return self.pieces[before:]

    def last(self, order):
        got = self.step(order)
        while self.steps < self.n - 1:
            got = self.step(order)
        return got

    def whole(self):
        share = self.pieces[0]
        t, width = share.shape
        return prefetched(
            functools.partial(assemble_body, self.held),
            [lax.axis_index("tensor")],
            (self.n,),
            self.pieces,
            [still((t, width), lambda j, me: (0, 0))] * len(self.pieces),
            [sds((t, self.n * width), share.dtype)],
            [pl.BlockSpec((t, width), lambda j, me: (0, j))],
            mib=14,
            name="assemble",
        )[0]


def scatter_order(n):
    me = lax.axis_index("tensor")
    first = jnp.where(me < n // 2, n - 1, 0)
    return [(first + k) % n for k in range(n)]


class Scatter:
    def __init__(self, first, rest):
        self.n, self.me = lax.axis_size("tensor"), lax.axis_index("tensor")
        self.first, self.rest, self.steps, self.got = first, rest, 0, {}
        self.width = first.shape[1]

    def part(self, owner, *got):
        place = (owner - jnp.where(self.me < self.n // 2, self.n - 1, 0) - 1) % self.n
        place = jnp.clip(place, 0, self.n - 2)
        value = lax.dynamic_slice_in_dim(self.rest, place * self.width, self.width, 1)
        return functools.reduce(add, got, value)

    def any(self, owner, *got):
        first = jnp.where(self.me < self.n // 2, self.n - 1, 0)
        value = jnp.where(owner % self.n == first, self.first, self.part(owner % self.n))
        return functools.reduce(add, got, value)

    def send(self, name, value, pairs, order):
        self.got[name] = lax.ppermute(order(value), "tensor", pairs)

    def step(self, order):
        n, me, s = self.n, self.me, self.steps
        self.got = got = {name: order(value) for name, value in self.got.items()}
        self.steps += 1
        if n == 4:
            inward, inner, outer = [(0, 1), (3, 2)], [(1, 2), (2, 1)], [(0, 1), (1, 0), (2, 3), (3, 2)]
            if s == 0:
                self.send("far", self.first, inward, order)
                return [got["far"]]
            if s == 1:
                self.send("far", add(self.first, got["far"]), inner, order)
                self.send("next", self.part(jnp.where(me == 0, 2, 1)), inward, order)
            else:
                self.send("far", self.part(me ^ 1, got["far"]), outer, order)
                self.send("next", self.part(3 - me, got["next"]), inner, order)
            return [got["far"], got["next"]]
        up, down = ((got["up"],), (got["down"],)) if s else ((), ())
        self.send("up", self.any(me + n - 1 - s, *up), [(i, i + 1) for i in range(s + 1)], order)
        self.send("down", self.any(me - n + 1 + s, *down), [(i + 1, i) for i in range(n - 2 - s, n - 1)], order)
        return [got["up"], got["down"]]

    def last(self, order):
        got = self.step(order)
        while self.steps < self.n - 1:
            got = self.step(order)
        return got

    def total(self):
        own = self.any(self.me) if self.n != 4 else self.part(self.me)
        return sum((g.astype(F32) for g in self.got.values()), own.astype(F32))


def assemble_body(held, me_ref, *refs):
    out_ref, owner, me = refs[-1], pl.program_id(0), me_ref[0]
    for k, ref in enumerate(refs[:-1]):
        places = [(device, o) for (device, o), at in held.items() if at == k]
        here = functools.reduce(jnp.logical_or, [(me == device) & (owner == o) for device, o in places])

        @pl.when(here)
        def _(ref=ref):
            out_ref[...] = ref[...]


def swap(value, bit, axis="dp"):
    n = lax.axis_size(axis)
    return lax.ppermute(value, axis, [(i, i ^ (1 << bit)) for i in range(n)])


def split_body(groups, bits_ref, *refs):
    parts, outs = refs[: 4 * groups], refs[4 * groups :]
    for part in range(2):
        for phase in range(2):

            @pl.when(pl.program_id(0) == phase)
            def _(part=part, phase=phase):
                at = 0
                for g in range(groups):
                    keep, got = parts[2 * (part * groups + g)], parts[2 * (part * groups + g) + 1]
                    wide = keep.shape[1]
                    outs[2 * part + phase][:, at : at + wide] = add(keep[...], got[...])
                    at += wide


def split(upper, lower, bits, joined):
    groups = len(upper)
    rows = upper[0][0].shape[0] // (4 if joined else 2)
    block = min(128, rows)
    nb = rows // block
    columns = sum(keep.shape[1] for keep, _ in upper)
    ins, in_specs = [], []
    for part, pairs in enumerate((upper, lower)):
        first = 2 * nb * part if joined else 0

        def index(phase, j, bits, part=part, first=first):
            half = jnp.where(phase == 0, 1 - bits[part], bits[part])
            return (first + half * nb + j, 0)

        for pair in pairs:
            for array in pair:
                ins.append(array)
                in_specs.append(pl.BlockSpec((block, array.shape[1]), index))
    given = pl.BlockSpec((block, columns), lambda phase, j, bits: (jnp.where(phase == 0, j, nb - 1), 0))
    kept = pl.BlockSpec((block, columns), lambda phase, j, bits: (jnp.where(phase == 0, 0, j), 0))
    return prefetched(
        functools.partial(split_body, groups),
        bits,
        (2, nb),
        ins,
        in_specs,
        [sds((rows, columns), BF)] * 4,
        [given, kept] * 2,
        mib=28,
        name="split",
    )


def merge_body(joined, bits_ref, *refs):
    for part in range(2):
        for which in range(2):

            @pl.when((pl.program_id(0) == bits_ref[part]) == (which == 0))
            def _(part=part, which=which):
                value = refs[2 * part + which][...]
                if joined:
                    refs[4][part] = value
                else:
                    refs[4 + part][...] = value


def merge(upper, lower, bits, joined):
    rows, columns = upper[0].shape
    block = min(128, rows)
    nb = rows // block

    def spec(part, which):
        def index(i, j, bits):
            half = bits[part] if which == 0 else 1 - bits[part]
            return (jnp.where(i == half, j, jnp.where(i < half, 0, nb - 1)), 0)

        return pl.BlockSpec((block, columns), index)

    if joined:
        outs = [sds((2, 2 * rows, columns), BF)]
        out_specs = [pl.BlockSpec((2, block, columns), lambda i, j, bits: (0, i * nb + j, 0))]
    else:
        outs = [sds((2 * rows, columns), BF)] * 2
        out_specs = [pl.BlockSpec((block, columns), lambda i, j, bits: (i * nb + j, 0))] * 2
    return prefetched(
        functools.partial(merge_body, joined),
        bits,
        (2, nb),
        [*upper, *lower],
        [spec(part, which) for part in range(2) for which in range(2)],
        outs,
        out_specs,
        mib=22,
        name="merge",
    )


def sum_over_dp(given, order):
    me, n = lax.axis_index("dp"), lax.axis_size("dp")
    count = n.bit_length() - 1
    bit = lambda b: (me >> b) & 1
    orders = [list(range(1, count)), list(range(count - 1, 0, -1))]
    got = [swap(g, 0) for g in given]
    kept = yield got
    upper = lower = [(order(k), g) for k, g in zip(kept, got)]
    for s in range(count - 1):
        a, b = orders[0][s], orders[1][s]
        p_give, p_keep, q_give, q_keep = split(upper, lower, [bit(a), bit(b)], s == 0)
        upper, lower = [(p_keep, swap(p_give, a))], [(q_keep, swap(q_give, b))]
        yield p_keep
        upper, lower = [(order(upper[0][0]), upper[0][1])], [(order(lower[0][0]), lower[0][1])]
    p, q = add(*upper[0]), add(*lower[0])
    for s in reversed(range(count - 1)):
        a, b = orders[0][s], orders[1][s]
        got = swap(p, a), swap(q, b)
        yield p
        out = merge([order(p), got[0]], [q, got[1]], [bit(a), bit(b)], s == 0)
        if s:
            p, q = out
    own = out[0].reshape(-1, out[0].shape[2])
    other = swap(own, 0)
    yield own
    yield own, other


def halves(core, own, other, nb):
    def index(mine):
        def of(i, bits):
            half = bits[0] if mine else 1 - bits[0]
            return (jnp.clip(i - half * nb, 0, nb - 1), 0)

        return of

    return index(True), index(False)


def mlp_out_body(units, core_ref, own_ref, other_ref, gate_up_ref, down_ref):
    half = pl.program_id(0) // (pl.num_programs(0) // 2)
    for ref, mine in ((own_ref, True), (other_ref, False)):

        @pl.when((half == core_ref[0]) == mine)
        def _(ref=ref):
            gate_up_ref[:, 0, :] = ref[:, :units].astype(F32)
            gate_up_ref[:, 1, :] = ref[:, units : 2 * units].astype(F32)
            down_ref[...] = ref[:, 2 * units :].astype(F32).T


def mlp_out(core, own, other):
    columns = own.shape[1]
    units = columns // 3
    block = 128
    nb = own.shape[0] // block
    mine, theirs = halves(core, own, other, nb)
    return prefetched(
        functools.partial(mlp_out_body, units),
        [core],
        (2 * nb,),
        [own, other],
        [pl.BlockSpec((block, columns), mine), pl.BlockSpec((block, columns), theirs)],
        [sds((D, 2, units), F32), sds((units, D), F32)],
        [pl.BlockSpec((block, 2, units), lambda i, c: (i, 0, 0)), pl.BlockSpec((units, block), lambda i, c: (0, i))],
        mib=26,
        name="mlp_out",
    )


def attention_out_body(width, core_ref, own_ref, other_ref, project_ref, output_ref):
    half = pl.program_id(0) // (pl.num_programs(0) // 2)
    for ref, mine in ((own_ref, True), (other_ref, False)):

        @pl.when((half == core_ref[0]) == mine)
        def _(ref=ref):
            for k in range(3):
                project_ref[k] = ref[:, k * width : (k + 1) * width].astype(F32)
            output_ref[...] = ref[:, 3 * width :].astype(F32).T


def attention_out(core, own, other):
    columns = own.shape[1]
    width = columns // 4
    block = 256
    nb = own.shape[0] // block
    mine, theirs = halves(core, own, other, nb)
    return prefetched(
        functools.partial(attention_out_body, width),
        [core],
        (2 * nb,),
        [own, other],
        [pl.BlockSpec((block, columns), mine), pl.BlockSpec((block, columns), theirs)],
        [sds((3, D, width), F32), sds((width, D), F32)],
        [pl.BlockSpec((3, block, width), lambda i, c: (0, i, 0)), pl.BlockSpec((width, block), lambda i, c: (0, i))],
        mib=22,
        name="attention_out",
    )


def per_device(
    tokens,
    norm_one_gain,
    norm_one_shift,
    project_weight,
    project_bias,
    output_weight,
    norm_two_gain,
    norm_two_shift,
    gate_up_weight,
    down_weight,
    cotangent,
):
    width = tokens.shape[1]
    t = tokens.shape[0] // CHUNKS
    offset = lax.axis_index("tensor") * width
    core = lax.axis_index("dp") & 1
    mine = lambda full: lax.dynamic_slice_in_dim(full, offset, width, full.ndim - 1)
    half_of = lambda array, which: lax.dynamic_slice_in_dim(array, which * (D // 2), D // 2, 1)
    order = Order()

    small = jnp.stack([norm_one_gain, norm_one_shift, norm_two_gain, norm_two_shift])
    whole_x = Gather(jnp.concatenate([tokens, jnp.pad(small, ((0, EXTRA - 4), (0, 0)))]))
    whole_up = Gather(cotangent)
    got = whole_x.step(order)
    gate_w = order(gate_up_weight)[:, 0]
    order.done(*got, gate_w)
    got = whole_x.step(order)
    up_w = order(gate_up_weight)[:, 1]
    order.done(*got, up_w)
    whole_x.last(order)
    tables = rope_tables()
    x = whole_x.whole()
    gain_one, gain_two, shift_two = (x[t + i : t + i + 1].astype(F32) for i in (0, 2, 3))
    project_w = project_weight.transpose(1, 0, 2)
    bias = project_bias.astype(F32)[:, None, :]

    through = lambda row: jnp.einsum("d,kdc->kc", row[0].astype(BF), project_w, preferred_element_type=F32)
    with_rows = jnp.stack([through(gain_one), through(x[t + 1 : t + 2]) + bias[:, 0]])

    order.done(x)
    got = whole_up.step(order)
    normed_one, stats_one, heads = project(0, x, project_w, bias, tables, ())
    order.done(*got, stats_one)
    owners = scatter_order(whole_up.n)
    first, rest, context, lse = attend(owners, order(heads), output_weight)
    order.done(lse)
    branch = Scatter(first, rest)
    for _ in range(2):
        order.done(*whole_up.step(order), *branch.step(order))
    if whole_up.n > 4:
        whole_up.last(order)
    branch.last(order)
    upstream = whole_up.whole()
    middle_share = tokens.astype(F32) + branch.total()
    middle_sent = (middle_share - stats_one[:, 0:1]).astype(BF)
    order.done(middle_sent)
    whole_middle = Gather(middle_sent)
    while whole_middle.steps < whole_middle.n - 1:
        whole_middle.step(order)
    middle = whole_middle.whole()

    normed_two, stats_two, hidden, dgate, dup = mlp(
        0, middle, upstream, gain_two, shift_two, gate_w, up_w, down_weight, ()
    )
    first = mlp_back(owners[:1], width, dgate, dup, gate_w, up_w)
    rest = mlp_back(owners[1:], width, after(dgate, first), dup, gate_w, up_w)
    order.done(first)
    delta_two = Scatter(first, rest)
    got = delta_two.step(order)
    order.done(rest)
    mlp_half = lambda which: [
        dot(half_of(normed_two, which), order(jnp.concatenate([dgate, dup], axis=1)), TN).astype(BF),
        dot(half_of(upstream, which), order(hidden), TN).astype(BF),
    ]
    mlp_given = mlp_half(1 - core)
    mlp_sum = sum_over_dp(mlp_given, order)
    next(mlp_sum)
    order.done(*got, *mlp_given)
    got = delta_two.step(order)
    mlp_kept = mlp_half(core)
    order.done(*mlp_kept)
    held = mlp_sum.send(mlp_kept)
    order.done(*got, held)
    got = delta_two.last(order)
    mlp_parts = dot(order(hidden), down_weight).astype(BF)
    order.done(*got, mlp_parts)
    delta_two = order(delta_two.total())
    unit_two = (mine(middle).astype(F32) - stats_two[:, 0:1]) * stats_two[:, 1:2]
    two_grads = [jnp.sum(delta_two * unit_two, axis=0), jnp.sum(delta_two, axis=0)]
    e_own = delta_two * norm_two_gain.astype(F32)
    e_sent = e_own.astype(BF)
    order.done(e_sent)
    whole_e = Gather(e_sent)
    got = whole_e.step(order)
    held = next(mlp_sum)
    piece = lambda owner: lax.dynamic_slice_in_dim(mlp_parts, owner * width, width, 1)
    mlp_share = Scatter(piece(owners[0]), jnp.concatenate([piece(owner) for owner in owners[1:]], axis=1))
    order.done(*got, held, mlp_share.rest)
    got = whole_e.step(order) + mlp_share.step(order)
    order.done(*got)
    got = whole_e.last(order) + mlp_share.step(order)
    held = next(mlp_sum)
    e = whole_e.whole()

    order.done(e, held, *got)
    mlp_share.last(order)
    means_two, dbranch, dctx = branch_back(order(e), middle, stats_two, upstream, output_weight)
    order.done(dctx)
    dq, dk, dv, sums = attend_back(heads, lse, context, order(dctx), tables, with_rows)
    order.done(dq)
    mlp_share.got = {name: order(value) for name, value in mlp_share.got.items()}
    result = (middle_share + mlp_share.total()).astype(BF)
    held = next(mlp_sum)
    order.done(held, result)
    delta_heads = (dq, dk, dv)
    attention_half = lambda which: [
        dot(half_of(normed_one, which), order(jnp.concatenate(delta_heads, axis=1)), TN).astype(BF),
        dot(half_of(dbranch, which), order(context), TN).astype(BF),
    ]
    attention_given = attention_half(1 - core)
    attention_sum = sum_over_dp(attention_given, order)
    next(attention_sum)
    sum_rows = 2 * t // width
    below = jnp.pad(sums[:2].reshape(sum_rows, width), ((2, EXTRA - 2 - sum_rows), (0, 0)))
    order.done(*attention_given, below)
    back = lambda owners, dq: project_back(owners, dq, dk, dv, project_w, x, stats_one, below)
    first = back(owners[:1], order(dq))
    rest = back(owners[1:], after(dq, first))
    order.done(first)
    delta_one = Scatter(first, rest)
    got = delta_one.step(order)
    order.done(rest)
    attention_kept = attention_half(core)
    order.done(*attention_kept)
    held = attention_sum.send(attention_kept)
    order.done(held, *got)
    got = delta_one.step(order)
    held = next(mlp_sum)
    order.done(held)
    if lax.axis_size("dp") > 8:
        for _ in range(2):
            order.done(next(mlp_sum))
            order.done(next(attention_sum))
    held = next(attention_sum)
    order.done(held, *got)
    got = delta_one.last(order)
    held = next(attention_sum)
    order.done(held, *got)
    mlp_halves = next(mlp_sum)
    gate_up_grad, down_grad = mlp_out(core, order(mlp_halves[0]), mlp_halves[1])
    order.done(down_grad)
    delta_one = order(delta_one.total())
    bias_grad = [jnp.sum(a, axis=0, dtype=F32) for a in delta_heads]
    small = jnp.stack([delta_one[t], delta_one[t + 1], *two_grads, *bias_grad])
    devices = lax.axis_size("dp")
    others = [lax.ppermute(order(small), "dp", [(i, i ^ k) for i in range(devices)]) for k in range(1, devices)]
    held = next(attention_sum)
    order.done(held)
    sums = (delta_one[t + 2 : t + 2 + sum_rows] / D).reshape(2, t).T
    unit_one = (tokens.astype(F32) - stats_one[:, 0:1]) * stats_one[:, 1:2]
    dmid = cotangent.astype(F32) + stats_two[:, 1:2] * (e_own - means_two[:, 0:1] - unit_two * means_two[:, 1:2])
    tokens_grad = order(dmid) + stats_one[:, 1:2] * (
        delta_one[:t] * norm_one_gain.astype(F32) - sums[:, 0:1] - unit_one * sums[:, 1:2]
    )
    order.done(tokens_grad)
    small = sum((order(other) for other in others), small)
    order.done(small)
    held = next(attention_sum)
    order.done(held)
    attention_halves = next(attention_sum)
    project_grad, output_grad = attention_out(core, order(attention_halves[0]), attention_halves[1])
    return (
        result,
        tokens_grad,
        small[0],
        small[1],
        project_grad.transpose(1, 0, 2),
        small[4:7],
        output_grad,
        small[2],
        small[3],
        gate_up_grad,
        down_grad,
    )


def solution(mesh):
    return jax.shard_map(
        per_device,
        mesh=mesh,
        in_specs=(
            P("dp", "tensor"),
            P("tensor"),
            P("tensor"),
            P(None, None, "tensor"),
            P(None, "tensor"),
            P("tensor", None),
            P("tensor"),
            P("tensor"),
            P(None, None, "tensor"),
            P("tensor", None),
            P("dp", "tensor"),
        ),
        out_specs=(
            P("dp", "tensor"),
            P("dp", "tensor"),
            P("tensor"),
            P("tensor"),
            P(None, None, "tensor"),
            P(None, "tensor"),
            P("tensor", None),
            P("tensor"),
            P("tensor"),
            P(None, None, "tensor"),
            P("tensor", None),
        ),
        check_vma=False,
    )
```

```python
import functools

import jax
import jax.numpy as jnp
from jax import lax
from jax.experimental import pallas as pl
from jax.experimental.pallas import tpu as pltpu
from jax.sharding import PartitionSpec as P

D = 2048
HEAD_DIM = 64
ROT = 16
SEQ = 1024
PAIR = 2 * HEAD_DIM
CHUNKS = 1
SUB = 256
WEIGHTS = {"mlp_kept": 30}
EXTRA = 16

EPSILON = 1e-05
ROPE_BASE = 10000.0
BF = jnp.bfloat16
F32 = jnp.float32
NT = (((1,), (1,)), ((), ()))
TN = (((0,), (0,)), ((), ()))
ANY = pl.BlockSpec(memory_space=pl.ANY)


def dot(a, b, dims=(((1,), (0,)), ((), ()))):
    return lax.dot_general(a, b, dims, preferred_element_type=F32)


def params(mib):
    return pltpu.CompilerParams(vmem_limit_bytes=mib << 20)


def cost(name):
    return pl.CostEstimate(flops=int(WEIGHTS.get(name, 0) * 1e9), bytes_accessed=0, transcendentals=0)


def after(value, *others):
    return lax.optimization_barrier((value, *others))[0]


def kernel_call(body, grid, ins, in_specs, outs, out_specs, previous=(), scratch=(), mib=56, name=None):
    given = len(ins)
    previous = dict(previous)
    aliases = {given + i: out for i, out in enumerate(previous)}

    def run(*refs):
        body(*refs[:given], *refs[given + len(previous) :])

    return pl.pallas_call(
        run,
        grid=grid,
        in_specs=list(in_specs) + [ANY] * len(previous),
        out_specs=list(out_specs),
        out_shape=list(outs),
        input_output_aliases=aliases,
        scratch_shapes=list(scratch),
        compiler_params=params(mib),
        cost_estimate=cost(name),
        name=name,
    )(*ins, *previous.values())


def still(block, index):
    return pl.BlockSpec(block, index, pipeline_mode=pl.Buffered(1))


def sds(shape, dtype):
    return jax.ShapeDtypeStruct(shape, dtype)


def prefetched(body, scalars, grid, ins, in_specs, outs, out_specs, mib=56, name=None):
    return pl.pallas_call(
        body,
        grid_spec=pltpu.PrefetchScalarGridSpec(
            num_scalar_prefetch=1, grid=grid, in_specs=in_specs, out_specs=out_specs
        ),
        out_shape=outs,
        compiler_params=params(mib),
        cost_estimate=cost(name),
        name=name,
    )(jnp.stack(scalars).astype(jnp.int32), *ins)


def norm_rows(x_ref, gain, shift, normed_ref, stats_ref, rows=64):
    def step(i, carry):
        at = pl.ds(pl.multiple_of(i * rows, rows), rows)
        x = x_ref[at, :].astype(F32)
        mean = jnp.mean(x, axis=-1, keepdims=True)
        centered = x - mean
        inverse = lax.rsqrt(jnp.mean(centered * centered, axis=-1, keepdims=True) + EPSILON)
        normed_ref[at, :] = (centered * inverse * gain + shift).astype(BF)
        lane = lax.broadcasted_iota(jnp.int32, (rows, 128), 1)
        stats_ref[at, :] = jnp.where(lane == 0, mean, inverse)
        return carry

    lax.fori_loop(0, x_ref.shape[0] // rows, step, 0)


def rope_tables():
    lane = jnp.arange(PAIR, dtype=jnp.int32)[None, :] % HEAD_DIM
    half = ROT // 2
    index = (lane % half).astype(F32)
    angles = jnp.arange(SEQ, dtype=F32)[:, None] * ROPE_BASE ** (-(index * (2.0 / ROT)))
    turned = lane < ROT
    cosine = jnp.where(turned, jnp.cos(angles), 1.0)
    low = jnp.where(turned & (lane >= half), jnp.sin(angles), 0.0)
    high = jnp.where(lane < half, -jnp.sin(angles), 0.0)
    return jnp.stack([cosine, low, high])


def turn(values, table):
    half = ROT // 2
    return (
        values * table[0]
        + pltpu.roll(values, half, 1) * table[1]
        + pltpu.roll(values, values.shape[1] - half, 1) * table[2]
    )


def turn_back(values, table):
    half = ROT // 2
    return (
        values * table[0]
        - pltpu.roll(values, half, 1) * table[1]
        - pltpu.roll(values, values.shape[1] - half, 1) * table[2]
    )


def project_body(x_ref, small_ref, weight_ref, bias_ref, table_ref, normed_ref, stats_ref, heads_ref):
    part = pl.program_id(0)

    @pl.when(part == 0)
    def _():
        gain, shift = (small_ref[k : k + 1, :].astype(F32) for k in (0, 1))
        norm_rows(x_ref, gain, shift, normed_ref, stats_ref)

    out = dot(normed_ref[...], weight_ref[0]) + bias_ref[0]
    width = out.shape[1]

    @pl.when(part < 2)
    def _():
        table = table_ref[...]
        for p in range(width // PAIR):
            heads_ref[0, :, p * PAIR : (p + 1) * PAIR] = turn(out[:, p * PAIR : (p + 1) * PAIR], table).astype(BF)

    @pl.when(part == 2)
    def _():
        heads_ref[0] = out.astype(BF)


def project(c, x, weight, bias, tables, previous):
    t, width = x.shape[0] - EXTRA, weight.shape[2]
    total = t * CHUNKS
    one = lambda k: (0, 0)
    return kernel_call(
        project_body,
        (3,),
        [x, x, weight, bias, tables],
        [
            still((t, D), one),
            pl.BlockSpec((EXTRA, D), lambda k: (t // EXTRA, 0)),
            pl.BlockSpec((1, D, width), lambda k: (k, 0, 0)),
            pl.BlockSpec((1, 1, width), lambda k: (k, 0, 0)),
            still((3, t, PAIR), lambda k: (0, c, 0)),
        ],
        [sds((total, D), BF), sds((total, 128), F32), sds((3, total, width), BF)],
        [
            pl.BlockSpec((t, D), lambda k: (c, 0)),
            pl.BlockSpec((t, 128), lambda k: (c, 0)),
            pl.BlockSpec((1, t, width), lambda k: (k, c, 0)),
        ],
        previous,
        mib=34,
        name="project",
    )


def lane_of(rows):
    return lax.broadcasted_iota(jnp.int32, (rows, PAIR), 1) < HEAD_DIM


def attend_body(c, owners_ref, q_ref, k_ref, v_ref, out_weight_ref, first_ref, rest_ref, ctx_ref, lse_ref):
    pair = pl.program_id(0)
    t = q_ref.shape[1]
    scale = HEAD_DIM ** (-0.5)
    low = lane_of(SUB)
    for r in range(t // SUB):
        start = c * t + r * SUB
        extent = start + SUB
        q = q_ref[0, r * SUB : (r + 1) * SUB, :].astype(F32) * scale
        keys = k_ref[0, :extent, :]
        values = v_ref[0, :extent, :]
        row = start + lax.broadcasted_iota(jnp.int32, (SUB, extent), 0)
        seen = lax.broadcasted_iota(jnp.int32, (SUB, extent), 1) <= row
        contexts, sums = [], []
        for h in range(2):
            own = jnp.where(low if h == 0 else ~low, q, 0.0).astype(BF)
            scores = jnp.where(seen, dot(own, keys, NT), -1000000000.0)
            top = jnp.max(scores, axis=-1, keepdims=True)
            raised = jnp.exp(scores - top)
            total = jnp.sum(raised, axis=-1, keepdims=True)
            contexts.append(dot(raised.astype(BF), values) / total)
            sums.append(top + jnp.log(total))
        at = pl.ds(pl.multiple_of(pair * PAIR, PAIR), PAIR)
        ctx_ref[r * SUB : (r + 1) * SUB, at] = jnp.where(low, contexts[0], contexts[1]).astype(BF)
        lse_ref[r * SUB : (r + 1) * SUB, :] = jnp.where(low, sums[0], sums[1])

    @pl.when(pair == pl.num_programs(0) - 1)
    def _():
        wide = first_ref.shape[1]
        for j in range(D // wide):
            at = pl.ds(pl.multiple_of(owners_ref[j] * wide, wide), wide)
            out = dot(ctx_ref[...], out_weight_ref[:, at]).astype(BF)
            if j == 0:
                first_ref[...] = out
            else:
                rest_ref[:, (j - 1) * wide : j * wide] = out


def attend(owners, heads, out_weight):
    t, width = heads.shape[1], heads.shape[2]
    here = lambda p, owners: (0, p)
    fixed = lambda p, owners: (0, 0)
    return prefetched(
        functools.partial(attend_body, 0),
        owners,
        (width // PAIR,),
        [heads, heads, heads, out_weight],
        [pl.BlockSpec((1, t, PAIR), lambda p, owners, k=k: (k, 0, p)) for k in range(3)]
        + [still((width, D), fixed)],
        [sds((t, width), BF), sds((t, D - width), BF), sds((t, width), BF), sds((t, width), F32)],
        [
            pl.BlockSpec((t, width), fixed),
            pl.BlockSpec((t, D - width), fixed),
            pl.BlockSpec((t, width), fixed),
            pl.BlockSpec((t, PAIR), here),
        ],
        mib=30,
        name="attend",
    )


def attend_back_body(c, *refs):
    q_ref, k_ref, v_ref, lse_ref, ctx_ref, dctx_ref, table_ref, with_ref, dq_ref, dk_ref, dv_ref, sums_ref, dk_sum, dv_sum = refs
    t = q_ref.shape[1]

    @pl.when(pl.program_id(0) == 0)
    def _():
        sums_ref[...] = jnp.zeros_like(sums_ref)

    def row_sums(k, gradient, values, at):
        first = gradient * with_ref[0, k : k + 1, :]
        second = gradient * (values - with_ref[1, k : k + 1, :])
        sums_ref[0:1, at] += jnp.sum(first.T, axis=0, keepdims=True)
        sums_ref[1:2, at] += jnp.sum(second.T, axis=0, keepdims=True)

    scale = HEAD_DIM ** (-0.5)
    low = lane_of(SUB)
    dk_sum[...] = jnp.zeros_like(dk_sum)
    dv_sum[...] = jnp.zeros_like(dv_sum)
    for r in range(t // SUB):
        here = slice(r * SUB, (r + 1) * SUB)
        start = c * t + r * SUB
        extent = start + SUB
        q = q_ref[0, here, :].astype(F32) * scale
        keys = k_ref[0, :extent, :]
        values = v_ref[0, :extent, :]
        dctx = dctx_ref[here, :]
        lse_t = lse_ref[here, :].T
        product_t = (ctx_ref[here, :].astype(F32) * dctx.astype(F32)).T
        low_keys = lane_of(extent)
        column = start + lax.broadcasted_iota(jnp.int32, (extent, SUB), 1)
        seen = lax.broadcasted_iota(jnp.int32, (extent, SUB), 0) <= column
        dq = jnp.zeros((SUB, PAIR), F32)
        for h in range(2):
            own = low if h == 0 else ~low
            q_own = jnp.where(own, q, 0.0).astype(BF)
            dctx_own = jnp.where(own, dctx, jnp.zeros_like(dctx))
            rows = slice(h * HEAD_DIM, (h + 1) * HEAD_DIM)
            row_dot = jnp.sum(product_t[rows, :], axis=0, keepdims=True)
            scores = dot(keys, q_own, NT) - lse_t[h * HEAD_DIM : h * HEAD_DIM + 1, :]
            probs = jnp.where(seen, jnp.exp(scores), 0.0)
            delta_probs = dot(values, dctx_own, NT)
            delta_scores = (probs * (delta_probs - row_dot)).astype(BF)
            dv_sum[:extent, :] += dot(probs.astype(BF), dctx_own)
            dk_sum[:extent, :] += dot(delta_scores, q_own)
            keys_own = jnp.where(low_keys if h == 0 else ~low_keys, keys, jnp.zeros_like(keys))
            dq = dq + dot(delta_scores, keys_own, TN)
        table = table_ref[:, start:extent, :]
        dq = turn_back(dq * scale, table)
        dq_ref[here, :] = dq.astype(BF)
        row_sums(0, dq, turn_back(q_ref[0, here, :].astype(F32), table), here)
    for r in range(t // SUB):
        here = slice(r * SUB, (r + 1) * SUB)
        table = table_ref[:, here, :]
        dk = turn_back(dk_sum[here, :], table)
        dk_ref[here, :] = dk.astype(BF)
        row_sums(1, dk, turn_back(k_ref[0, here, :].astype(F32), table), here)
        dv = dv_sum[here, :]
        dv_ref[here, :] = dv.astype(BF)
        row_sums(2, dv, v_ref[0, here, :].astype(F32), here)


def attend_back(heads, lse, ctx, dctx, tables, with_rows):
    t, width = heads.shape[1], heads.shape[2]
    own = pl.BlockSpec((t, PAIR), lambda p: (0, p))
    return kernel_call(
        functools.partial(attend_back_body, 0),
        (width // PAIR,),
        [heads, heads, heads, lse, ctx, dctx, tables, with_rows],
        [pl.BlockSpec((1, t, PAIR), lambda p, k=k: (k, 0, p)) for k in range(3)]
        + [own, own, own, still((3, t, PAIR), lambda p: (0, 0, 0)), pl.BlockSpec((2, 3, PAIR), lambda p: (0, 0, p))],
        [sds((t, width), BF)] * 3 + [sds((8, t), F32)],
        [own, own, own, pl.BlockSpec((8, t), lambda p: (0, 0))],
        scratch=[pltpu.VMEM((t, PAIR), F32)] * 2,
        mib=28,
        name="attend_back",
    )


def mlp_body(mid_ref, up_ref, gain_ref, shift_ref, gate_w_ref, up_w_ref, down_w_ref, normed_ref, stats_ref, hidden_ref, dgate_ref, dup_ref):
    @pl.when(pl.program_id(0) == 0)
    def _():
        norm_rows(mid_ref, gain_ref[...], shift_ref[...], normed_ref, stats_ref)

    normed = normed_ref[...]
    gate = dot(normed, gate_w_ref[...])
    upward = dot(normed, up_w_ref[...])
    delta_hidden = dot(up_ref[...], down_w_ref[...], NT)
    sigmoid = jax.nn.sigmoid(gate)
    silu = gate * sigmoid
    hidden_ref[...] = (silu * upward).astype(BF)
    dgate_ref[...] = (delta_hidden * upward * (sigmoid + silu * (1.0 - sigmoid))).astype(BF)
    dup_ref[...] = (delta_hidden * silu).astype(BF)


def mlp(c, mid, upstream, gain, shift, gate_w, up_w, down_w, previous):
    t, units = mid.shape[0], gate_w.shape[1]
    total = t * CHUNKS
    tile = 256
    one = lambda j: (0, 0)
    own = lambda j: (c, 0)
    column = pl.BlockSpec((t, tile), lambda j: (c, j))
    return kernel_call(
        mlp_body,
        (pl.cdiv(units, tile),),
        [mid, upstream, gain, shift, gate_w, up_w, down_w],
        [
            still((t, D), one),
            still((t, D), own),
            pl.BlockSpec((1, D), one),
            pl.BlockSpec((1, D), one),
            pl.BlockSpec((D, tile), lambda j: (0, j)),
            pl.BlockSpec((D, tile), lambda j: (0, j)),
            pl.BlockSpec((tile, D), lambda j: (j, 0)),
        ],
        [sds((total, D), BF), sds((total, 128), F32)] + [sds((total, units), BF)] * 3,
        [pl.BlockSpec((t, D), own), pl.BlockSpec((t, 128), own), column, column, column],
        previous,
        mib=46,
        name="mlp",
    )


def mlp_back_body(owners_ref, dgate_ref, dup_ref, gate_w_ref, up_w_ref, out_ref):
    out_ref[...] = (dot(dgate_ref[...], gate_w_ref[...], NT) + dot(dup_ref[...], up_w_ref[...], NT)).astype(BF)


def mlp_back(owners, width, dgate, dup, gate_w, up_w):
    t, units = dgate.shape
    whole = still((t, units), lambda j, owners: (0, 0))
    weight = pl.BlockSpec((width, units), lambda j, owners: (owners[j], 0))
    return prefetched(
        mlp_back_body,
        owners,
        (len(owners),),
        [dgate, dup, gate_w, up_w],
        [whole, whole, weight, weight],
        [sds((t, len(owners) * width), BF)],
        [pl.BlockSpec((t, width), lambda j, owners: (0, j))],
        mib=28,
        name="mlp_back",
    )[0]


def branch_back_body(e_ref, mid_ref, stats_ref, up_ref, weight_ref, means_ref, dbranch_ref, dctx_ref):
    rows = 64

    def step(i, carry):
        at = pl.ds(pl.multiple_of(i * rows, rows), rows)
        e = e_ref[at, :].astype(F32)
        mean, inverse = stats_ref[at, 0:1], stats_ref[at, 1:2]
        unit = (mid_ref[at, :].astype(F32) - mean) * inverse
        first = jnp.mean(e, axis=-1, keepdims=True)
        second = jnp.mean(e * unit, axis=-1, keepdims=True)
        dbranch_ref[at, :] = (up_ref[at, :].astype(F32) + inverse * (e - first - unit * second)).astype(BF)
        lane = lax.broadcasted_iota(jnp.int32, (rows, 128), 1)
        means_ref[at, :] = jnp.where(lane == 0, first, second)
        return carry

    lax.fori_loop(0, e_ref.shape[0] // rows, step, 0)
    dctx_ref[...] = dot(dbranch_ref[...], weight_ref[...], NT).astype(BF)


def branch_back(e, mid, stats, upstream, weight):
    t, width = e.shape[0], weight.shape[0]
    tile = SUB
    row = lambda i: (i, 0)
    return kernel_call(
        branch_back_body,
        (t // tile,),
        [e, mid, stats, upstream, weight],
        [
            pl.BlockSpec((tile, D), row),
            pl.BlockSpec((tile, D), row),
            pl.BlockSpec((tile, 128), row),
            pl.BlockSpec((tile, D), row),
            still((width, D), lambda i: (0, 0)),
        ],
        [sds((t, 128), F32), sds((t, D), BF), sds((t, width), BF)],
        [pl.BlockSpec((tile, 128), row), pl.BlockSpec((tile, D), row), pl.BlockSpec((tile, width), row)],
        mib=24,
        name="branch_back",
    )


def project_back_body(owners_ref, dq_ref, dk_ref, dv_ref, weight_ref, x_ref, stats_ref, below_ref, out_ref):
    n = dot(dq_ref[...], weight_ref[0], NT) + dot(dk_ref[...], weight_ref[1], NT) + dot(dv_ref[...], weight_ref[2], NT)
    out_ref[: n.shape[0], :] = n.astype(BF)
    unit = (x_ref[...].astype(F32) - stats_ref[:, 0:1]) * stats_ref[:, 1:2]
    with_unit = n * unit
    row = lax.broadcasted_iota(jnp.int32, (EXTRA, n.shape[1]), 0)
    gain_grad = jnp.sum(with_unit, axis=0, keepdims=True)
    shift_grad = jnp.sum(n, axis=0, keepdims=True)
    out_ref[n.shape[0] :, :] = jnp.where(row == 0, gain_grad, jnp.where(row == 1, shift_grad, below_ref[...])).astype(BF)


def project_back(owners, dq, dk, dv, weight, x, stats, below):
    t, width = dq.shape
    count = len(owners)
    whole = still((t, width), lambda j, owners: (0, 0))
    return prefetched(
        project_back_body,
        owners,
        (count,),
        [dq, dk, dv, weight, x, stats, below],
        [
            whole,
            whole,
            whole,
            pl.BlockSpec((3, width, width), lambda j, owners: (0, owners[j], 0)),
            pl.BlockSpec((t, width), lambda j, owners: (0, owners[j])),
            still((t, 128), lambda j, owners: (0, 0)),
            still((EXTRA, width), lambda j, owners: (0, 0)),
        ],
        [sds((t + EXTRA, count * width), BF)],
        [pl.BlockSpec((t + EXTRA, width), lambda j, owners: (0, j))],
        mib=34,
        name="project_back",
    )[0]


def add(a, b):
    return (a.astype(F32) + b.astype(F32)).astype(BF)


class Order:
    def __init__(self):
        self.before = ()

    def __call__(self, value):
        return after(value, *self.before) if self.before else value

    def done(self, *values):
        self.before = tuple(values)


class Gather:
    def __init__(self, share):
        self.n = lax.axis_size("tensor")
        self.pieces = [share]
        self.held = {(i, i): 0 for i in range(self.n)}
        self.steps = 0

    def send(self, piece, pairs, order):
        self.pieces.append(lax.ppermute(order(self.pieces[piece]), "tensor", pairs))

    def step(self, order):
        n, s = self.n, self.steps
        self.steps += 1
        before = len(self.pieces)
        if n == 4:
            outer, inner, out = [(0, 1), (1, 0), (2, 3), (3, 2)], [(1, 2), (2, 1)], [(1, 0), (2, 3)]
            for piece, pairs in (((0, outer), (0, inner)), ((2, out), (1, inner)), ((4, out),))[s]:
                self.send(piece, pairs, order)
            owners = ((1, None, 2, None, 3), (0, 2, None, 3, None), (3, 1, None, 0, None), (2, None, 1, None, 0))
            self.held = {(i, i): 0 for i in range(n)} | {
                (i, owner): 1 + k for i, row in enumerate(owners) for k, owner in enumerate(row) if owner is not None
            }
        else:
            up, down = (0, 0) if s == 0 else (before - 2, before - 1)
            self.held.update({(i + 1, i - s): before for i in range(s, n - 1)})
            self.held.update({(i, i + 1 + s): before + 1 for i in range(n - 1 - s)})
            self.send(up, [(i, i + 1) for i in range(s, n - 1)], order)
            self.send(down, [(i + 1, i) for i in range(n - 1 - s)], order)
        return self.pieces[before:]

    def last(self, order):
        got = self.step(order)
        while self.steps < self.n - 1:
            got = self.step(order)
        return got

    def whole(self):
        share = self.pieces[0]
        t, width = share.shape
        return prefetched(
            functools.partial(assemble_body, self.held),
            [lax.axis_index("tensor")],
            (self.n,),
            self.pieces,
            [still((t, width), lambda j, me: (0, 0))] * len(self.pieces),
            [sds((t, self.n * width), share.dtype)],
            [pl.BlockSpec((t, width), lambda j, me: (0, j))],
            mib=14,
            name="assemble",
        )[0]


def steps(order, *ops):
    return [got for op in ops if op.steps < op.n - 1 for got in op.step(order)]


def finish(order, *ops):
    got = steps(order, *ops)
    while any(op.steps < op.n - 1 for op in ops):
        got = steps(order, *ops)
    return got


def scatter_order(n):
    me = lax.axis_index("tensor")
    first = jnp.where(me < n // 2, n - 1, 0)
    return [(first + k) % n for k in range(n)]


class Scatter:
    def __init__(self, first, rest):
        self.n, self.me = lax.axis_size("tensor"), lax.axis_index("tensor")
        self.first, self.rest, self.steps, self.got = first, rest, 0, {}
        self.width = first.shape[1]

    def part(self, owner, *got):
        place = (owner - jnp.where(self.me < self.n // 2, self.n - 1, 0) - 1) % self.n
        place = jnp.clip(place, 0, self.n - 2)
        value = lax.dynamic_slice_in_dim(self.rest, place * self.width, self.width, 1)
        return functools.reduce(add, got, value)

    def any(self, owner, *got):
        first = jnp.where(self.me < self.n // 2, self.n - 1, 0)
        value = jnp.where(owner % self.n == first, self.first, self.part(owner % self.n))
        return functools.reduce(add, got, value)

    def send(self, name, value, pairs, order):
        self.got[name] = lax.ppermute(order(value), "tensor", pairs)

    def step(self, order):
        n, me, s = self.n, self.me, self.steps
        self.got = got = {name: order(value) for name, value in self.got.items()}
        self.steps += 1
        if n == 4:
            inward, inner, outer = [(0, 1), (3, 2)], [(1, 2), (2, 1)], [(0, 1), (1, 0), (2, 3), (3, 2)]
            if s == 0:
                self.send("far", self.first, inward, order)
                return [got["far"]]
            if s == 1:
                self.send("far", add(self.first, got["far"]), inner, order)
                self.send("next", self.part(jnp.where(me == 0, 2, 1)), inward, order)
            else:
                self.send("far", self.part(me ^ 1, got["far"]), outer, order)
                self.send("next", self.part(3 - me, got["next"]), inner, order)
            return [got["far"], got["next"]]
        up, down = ((got["up"],), (got["down"],)) if s else ((), ())
        self.send("up", self.any(me + n - 1 - s, *up), [(i, i + 1) for i in range(s + 1)], order)
        self.send("down", self.any(me - n + 1 + s, *down), [(i + 1, i) for i in range(n - 2 - s, n - 1)], order)
        return [got["up"], got["down"]]

    def last(self, order):
        got = self.step(order)
        while self.steps < self.n - 1:
            got = self.step(order)
        return got

    def total(self, order):
        self.got = {name: order(value) for name, value in self.got.items()}
        own = self.any(self.me) if self.n != 4 else self.part(self.me)
        return sum((g.astype(F32) for g in self.got.values()), own.astype(F32))


def assemble_body(held, me_ref, *refs):
    out_ref, owner, me = refs[-1], pl.program_id(0), me_ref[0]
    for k, ref in enumerate(refs[:-1]):
        places = [(device, o) for (device, o), at in held.items() if at == k]
        here = functools.reduce(jnp.logical_or, [(me == device) & (owner == o) for device, o in places])

        @pl.when(here)
        def _(ref=ref):
            out_ref[...] = ref[...]


def gradients_body(groups, which_ref, *refs):
    lefts, rest = refs[: len(groups)], refs[len(groups) :]
    rights, outs = rest[: len(rest) // 2], rest[len(rest) // 2 :]
    for left, count in zip(lefts, groups):
        turned = left[...].T
        for right, out in zip(rights[:count], outs[:count]):
            out[...] = dot(turned, right[...]).astype(BF)
        rights, outs = rights[count:], outs[count:]


def gradients(which, pairs, name):
    t = pairs[0][0].shape[0]
    block = 256
    nb = D // 2 // block
    lefts, rights = [left for left, _ in pairs], [right for _, some in pairs for right in some]
    return prefetched(
        functools.partial(gradients_body, [len(some) for _, some in pairs]),
        [which],
        (nb,),
        lefts + rights,
        [pl.BlockSpec((t, block), lambda i, which: (0, which[0] * nb + i))] * len(lefts)
        + [still(right.shape, lambda i, which: (0, 0)) for right in rights],
        [sds((D // 2, right.shape[1]), BF) for right in rights],
        [pl.BlockSpec((block, right.shape[1]), lambda i, which: (i, 0)) for right in rights],
        mib=30,
        name=name,
    )


def mlp_out_body(owners_ref, hidden_ref, weight_ref, first_ref, rest_ref):
    out = dot(hidden_ref[...], weight_ref[...]).astype(BF)

    @pl.when(pl.program_id(0) == 0)
    def _():
        first_ref[...] = out

    @pl.when(pl.program_id(0) > 0)
    def _():
        rest_ref[...] = out


def mlp_out(owners, width, hidden, weight):
    t, units = hidden.shape
    return prefetched(
        mlp_out_body,
        owners,
        (len(owners),),
        [hidden, weight],
        [
            still((t, units), lambda j, owners: (0, 0)),
            pl.BlockSpec((units, width), lambda j, owners: (0, owners[j])),
        ],
        [sds((t, width), BF), sds((t, D - width), BF)],
        [
            pl.BlockSpec((t, width), lambda j, owners: (0, 0)),
            pl.BlockSpec((t, width), lambda j, owners: (0, jnp.maximum(j - 1, 0))),
        ],
        mib=22,
        name="mlp_out",
    )


def swap(value, bit, axis="dp"):
    n = lax.axis_size(axis)
    return lax.ppermute(value, axis, [(i, i ^ (1 << bit)) for i in range(n)])


def split_body(groups, bits_ref, *refs):
    parts, outs = refs[: 4 * groups], refs[4 * groups :]
    for part in range(2):
        for phase in range(2):

            @pl.when(pl.program_id(0) == phase)
            def _(part=part, phase=phase):
                at = 0
                for g in range(groups):
                    keep, got = parts[2 * (part * groups + g)], parts[2 * (part * groups + g) + 1]
                    wide = keep.shape[1]
                    outs[2 * part + phase][:, at : at + wide] = add(keep[...], got[...])
                    at += wide


def split(upper, lower, bits, joined):
    groups = len(upper)
    rows = upper[0][0].shape[0] // (4 if joined else 2)
    block = min(128, rows)
    nb = rows // block
    columns = sum(keep.shape[1] for keep, _ in upper)
    ins, in_specs = [], []
    for part, pairs in enumerate((upper, lower)):
        first = 2 * nb * part if joined else 0

        def index(phase, j, bits, part=part, first=first):
            half = jnp.where(phase == 0, 1 - bits[part], bits[part])
            return (first + half * nb + j, 0)

        for pair in pairs:
            for array in pair:
                ins.append(array)
                in_specs.append(pl.BlockSpec((block, array.shape[1]), index))
    given = pl.BlockSpec((block, columns), lambda phase, j, bits: (jnp.where(phase == 0, j, nb - 1), 0))
    kept = pl.BlockSpec((block, columns), lambda phase, j, bits: (jnp.where(phase == 0, 0, j), 0))
    return prefetched(
        functools.partial(split_body, groups),
        bits,
        (2, nb),
        ins,
        in_specs,
        [sds((rows, columns), BF)] * 4,
        [given, kept] * 2,
        mib=28,
        name="split",
    )


def merge_body(widths, bits_ref, *refs):
    for part in range(2):
        for which in range(2):

            @pl.when((pl.program_id(0) == bits_ref[part]) == (which == 0))
            def _(part=part, which=which):
                value = refs[2 * part + which][...]
                if widths:
                    at = 0
                    for out, wide in zip(refs[4:], widths):
                        out[part] = value[:, at : at + wide]
                        at += wide
                else:
                    refs[4 + part][...] = value


def merge(upper, lower, bits, widths=()):
    rows, columns = upper[0].shape
    block = min(128, rows)
    nb = rows // block

    def spec(part, which):
        def index(i, j, bits):
            half = bits[part] if which == 0 else 1 - bits[part]
            return (jnp.where(i == half, j, jnp.where(i < half, 0, nb - 1)), 0)

        return pl.BlockSpec((block, columns), index)

    if widths:
        outs = [sds((2, 2 * rows, wide), BF) for wide in widths]
        out_specs = [pl.BlockSpec((2, block, wide), lambda i, j, bits: (0, i * nb + j, 0)) for wide in widths]
    else:
        outs = [sds((2 * rows, columns), BF)] * 2
        out_specs = [pl.BlockSpec((block, columns), lambda i, j, bits: (i * nb + j, 0))] * 2
    return prefetched(
        functools.partial(merge_body, widths),
        bits,
        (2, nb),
        [*upper, *lower],
        [spec(part, which) for part in range(2) for which in range(2)],
        outs,
        out_specs,
        mib=22,
        name="merge",
    )


def sum_over_dp(given, order):
    me, n = lax.axis_index("dp"), lax.axis_size("dp")
    count = n.bit_length() - 1
    bit = lambda b: (me >> b) & 1
    orders = [list(range(1, count)), list(range(count - 1, 0, -1))]
    got = [swap(g, 0) for g in given]
    kept = yield got
    upper = lower = [(order(k), g) for k, g in zip(kept, got)]
    for s in range(count - 1):
        a, b = orders[0][s], orders[1][s]
        p_give, p_keep, q_give, q_keep = split(upper, lower, [bit(a), bit(b)], s == 0)
        upper, lower = [(p_keep, swap(p_give, a))], [(q_keep, swap(q_give, b))]
        yield p_keep
        upper, lower = [(order(upper[0][0]), upper[0][1])], [(order(lower[0][0]), lower[0][1])]
    p, q = add(*upper[0]), add(*lower[0])
    for s in reversed(range(count - 1)):
        a, b = orders[0][s], orders[1][s]
        p, q = lax.optimization_barrier((p, q))
        got = swap(p, a), swap(q, b)
        yield p
        out = merge([order(p), got[0]], [q, got[1]], [bit(a), bit(b)], () if s else [g.shape[1] for g in given])
        if s:
            p, q = out
    own = [array.reshape(-1, array.shape[2]) for array in out]
    other = [swap(array, 0) for array in own]
    yield own[0]
    yield own, other


def finish_sum(steps_left):
    *_, last = steps_left
    return last


def halves(core, own, other, nb):
    def index(mine):
        def of(i, bits):
            half = bits[0] if mine else 1 - bits[0]
            return (jnp.clip(i - half * nb, 0, nb - 1), 0)

        return of

    return index(True), index(False)


def halves_body(store, core_ref, *refs):
    half = pl.program_id(0) // (pl.num_programs(0) // 2)
    groups = store.groups
    own, other, outs = refs[:groups], refs[groups : 2 * groups], refs[2 * groups :]
    for arrays, mine in ((own, True), (other, False)):

        @pl.when((half == core_ref[0]) == mine)
        def _(arrays=arrays):
            store(arrays, outs)


def from_halves(store, core, own, other, outs, out_specs, block, mib, name):
    store.groups = len(own)
    nb = own[0].shape[0] // block
    return prefetched(
        functools.partial(halves_body, store),
        [core],
        (2 * nb,),
        [*own, *other],
        [
            pl.BlockSpec((block, array.shape[1]), index)
            for arrays, index in zip((own, other), halves(core, own, other, nb))
            for array in arrays
        ],
        outs,
        out_specs,
        mib=mib,
        name=name,
    )


def gate_up_out(core, own, other):
    def store(arrays, outs):
        for k in range(2):
            outs[0][:, k, :] = arrays[k][...].astype(F32)

    units, block = own[0].shape[1], 128
    outs, spec = [sds((D, 2, units), F32)], [pl.BlockSpec((block, 2, units), lambda i, c: (i, 0, 0))]
    return from_halves(store, core, own, other, outs, spec, block, 22, "gate_up_out")[0]


def down_out(core, own, other):
    def store(arrays, outs):
        outs[0][...] = arrays[0][...].astype(F32).T

    units, block = own[0].shape[1], 128
    outs, spec = [sds((units, D), F32)], [pl.BlockSpec((units, block), lambda i, c: (0, i))]
    return from_halves(store, core, own, other, outs, spec, block, 16, "down_out")[0]


def attention_out(core, own, other):
    def store(arrays, outs):
        for k in range(3):
            outs[0][k] = arrays[k][...].astype(F32)
        outs[1][...] = arrays[3][...].astype(F32).T

    width, block = own[0].shape[1], 256
    outs = [sds((3, D, width), F32), sds((width, D), F32)]
    specs = [
        pl.BlockSpec((3, block, width), lambda i, c: (0, i, 0)),
        pl.BlockSpec((width, block), lambda i, c: (0, i)),
    ]
    return from_halves(store, core, own, other, outs, specs, block, 22, "attention_out")


def per_device(
    tokens,
    norm_one_gain,
    norm_one_shift,
    project_weight,
    project_bias,
    output_weight,
    norm_two_gain,
    norm_two_shift,
    gate_up_weight,
    down_weight,
    cotangent,
):
    width = tokens.shape[1]
    t = tokens.shape[0] // CHUNKS
    offset = lax.axis_index("tensor") * width
    core = lax.axis_index("dp") & 1
    mine = lambda full: lax.dynamic_slice_in_dim(full, offset, width, full.ndim - 1)
    half_of = lambda array, which: lax.dynamic_slice_in_dim(array, which * (D // 2), D // 2, 1)
    order = Order()

    small = jnp.stack([norm_one_gain, norm_one_shift, norm_two_gain, norm_two_shift])
    whole_x = Gather(jnp.concatenate([tokens, jnp.pad(small, ((0, EXTRA - 4), (0, 0)))]))
    whole_up = Gather(cotangent)
    got = whole_x.step(order)
    gate_w = order(gate_up_weight)[:, 0]
    order.done(*got, gate_w)
    got = whole_x.step(order)
    up_w = order(gate_up_weight)[:, 1]
    tables = rope_tables()
    order.done(*got, up_w, tables)
    whole_x.last(order)
    x = whole_x.whole()
    gain_one, gain_two, shift_two = (x[t + i : t + i + 1].astype(F32) for i in (0, 2, 3))
    project_w = project_weight.transpose(1, 0, 2)
    bias = project_bias.astype(F32)[:, None, :]

    through = lambda row: jnp.einsum("d,kdc->kc", row[0].astype(BF), project_w, preferred_element_type=F32)
    with_rows = jnp.stack([through(gain_one), through(x[t + 1 : t + 2]) + bias[:, 0]])

    order.done(x)
    got = whole_up.step(order)
    normed_one, stats_one, heads = project(0, x, project_w, bias, tables, ())
    order.done(*got, stats_one)
    owners = scatter_order(whole_up.n)
    first, rest, context, lse = attend(owners, order(heads), output_weight)
    order.done(lse)
    branch = Scatter(first, rest)
    for _ in range(2):
        order.done(*whole_up.step(order), *branch.step(order), with_rows)
    if whole_up.n > 4:
        whole_up.last(order)
    branch.last(order)
    upstream = whole_up.whole()
    middle_share = tokens.astype(F32) + branch.total(order)
    middle_sent = (middle_share - stats_one[:, 0:1]).astype(BF)
    order.done(middle_sent)
    whole_middle = Gather(middle_sent)
    while whole_middle.steps < whole_middle.n - 1:
        whole_middle.step(order)
    middle = whole_middle.whole()

    normed_two, stats_two, hidden, dgate, dup = mlp(
        0, middle, upstream, gain_two, shift_two, gate_w, up_w, down_weight, ()
    )
    first = mlp_back(owners[:1], width, dgate, dup, gate_w, up_w)
    rest = mlp_back(owners[1:], width, after(dgate, first), dup, gate_w, up_w)
    order.done(first)
    delta_two = Scatter(first, rest)
    got = steps(order, delta_two)
    order.done(rest, *got)
    got = steps(order, delta_two)
    mlp_grads = lambda which, name: gradients(
        which, [(normed_two, [order(dgate), dup]), (upstream, [hidden])], name
    )
    mlp_given = mlp_grads(1 - core, "mlp_given")
    mlp_sum = sum_over_dp(mlp_given, order)
    next(mlp_sum)
    order.done(*got, *mlp_given)
    got = finish(order, delta_two)
    mlp_kept = mlp_grads(core, "mlp_kept")
    order.done(*got, *mlp_kept)
    delta_two = delta_two.total(order)
    unit_two = (mine(middle).astype(F32) - stats_two[:, 0:1]) * stats_two[:, 1:2]
    two_grads = [jnp.sum(delta_two * unit_two, axis=0), jnp.sum(delta_two, axis=0)]
    e_own = delta_two * norm_two_gain.astype(F32)
    e_sent = e_own.astype(BF)
    order.done(e_sent)
    whole_e = Gather(e_sent)
    got = steps(order, whole_e)
    held = mlp_sum.send(mlp_kept)
    order.done(*got, held)
    got = steps(order, whole_e)
    mlp_share = Scatter(*mlp_out(owners, width, order(hidden), down_weight))
    order.done(*got, mlp_share.rest)
    got = finish(order, whole_e) + steps(order, mlp_share)
    held = next(mlp_sum)
    e = whole_e.whole()

    order.done(e, held, *got)
    share_got = steps(order, mlp_share)
    means_two, dbranch, dctx = branch_back(order(e), middle, stats_two, upstream, output_weight)
    order.done(dctx)
    held = next(mlp_sum)
    order.done(held)
    dq, dk, dv, sums = attend_back(heads, lse, context, order(dctx), tables, with_rows)
    held = next(mlp_sum)
    order.done(dq, held, *share_got)
    delta_heads = (dq, dk, dv)
    attention_grads = lambda which, name: gradients(
        which, [(normed_one, [order(dq), dk, dv]), (dbranch, [context])], name
    )
    attention_given = attention_grads(1 - core, "attention_given")
    attention_sum = sum_over_dp(attention_given, order)
    next(attention_sum)
    sum_rows = 2 * t // width
    below = jnp.pad(sums[:2].reshape(sum_rows, width), ((2, EXTRA - 2 - sum_rows), (0, 0)))
    order.done(*attention_given, below)
    back = lambda owners, dq: project_back(owners, dq, dk, dv, project_w, x, stats_one, below)
    first = back(owners[:1], order(dq))
    rest = back(owners[1:], after(dq, first))
    order.done(first)
    delta_one = Scatter(first, rest)
    got = steps(order, delta_one)
    order.done(rest)
    attention_kept = attention_grads(core, "attention_kept")
    order.done(*attention_kept)
    held = attention_sum.send(attention_kept)
    order.done(held, *got)
    got = steps(order, delta_one)
    held = next(mlp_sum)
    order.done(held)
    held = next(attention_sum)
    order.done(held, *got)
    got = finish(order, delta_one)
    if lax.axis_size("dp") > 8:
        for _ in range(2):
            order.done(next(mlp_sum))
            order.done(next(attention_sum))
    held = next(attention_sum)
    order.done(held)
    mlp_halves = next(mlp_sum)
    down_grad = down_out(core, [order(mlp_halves[0][2])], mlp_halves[1][2:])
    order.done(down_grad)
    held = next(attention_sum)
    order.done(held, *got)
    delta_one = delta_one.total(order)
    bias_grad = [jnp.sum(a, axis=0, dtype=F32) for a in delta_heads]
    small = jnp.stack([delta_one[t], delta_one[t + 1], *two_grads, *bias_grad])
    small = small + swap(order(small), 0)
    order.done(small)
    finish(order, mlp_share)
    devices = lax.axis_size("dp")
    others = [lax.ppermute(order(small), "dp", [(i, i ^ k) for i in range(devices)]) for k in range(2, devices, 2)]
    gate_up_grad = gate_up_out(core, [order(mlp_halves[0][0]), mlp_halves[0][1]], mlp_halves[1][:2])
    order.done(gate_up_grad)
    held = next(attention_sum)
    order.done(held)
    result = (middle_share + mlp_share.total(order)).astype(BF)
    sums = (delta_one[t + 2 : t + 2 + sum_rows] / D).reshape(2, t).T
    unit_one = (tokens.astype(F32) - stats_one[:, 0:1]) * stats_one[:, 1:2]
    dmid = cotangent.astype(F32) + stats_two[:, 1:2] * (e_own - means_two[:, 0:1] - unit_two * means_two[:, 1:2])
    tokens_grad = order(dmid) + stats_one[:, 1:2] * (
        delta_one[:t] * norm_one_gain.astype(F32) - sums[:, 0:1] - unit_one * sums[:, 1:2]
    )
    small = sum((order(other) for other in others), small)
    order.done(tokens_grad, small, result)
    attention_halves = next(attention_sum)
    project_grad, output_grad = attention_out(
        core, [order(attention_halves[0][0]), *attention_halves[0][1:]], attention_halves[1]
    )
    return (
        result,
        tokens_grad,
        small[0],
        small[1],
        project_grad.transpose(1, 0, 2),
        small[4:7],
        output_grad,
        small[2],
        small[3],
        gate_up_grad,
        down_grad,
    )


def solution(mesh):
    return jax.shard_map(
        per_device,
        mesh=mesh,
        in_specs=(
            P("dp", "tensor"),
            P("tensor"),
            P("tensor"),
            P(None, None, "tensor"),
            P(None, "tensor"),
            P("tensor", None),
            P("tensor"),
            P("tensor"),
            P(None, None, "tensor"),
            P("tensor", None),
            P("dp", "tensor"),
        ),
        out_specs=(
            P("dp", "tensor"),
            P("dp", "tensor"),
            P("tensor"),
            P("tensor"),
            P(None, None, "tensor"),
            P(None, "tensor"),
            P("tensor", None),
            P("tensor"),
            P("tensor"),
            P(None, None, "tensor"),
            P("tensor", None),
        ),
        check_vma=False,
    )
```

```python
import functools

import jax
import jax.numpy as jnp
from jax import lax
from jax.experimental import pallas as pl
from jax.experimental.pallas import tpu as pltpu
from jax.sharding import PartitionSpec as P

D = 2048
HEAD_DIM = 64
ROT = 16
SEQ = 1024
PAIR = 2 * HEAD_DIM
CHUNKS = 1
SUB = 256
WEIGHTS = {"mlp_kept": 30, "mlp_out": 10, "project_back": 5, "attend_back": 20}
EXTRA = 16

EPSILON = 1e-05
ROPE_BASE = 10000.0
BF = jnp.bfloat16
F32 = jnp.float32
NT = (((1,), (1,)), ((), ()))
TN = (((0,), (0,)), ((), ()))
ANY = pl.BlockSpec(memory_space=pl.ANY)


def dot(a, b, dims=(((1,), (0,)), ((), ()))):
    return lax.dot_general(a, b, dims, preferred_element_type=F32)


def params(mib):
    return pltpu.CompilerParams(vmem_limit_bytes=mib << 20)


def cost(name):
    return pl.CostEstimate(flops=int(WEIGHTS.get(name, 0) * 1e9), bytes_accessed=0, transcendentals=0)


def after(value, *others):
    return lax.optimization_barrier((value, *others))[0]


def kernel_call(body, grid, ins, in_specs, outs, out_specs, previous=(), scratch=(), mib=56, name=None):
    given = len(ins)
    previous = dict(previous)
    aliases = {given + i: out for i, out in enumerate(previous)}

    def run(*refs):
        body(*refs[:given], *refs[given + len(previous) :])

    return pl.pallas_call(
        run,
        grid=grid,
        in_specs=list(in_specs) + [ANY] * len(previous),
        out_specs=list(out_specs),
        out_shape=list(outs),
        input_output_aliases=aliases,
        scratch_shapes=list(scratch),
        compiler_params=params(mib),
        cost_estimate=cost(name),
        name=name,
    )(*ins, *previous.values())


def still(block, index):
    return pl.BlockSpec(block, index, pipeline_mode=pl.Buffered(1))


def sds(shape, dtype):
    return jax.ShapeDtypeStruct(shape, dtype)


def prefetched(body, scalars, grid, ins, in_specs, outs, out_specs, mib=56, name=None):
    return pl.pallas_call(
        body,
        grid_spec=pltpu.PrefetchScalarGridSpec(
            num_scalar_prefetch=1, grid=grid, in_specs=in_specs, out_specs=out_specs
        ),
        out_shape=outs,
        compiler_params=params(mib),
        cost_estimate=cost(name),
        name=name,
    )(jnp.stack(scalars).astype(jnp.int32), *ins)


def norm_rows(x_ref, gain, shift, normed_ref, stats_ref, rows=64):
    def step(i, carry):
        at = pl.ds(pl.multiple_of(i * rows, rows), rows)
        x = x_ref[at, :].astype(F32)
        mean = jnp.mean(x, axis=-1, keepdims=True)
        centered = x - mean
        inverse = lax.rsqrt(jnp.mean(centered * centered, axis=-1, keepdims=True) + EPSILON)
        normed_ref[at, :] = (centered * inverse * gain + shift).astype(BF)
        lane = lax.broadcasted_iota(jnp.int32, (rows, 128), 1)
        stats_ref[at, :] = jnp.where(lane == 0, mean, inverse)
        return carry

    lax.fori_loop(0, x_ref.shape[0] // rows, step, 0)


def rope_tables():
    lane = jnp.arange(PAIR, dtype=jnp.int32)[None, :] % HEAD_DIM
    half = ROT // 2
    index = (lane % half).astype(F32)
    angles = jnp.arange(SEQ, dtype=F32)[:, None] * ROPE_BASE ** (-(index * (2.0 / ROT)))
    turned = lane < ROT
    cosine = jnp.where(turned, jnp.cos(angles), 1.0)
    low = jnp.where(turned & (lane >= half), jnp.sin(angles), 0.0)
    high = jnp.where(lane < half, -jnp.sin(angles), 0.0)
    return jnp.stack([cosine, low, high])


def turn(values, table):
    half = ROT // 2
    return (
        values * table[0]
        + pltpu.roll(values, half, 1) * table[1]
        + pltpu.roll(values, values.shape[1] - half, 1) * table[2]
    )


def turn_back(values, table):
    half = ROT // 2
    return (
        values * table[0]
        - pltpu.roll(values, half, 1) * table[1]
        - pltpu.roll(values, values.shape[1] - half, 1) * table[2]
    )


def project_body(x_ref, small_ref, weight_ref, bias_ref, table_ref, normed_ref, stats_ref, heads_ref):
    part = pl.program_id(0)

    @pl.when(part == 0)
    def _():
        gain, shift = (small_ref[k : k + 1, :].astype(F32) for k in (0, 1))
        norm_rows(x_ref, gain, shift, normed_ref, stats_ref)

    out = dot(normed_ref[...], weight_ref[0]) + bias_ref[0]
    width = out.shape[1]

    @pl.when(part < 2)
    def _():
        table = table_ref[...]
        for p in range(width // PAIR):
            heads_ref[0, :, p * PAIR : (p + 1) * PAIR] = turn(out[:, p * PAIR : (p + 1) * PAIR], table).astype(BF)

    @pl.when(part == 2)
    def _():
        heads_ref[0] = out.astype(BF)


def project(c, x, weight, bias, tables, previous):
    t, width = x.shape[0] - EXTRA, weight.shape[2]
    total = t * CHUNKS
    one = lambda k: (0, 0)
    return kernel_call(
        project_body,
        (3,),
        [x, x, weight, bias, tables],
        [
            still((t, D), one),
            pl.BlockSpec((EXTRA, D), lambda k: (t // EXTRA, 0)),
            pl.BlockSpec((1, D, width), lambda k: (k, 0, 0)),
            pl.BlockSpec((1, 1, width), lambda k: (k, 0, 0)),
            still((3, t, PAIR), lambda k: (0, c, 0)),
        ],
        [sds((total, D), BF), sds((total, 128), F32), sds((3, total, width), BF)],
        [
            pl.BlockSpec((t, D), lambda k: (c, 0)),
            pl.BlockSpec((t, 128), lambda k: (c, 0)),
            pl.BlockSpec((1, t, width), lambda k: (k, c, 0)),
        ],
        previous,
        mib=34,
        name="project",
    )


def lane_of(rows):
    return lax.broadcasted_iota(jnp.int32, (rows, PAIR), 1) < HEAD_DIM


def attend_body(c, owners_ref, q_ref, k_ref, v_ref, out_weight_ref, first_ref, rest_ref, ctx_ref, lse_ref):
    pair = pl.program_id(0)
    t = q_ref.shape[1]
    scale = HEAD_DIM ** (-0.5)
    low = lane_of(SUB)
    for r in range(t // SUB):
        start = c * t + r * SUB
        extent = start + SUB
        q = q_ref[0, r * SUB : (r + 1) * SUB, :].astype(F32) * scale
        keys = k_ref[0, :extent, :]
        values = v_ref[0, :extent, :]
        row = start + lax.broadcasted_iota(jnp.int32, (SUB, extent), 0)
        seen = lax.broadcasted_iota(jnp.int32, (SUB, extent), 1) <= row
        contexts, sums = [], []
        for h in range(2):
            own = jnp.where(low if h == 0 else ~low, q, 0.0).astype(BF)
            scores = jnp.where(seen, dot(own, keys, NT), -1000000000.0)
            top = jnp.max(scores, axis=-1, keepdims=True)
            raised = jnp.exp(scores - top)
            total = jnp.sum(raised, axis=-1, keepdims=True)
            contexts.append(dot(raised.astype(BF), values) / total)
            sums.append(top + jnp.log(total))
        at = pl.ds(pl.multiple_of(pair * PAIR, PAIR), PAIR)
        ctx_ref[r * SUB : (r + 1) * SUB, at] = jnp.where(low, contexts[0], contexts[1]).astype(BF)
        lse_ref[r * SUB : (r + 1) * SUB, :] = jnp.where(low, sums[0], sums[1])

    @pl.when(pair == pl.num_programs(0) - 1)
    def _():
        wide = first_ref.shape[1]
        for j in range(D // wide):
            at = pl.ds(pl.multiple_of(owners_ref[j] * wide, wide), wide)
            out = dot(ctx_ref[...], out_weight_ref[:, at]).astype(BF)
            if j == 0:
                first_ref[...] = out
            else:
                rest_ref[:, (j - 1) * wide : j * wide] = out


def attend(owners, heads, out_weight):
    t, width = heads.shape[1], heads.shape[2]
    here = lambda p, owners: (0, p)
    fixed = lambda p, owners: (0, 0)
    return prefetched(
        functools.partial(attend_body, 0),
        owners,
        (width // PAIR,),
        [heads, heads, heads, out_weight],
        [pl.BlockSpec((1, t, PAIR), lambda p, owners, k=k: (k, 0, p)) for k in range(3)]
        + [still((width, D), fixed)],
        [sds((t, width), BF), sds((t, D - width), BF), sds((t, width), BF), sds((t, width), F32)],
        [
            pl.BlockSpec((t, width), fixed),
            pl.BlockSpec((t, D - width), fixed),
            pl.BlockSpec((t, width), fixed),
            pl.BlockSpec((t, PAIR), here),
        ],
        mib=30,
        name="attend",
    )


def attend_back_body(c, *refs):
    q_ref, k_ref, v_ref, lse_ref, ctx_ref, dctx_ref, table_ref, with_ref, dq_ref, dk_ref, dv_ref, sums_ref, dk_sum, dv_sum = refs
    t = q_ref.shape[1]

    @pl.when(pl.program_id(0) == 0)
    def _():
        sums_ref[...] = jnp.zeros_like(sums_ref)

    def row_sums(k, gradient, values, at):
        first = gradient * with_ref[0, k : k + 1, :]
        second = gradient * (values - with_ref[1, k : k + 1, :])
        sums_ref[0:1, at] += jnp.sum(first.T, axis=0, keepdims=True)
        sums_ref[1:2, at] += jnp.sum(second.T, axis=0, keepdims=True)

    scale = HEAD_DIM ** (-0.5)
    low = lane_of(SUB)
    dk_sum[...] = jnp.zeros_like(dk_sum)
    dv_sum[...] = jnp.zeros_like(dv_sum)
    for r in range(t // SUB):
        here = slice(r * SUB, (r + 1) * SUB)
        start = c * t + r * SUB
        extent = start + SUB
        q = q_ref[0, here, :].astype(F32) * scale
        keys = k_ref[0, :extent, :]
        values = v_ref[0, :extent, :]
        dctx = dctx_ref[here, :]
        lse_t = lse_ref[here, :].T
        product_t = (ctx_ref[here, :].astype(F32) * dctx.astype(F32)).T
        low_keys = lane_of(extent)
        column = start + lax.broadcasted_iota(jnp.int32, (extent, SUB), 1)
        seen = lax.broadcasted_iota(jnp.int32, (extent, SUB), 0) <= column
        dq = jnp.zeros((SUB, PAIR), F32)
        for h in range(2):
            own = low if h == 0 else ~low
            q_own = jnp.where(own, q, 0.0).astype(BF)
            dctx_own = jnp.where(own, dctx, jnp.zeros_like(dctx))
            rows = slice(h * HEAD_DIM, (h + 1) * HEAD_DIM)
            row_dot = jnp.sum(product_t[rows, :], axis=0, keepdims=True)
            scores = dot(keys, q_own, NT) - lse_t[h * HEAD_DIM : h * HEAD_DIM + 1, :]
            probs = jnp.where(seen, jnp.exp(scores), 0.0)
            delta_probs = dot(values, dctx_own, NT)
            delta_scores = (probs * (delta_probs - row_dot)).astype(BF)
            dv_sum[:extent, :] += dot(probs.astype(BF), dctx_own)
            dk_sum[:extent, :] += dot(delta_scores, q_own)
            keys_own = jnp.where(low_keys if h == 0 else ~low_keys, keys, jnp.zeros_like(keys))
            dq = dq + dot(delta_scores, keys_own, TN)
        table = table_ref[:, start:extent, :]
        dq = turn_back(dq * scale, table)
        dq_ref[here, :] = dq.astype(BF)
        row_sums(0, dq, turn_back(q_ref[0, here, :].astype(F32), table), here)
    for r in range(t // SUB):
        here = slice(r * SUB, (r + 1) * SUB)
        table = table_ref[:, here, :]
        dk = turn_back(dk_sum[here, :], table)
        dk_ref[here, :] = dk.astype(BF)
        row_sums(1, dk, turn_back(k_ref[0, here, :].astype(F32), table), here)
        dv = dv_sum[here, :]
        dv_ref[here, :] = dv.astype(BF)
        row_sums(2, dv, v_ref[0, here, :].astype(F32), here)


def attend_back(heads, lse, ctx, dctx, tables, with_rows):
    t, width = heads.shape[1], heads.shape[2]
    own = pl.BlockSpec((t, PAIR), lambda p: (0, p))
    return kernel_call(
        functools.partial(attend_back_body, 0),
        (width // PAIR,),
        [heads, heads, heads, lse, ctx, dctx, tables, with_rows],
        [pl.BlockSpec((1, t, PAIR), lambda p, k=k: (k, 0, p)) for k in range(3)]
        + [own, own, own, still((3, t, PAIR), lambda p: (0, 0, 0)), pl.BlockSpec((2, 3, PAIR), lambda p: (0, 0, p))],
        [sds((t, width), BF)] * 3 + [sds((8, t), F32)],
        [own, own, own, pl.BlockSpec((8, t), lambda p: (0, 0))],
        scratch=[pltpu.VMEM((t, PAIR), F32)] * 2,
        mib=28,
        name="attend_back",
    )


def mlp_body(mid_ref, up_ref, gain_ref, shift_ref, gate_w_ref, up_w_ref, down_w_ref, normed_ref, stats_ref, hidden_ref, dgate_ref, dup_ref):
    @pl.when(pl.program_id(0) == 0)
    def _():
        norm_rows(mid_ref, gain_ref[...], shift_ref[...], normed_ref, stats_ref)

    normed = normed_ref[...]
    gate = dot(normed, gate_w_ref[...])
    upward = dot(normed, up_w_ref[...])
    delta_hidden = dot(up_ref[...], down_w_ref[...], NT)
    sigmoid = jax.nn.sigmoid(gate)
    silu = gate * sigmoid
    hidden_ref[...] = (silu * upward).astype(BF)
    dgate_ref[...] = (delta_hidden * upward * (sigmoid + silu * (1.0 - sigmoid))).astype(BF)
    dup_ref[...] = (delta_hidden * silu).astype(BF)


def mlp(c, mid, upstream, gain, shift, gate_w, up_w, down_w, previous):
    t, units = mid.shape[0], gate_w.shape[1]
    total = t * CHUNKS
    tile = 256
    one = lambda j: (0, 0)
    own = lambda j: (c, 0)
    column = pl.BlockSpec((t, tile), lambda j: (c, j))
    return kernel_call(
        mlp_body,
        (pl.cdiv(units, tile),),
        [mid, upstream, gain, shift, gate_w, up_w, down_w],
        [
            still((t, D), one),
            still((t, D), own),
            pl.BlockSpec((1, D), one),
            pl.BlockSpec((1, D), one),
            pl.BlockSpec((D, tile), lambda j: (0, j)),
            pl.BlockSpec((D, tile), lambda j: (0, j)),
            pl.BlockSpec((tile, D), lambda j: (j, 0)),
        ],
        [sds((total, D), BF), sds((total, 128), F32)] + [sds((total, units), BF)] * 3,
        [pl.BlockSpec((t, D), own), pl.BlockSpec((t, 128), own), column, column, column],
        previous,
        mib=46,
        name="mlp",
    )


def mlp_back_body(owners_ref, dgate_ref, dup_ref, gate_w_ref, up_w_ref, out_ref):
    out_ref[...] = (dot(dgate_ref[...], gate_w_ref[...], NT) + dot(dup_ref[...], up_w_ref[...], NT)).astype(BF)


def mlp_back(owners, width, dgate, dup, gate_w, up_w):
    t, units = dgate.shape
    whole = still((t, units), lambda j, owners: (0, 0))
    weight = pl.BlockSpec((width, units), lambda j, owners: (owners[j], 0))
    return prefetched(
        mlp_back_body,
        owners,
        (len(owners),),
        [dgate, dup, gate_w, up_w],
        [whole, whole, weight, weight],
        [sds((t, len(owners) * width), BF)],
        [pl.BlockSpec((t, width), lambda j, owners: (0, j))],
        mib=56,
        name="mlp_back",
    )[0]


def branch_back_body(e_ref, mid_ref, stats_ref, up_ref, weight_ref, means_ref, dbranch_ref, dctx_ref):
    rows = 64

    def step(i, carry):
        at = pl.ds(pl.multiple_of(i * rows, rows), rows)
        e = e_ref[at, :].astype(F32)
        mean, inverse = stats_ref[at, 0:1], stats_ref[at, 1:2]
        unit = (mid_ref[at, :].astype(F32) - mean) * inverse
        first = jnp.mean(e, axis=-1, keepdims=True)
        second = jnp.mean(e * unit, axis=-1, keepdims=True)
        dbranch_ref[at, :] = (up_ref[at, :].astype(F32) + inverse * (e - first - unit * second)).astype(BF)
        lane = lax.broadcasted_iota(jnp.int32, (rows, 128), 1)
        means_ref[at, :] = jnp.where(lane == 0, first, second)
        return carry

    lax.fori_loop(0, e_ref.shape[0] // rows, step, 0)
    dctx_ref[...] = dot(dbranch_ref[...], weight_ref[...], NT).astype(BF)


def branch_back(e, mid, stats, upstream, weight):
    t, width = e.shape[0], weight.shape[0]
    tile = SUB
    row = lambda i: (i, 0)
    return kernel_call(
        branch_back_body,
        (t // tile,),
        [e, mid, stats, upstream, weight],
        [
            pl.BlockSpec((tile, D), row),
            pl.BlockSpec((tile, D), row),
            pl.BlockSpec((tile, 128), row),
            pl.BlockSpec((tile, D), row),
            still((width, D), lambda i: (0, 0)),
        ],
        [sds((t, 128), F32), sds((t, D), BF), sds((t, width), BF)],
        [pl.BlockSpec((tile, 128), row), pl.BlockSpec((tile, D), row), pl.BlockSpec((tile, width), row)],
        mib=24,
        name="branch_back",
    )


def project_back_body(owners_ref, dq_ref, dk_ref, dv_ref, weight_ref, x_ref, stats_ref, below_ref, out_ref):
    n = dot(dq_ref[...], weight_ref[0], NT) + dot(dk_ref[...], weight_ref[1], NT) + dot(dv_ref[...], weight_ref[2], NT)
    out_ref[: n.shape[0], :] = n.astype(BF)
    unit = (x_ref[...].astype(F32) - stats_ref[:, 0:1]) * stats_ref[:, 1:2]
    with_unit = n * unit
    row = lax.broadcasted_iota(jnp.int32, (EXTRA, n.shape[1]), 0)
    gain_grad = jnp.sum(with_unit, axis=0, keepdims=True)
    shift_grad = jnp.sum(n, axis=0, keepdims=True)
    out_ref[n.shape[0] :, :] = jnp.where(row == 0, gain_grad, jnp.where(row == 1, shift_grad, below_ref[...])).astype(BF)


def project_back(owners, dq, dk, dv, weight, x, stats, below):
    t, width = dq.shape
    count = len(owners)
    whole = still((t, width), lambda j, owners: (0, 0))
    return prefetched(
        project_back_body,
        owners,
        (count,),
        [dq, dk, dv, weight, x, stats, below],
        [
            whole,
            whole,
            whole,
            pl.BlockSpec((3, width, width), lambda j, owners: (0, owners[j], 0)),
            pl.BlockSpec((t, width), lambda j, owners: (0, owners[j])),
            still((t, 128), lambda j, owners: (0, 0)),
            still((EXTRA, width), lambda j, owners: (0, 0)),
        ],
        [sds((t + EXTRA, count * width), BF)],
        [pl.BlockSpec((t + EXTRA, width), lambda j, owners: (0, j))],
        mib=56,
        name="project_back",
    )[0]


def add(a, b):
    return (a.astype(F32) + b.astype(F32)).astype(BF)


class Order:
    def __init__(self):
        self.before = ()

    def __call__(self, value):
        return after(value, *self.before) if self.before else value

    def done(self, *values):
        self.before = tuple(values)


class Gather:
    def __init__(self, share):
        self.n = lax.axis_size("tensor")
        self.pieces = [share]
        self.held = {(i, i): 0 for i in range(self.n)}
        self.steps = 0

    def send(self, piece, pairs, order):
        self.pieces.append(lax.ppermute(order(self.pieces[piece]), "tensor", pairs))

    def step(self, order):
        n, s = self.n, self.steps
        self.steps += 1
        before = len(self.pieces)
        if n == 4:
            outer, inner, out = [(0, 1), (1, 0), (2, 3), (3, 2)], [(1, 2), (2, 1)], [(1, 0), (2, 3)]
            for piece, pairs in (((0, outer), (0, inner)), ((2, out), (1, inner)), ((4, out),))[s]:
                self.send(piece, pairs, order)
            owners = ((1, None, 2, None, 3), (0, 2, None, 3, None), (3, 1, None, 0, None), (2, None, 1, None, 0))
            self.held = {(i, i): 0 for i in range(n)} | {
                (i, owner): 1 + k for i, row in enumerate(owners) for k, owner in enumerate(row) if owner is not None
            }
        else:
            up, down = (0, 0) if s == 0 else (before - 2, before - 1)
            self.held.update({(i + 1, i - s): before for i in range(s, n - 1)})
            self.held.update({(i, i + 1 + s): before + 1 for i in range(n - 1 - s)})
            self.send(up, [(i, i + 1) for i in range(s, n - 1)], order)
            self.send(down, [(i + 1, i) for i in range(n - 1 - s)], order)
        return self.pieces[before:]

    def last(self, order):
        got = self.step(order)
        while self.steps < self.n - 1:
            got = self.step(order)
        return got

    def whole(self):
        share = self.pieces[0]
        t, width = share.shape
        return prefetched(
            functools.partial(assemble_body, self.held),
            [lax.axis_index("tensor")],
            (self.n,),
            self.pieces,
            [still((t, width), lambda j, me: (0, 0))] * len(self.pieces),
            [sds((t, self.n * width), share.dtype)],
            [pl.BlockSpec((t, width), lambda j, me: (0, j))],
            mib=14,
            name="assemble",
        )[0]


def steps(order, *ops):
    return [got for op in ops if op.steps < op.n - 1 for got in op.step(order)]


def finish(order, *ops):
    got = steps(order, *ops)
    while any(op.steps < op.n - 1 for op in ops):
        got = steps(order, *ops)
    return got


def scatter_order(n):
    me = lax.axis_index("tensor")
    first = jnp.where(me < n // 2, n - 1, 0)
    return [(first + k) % n for k in range(n)]


class Scatter:
    def __init__(self, first, rest):
        self.n, self.me = lax.axis_size("tensor"), lax.axis_index("tensor")
        self.first, self.rest, self.steps, self.got = first, rest, 0, {}
        self.width = first.shape[1]

    def part(self, owner, *got):
        place = (owner - jnp.where(self.me < self.n // 2, self.n - 1, 0) - 1) % self.n
        place = jnp.clip(place, 0, self.n - 2)
        value = lax.dynamic_slice_in_dim(self.rest, place * self.width, self.width, 1)
        return functools.reduce(add, got, value)

    def any(self, owner, *got):
        first = jnp.where(self.me < self.n // 2, self.n - 1, 0)
        value = jnp.where(owner % self.n == first, self.first, self.part(owner % self.n))
        return functools.reduce(add, got, value)

    def send(self, name, value, pairs, order):
        self.got[name] = lax.ppermute(order(value), "tensor", pairs)

    def step(self, order):
        n, me, s = self.n, self.me, self.steps
        self.got = got = {name: order(value) for name, value in self.got.items()}
        self.steps += 1
        if n == 4:
            inward, inner, outer = [(0, 1), (3, 2)], [(1, 2), (2, 1)], [(0, 1), (1, 0), (2, 3), (3, 2)]
            if s == 0:
                self.send("far", self.first, inward, order)
                return [got["far"]]
            if s == 1:
                self.send("far", add(self.first, got["far"]), inner, order)
                self.send("next", self.part(jnp.where(me == 0, 2, 1)), inward, order)
            else:
                self.send("far", self.part(me ^ 1, got["far"]), outer, order)
                self.send("next", self.part(3 - me, got["next"]), inner, order)
            return [got["far"], got["next"]]
        up, down = ((got["up"],), (got["down"],)) if s else ((), ())
        self.send("up", self.any(me + n - 1 - s, *up), [(i, i + 1) for i in range(s + 1)], order)
        self.send("down", self.any(me - n + 1 + s, *down), [(i + 1, i) for i in range(n - 2 - s, n - 1)], order)
        return [got["up"], got["down"]]

    def last(self, order):
        got = self.step(order)
        while self.steps < self.n - 1:
            got = self.step(order)
        return got

    def total(self, order):
        self.got = {name: order(value) for name, value in self.got.items()}
        own = self.any(self.me) if self.n != 4 else self.part(self.me)
        return sum((g.astype(F32) for g in self.got.values()), own.astype(F32))


def assemble_body(held, me_ref, *refs):
    out_ref, owner, me = refs[-1], pl.program_id(0), me_ref[0]
    for k, ref in enumerate(refs[:-1]):
        places = [(device, o) for (device, o), at in held.items() if at == k]
        here = functools.reduce(jnp.logical_or, [(me == device) & (owner == o) for device, o in places])

        @pl.when(here)
        def _(ref=ref):
            out_ref[...] = ref[...]


def gradients_body(groups, join, which_ref, *refs):
    lefts, rest = refs[: len(groups)], refs[len(groups) :]
    rights, outs = rest[: sum(groups)], rest[sum(groups) :]
    k = 0
    for left, count in zip(lefts, groups):
        turned = left[...].T
        for right in rights[k : k + count]:
            wide = right.shape[1]
            at = k % join * wide
            outs[k // join][:, at : at + wide] = dot(turned, right[...]).astype(BF)
            k += 1


def gradients(which, pairs, name, join=1):
    t = pairs[0][0].shape[0]
    block = 256
    nb = D // 2 // block
    lefts, rights = [left for left, _ in pairs], [right for _, some in pairs for right in some]
    wide = join * rights[0].shape[1]
    return prefetched(
        functools.partial(gradients_body, [len(some) for _, some in pairs], join),
        [which],
        (nb,),
        lefts + rights,
        [pl.BlockSpec((t, block), lambda i, which: (0, which[0] * nb + i))] * len(lefts)
        + [still(right.shape, lambda i, which: (0, 0)) for right in rights],
        [sds((D // 2, wide), BF)] * (len(rights) // join),
        [pl.BlockSpec((block, wide), lambda i, which: (i, 0))] * (len(rights) // join),
        mib=56,
        name=name,
    )


def mlp_out_body(owners_ref, hidden_ref, weight_ref, first_ref, rest_ref):
    out = dot(hidden_ref[...], weight_ref[...]).astype(BF)

    @pl.when(pl.program_id(0) == 0)
    def _():
        first_ref[...] = out

    @pl.when(pl.program_id(0) > 0)
    def _():
        rest_ref[...] = out


def mlp_out(owners, width, hidden, weight):
    t, units = hidden.shape
    return prefetched(
        mlp_out_body,
        owners,
        (len(owners),),
        [hidden, weight],
        [
            still((t, units), lambda j, owners: (0, 0)),
            pl.BlockSpec((units, width), lambda j, owners: (0, owners[j])),
        ],
        [sds((t, width), BF), sds((t, D - width), BF)],
        [
            pl.BlockSpec((t, width), lambda j, owners: (0, 0)),
            pl.BlockSpec((t, width), lambda j, owners: (0, jnp.maximum(j - 1, 0))),
        ],
        mib=22,
        name="mlp_out",
    )


def swap(value, bit, axis="dp"):
    n = lax.axis_size(axis)
    return lax.ppermute(value, axis, [(i, i ^ (1 << bit)) for i in range(n)])


def split_body(groups, bits_ref, *refs):
    parts, outs = refs[: 4 * groups], refs[4 * groups :]
    for part in range(2):
        for phase in range(2):

            @pl.when(pl.program_id(0) == phase)
            def _(part=part, phase=phase):
                at = 0
                for g in range(groups):
                    keep, got = parts[2 * (part * groups + g)], parts[2 * (part * groups + g) + 1]
                    wide = keep.shape[1]
                    outs[2 * part + phase][:, at : at + wide] = add(keep[...], got[...])
                    at += wide


def split(upper, lower, bits, joined):
    groups = len(upper)
    rows = upper[0][0].shape[0] // (4 if joined else 2)
    block = min(128, rows)
    nb = rows // block
    columns = sum(keep.shape[1] for keep, _ in upper)
    ins, in_specs = [], []
    for part, pairs in enumerate((upper, lower)):
        first = 2 * nb * part if joined else 0

        def index(phase, j, bits, part=part, first=first):
            half = jnp.where(phase == 0, 1 - bits[part], bits[part])
            return (first + half * nb + j, 0)

        for pair in pairs:
            for array in pair:
                ins.append(array)
                in_specs.append(pl.BlockSpec((block, array.shape[1]), index))
    given = pl.BlockSpec((block, columns), lambda phase, j, bits: (jnp.where(phase == 0, j, nb - 1), 0))
    kept = pl.BlockSpec((block, columns), lambda phase, j, bits: (jnp.where(phase == 0, 0, j), 0))
    return prefetched(
        functools.partial(split_body, groups),
        bits,
        (2, nb),
        ins,
        in_specs,
        [sds((rows, columns), BF)] * 4,
        [given, kept] * 2,
        mib=56,
        name="split",
    )


def merge_body(widths, bits_ref, *refs):
    for part in range(2):
        for which in range(2):

            @pl.when((pl.program_id(0) == bits_ref[part]) == (which == 0))
            def _(part=part, which=which):
                value = refs[2 * part + which][...]
                if widths:
                    at = 0
                    for out, wide in zip(refs[4:], widths):
                        out[part] = value[:, at : at + wide]
                        at += wide
                else:
                    refs[4 + part][...] = value


def merge(upper, lower, bits, widths=()):
    rows, columns = upper[0].shape
    block = min(128, rows)
    nb = rows // block

    def spec(part, which):
        def index(i, j, bits):
            half = bits[part] if which == 0 else 1 - bits[part]
            return (jnp.where(i == half, j, jnp.where(i < half, 0, nb - 1)), 0)

        return pl.BlockSpec((block, columns), index)

    if widths:
        outs = [sds((2, 2 * rows, wide), BF) for wide in widths]
        out_specs = [pl.BlockSpec((2, block, wide), lambda i, j, bits: (0, i * nb + j, 0)) for wide in widths]
    else:
        outs = [sds((2 * rows, columns), BF)] * 2
        out_specs = [pl.BlockSpec((block, columns), lambda i, j, bits: (i * nb + j, 0))] * 2
    return prefetched(
        functools.partial(merge_body, widths),
        bits,
        (2, nb),
        [*upper, *lower],
        [spec(part, which) for part in range(2) for which in range(2)],
        outs,
        out_specs,
        mib=56,
        name="merge",
    )


def sum_over_dp(given, order):
    me, n = lax.axis_index("dp"), lax.axis_size("dp")
    count = n.bit_length() - 1
    bit = lambda b: (me >> b) & 1
    orders = [list(range(1, count)), list(range(count - 1, 0, -1))]
    got = [swap(g, 0) for g in given]
    kept = yield got
    upper = lower = [(order(k), g) for k, g in zip(kept, got)]
    for s in range(count - 1):
        a, b = orders[0][s], orders[1][s]
        p_give, p_keep, q_give, q_keep = split(upper, lower, [bit(a), bit(b)], s == 0)
        upper, lower = [(p_keep, swap(p_give, a))], [(q_keep, swap(q_give, b))]
        yield p_keep
        upper, lower = [(order(upper[0][0]), upper[0][1])], [(order(lower[0][0]), lower[0][1])]
    p, q = add(*upper[0]), add(*lower[0])
    for s in reversed(range(count - 1)):
        a, b = orders[0][s], orders[1][s]
        p, q = lax.optimization_barrier((p, q))
        got = swap(p, a), swap(q, b)
        yield p
        out = merge([order(p), got[0]], [q, got[1]], [bit(a), bit(b)], () if s else [g.shape[1] for g in given])
        if s:
            p, q = out
    own = [array.reshape(-1, array.shape[2]) for array in out]
    other = [swap(array, 0) for array in own]
    yield own[0]
    yield own, other


def finish_sum(steps_left):
    *_, last = steps_left
    return last


def halves(core, own, other, nb):
    def index(mine):
        def of(i, bits):
            half = bits[0] if mine else 1 - bits[0]
            return (jnp.clip(i - half * nb, 0, nb - 1), 0)

        return of

    return index(True), index(False)


def halves_body(store, core_ref, *refs):
    half = pl.program_id(0) // (pl.num_programs(0) // 2)
    groups = store.groups
    own, other, outs = refs[:groups], refs[groups : 2 * groups], refs[2 * groups :]
    for arrays, mine in ((own, True), (other, False)):

        @pl.when((half == core_ref[0]) == mine)
        def _(arrays=arrays):
            store(arrays, outs)


def from_halves(store, core, own, other, outs, out_specs, block, mib, name):
    store.groups = len(own)
    nb = own[0].shape[0] // block
    return prefetched(
        functools.partial(halves_body, store),
        [core],
        (2 * nb,),
        [*own, *other],
        [
            pl.BlockSpec((block, array.shape[1]), index)
            for arrays, index in zip((own, other), halves(core, own, other, nb))
            for array in arrays
        ],
        outs,
        out_specs,
        mib=mib,
        name=name,
    )


def gate_up_out(core, own, other):
    def store(arrays, outs):
        for k in range(2):
            outs[0][:, k, :] = arrays[k][...].astype(F32)

    units, block = own[0].shape[1], 128
    outs, spec = [sds((D, 2, units), F32)], [pl.BlockSpec((block, 2, units), lambda i, c: (i, 0, 0))]
    return from_halves(store, core, own, other, outs, spec, block, 56, "gate_up_out")[0]


def down_out(core, own, other):
    def store(arrays, outs):
        outs[0][...] = arrays[0][...].astype(F32).T

    units, block = own[0].shape[1], 128
    outs, spec = [sds((units, D), F32)], [pl.BlockSpec((units, block), lambda i, c: (0, i))]
    return from_halves(store, core, own, other, outs, spec, block, 56, "down_out")[0]


def attention_out(core, own, other):
    def store(arrays, outs):
        for k in range(3):
            outs[0][k] = arrays[k // 2][:, k % 2 * width : (k % 2 + 1) * width].astype(F32)
        outs[1][...] = arrays[1][:, width:].astype(F32).T

    width, block = own[0].shape[1] // 2, 256
    outs = [sds((3, D, width), F32), sds((width, D), F32)]
    specs = [
        pl.BlockSpec((3, block, width), lambda i, c: (0, i, 0)),
        pl.BlockSpec((width, block), lambda i, c: (0, i)),
    ]
    return from_halves(store, core, own, other, outs, specs, block, 56, "attention_out")


def per_device(
    tokens,
    norm_one_gain,
    norm_one_shift,
    project_weight,
    project_bias,
    output_weight,
    norm_two_gain,
    norm_two_shift,
    gate_up_weight,
    down_weight,
    cotangent,
):
    width = tokens.shape[1]
    t = tokens.shape[0] // CHUNKS
    offset = lax.axis_index("tensor") * width
    core = lax.axis_index("dp") & 1
    mine = lambda full: lax.dynamic_slice_in_dim(full, offset, width, full.ndim - 1)
    half_of = lambda array, which: lax.dynamic_slice_in_dim(array, which * (D // 2), D // 2, 1)
    order = Order()

    small = jnp.stack([norm_one_gain, norm_one_shift, norm_two_gain, norm_two_shift])
    whole_x = Gather(jnp.concatenate([tokens, jnp.pad(small, ((0, EXTRA - 4), (0, 0)))]))
    whole_up = Gather(cotangent)
    got = whole_x.step(order)
    gate_w = order(gate_up_weight)[:, 0]
    order.done(*got, gate_w)
    got = whole_x.step(order)
    up_w = order(gate_up_weight)[:, 1]
    tables = rope_tables()
    order.done(*got, up_w, tables)
    whole_x.last(order)
    x = whole_x.whole()
    gain_one, gain_two, shift_two = (x[t + i : t + i + 1].astype(F32) for i in (0, 2, 3))
    project_w = project_weight.transpose(1, 0, 2)
    bias = project_bias.astype(F32)[:, None, :]

    through = lambda row: jnp.einsum("d,kdc->kc", row[0].astype(BF), project_w, preferred_element_type=F32)
    with_rows = jnp.stack([through(gain_one), through(x[t + 1 : t + 2]) + bias[:, 0]])

    order.done(x)
    got = whole_up.step(order)
    normed_one, stats_one, heads = project(0, x, project_w, bias, tables, ())
    order.done(*got, stats_one)
    owners = scatter_order(whole_up.n)
    first, rest, context, lse = attend(owners, order(heads), output_weight)
    order.done(lse)
    branch = Scatter(first, rest)
    for _ in range(2):
        order.done(*whole_up.step(order), *branch.step(order), with_rows)
    if whole_up.n > 4:
        whole_up.last(order)
    branch.last(order)
    upstream = whole_up.whole()
    middle_share = tokens.astype(F32) + branch.total(order)
    middle_sent = (middle_share - stats_one[:, 0:1]).astype(BF)
    order.done(middle_sent)
    whole_middle = Gather(middle_sent)
    while whole_middle.steps < whole_middle.n - 1:
        whole_middle.step(order)
    middle = whole_middle.whole()

    normed_two, stats_two, hidden, dgate, dup = mlp(
        0, middle, upstream, gain_two, shift_two, gate_w, up_w, down_weight, ()
    )
    first = mlp_back(owners[:1], width, dgate, dup, gate_w, up_w)
    rest = mlp_back(owners[1:], width, after(dgate, first), dup, gate_w, up_w)
    order.done(first)
    delta_two = Scatter(first, rest)
    got = steps(order, delta_two)
    order.done(rest, *got)
    got = steps(order, delta_two)
    mlp_grads = lambda which, name: gradients(
        which, [(normed_two, [order(dgate), dup]), (upstream, [hidden])], name
    )
    mlp_given = mlp_grads(1 - core, "mlp_given")
    mlp_sum = sum_over_dp(mlp_given, order)
    next(mlp_sum)
    order.done(*got, *mlp_given)
    got = finish(order, delta_two)
    mlp_kept = mlp_grads(core, "mlp_kept")
    order.done(*got, *mlp_kept)
    delta_two = delta_two.total(order)
    unit_two = (mine(middle).astype(F32) - stats_two[:, 0:1]) * stats_two[:, 1:2]
    two_grads = [jnp.sum(delta_two * unit_two, axis=0), jnp.sum(delta_two, axis=0)]
    e_own = delta_two * norm_two_gain.astype(F32)
    e_sent = e_own.astype(BF)
    order.done(e_sent)
    whole_e = Gather(e_sent)
    got = steps(order, whole_e)
    held = mlp_sum.send(mlp_kept)
    order.done(*got, held)
    got = steps(order, whole_e)
    mlp_share = Scatter(*mlp_out(owners, width, order(hidden), down_weight))
    order.done(*got, mlp_share.rest)
    got = finish(order, whole_e) + steps(order, mlp_share)
    held = next(mlp_sum)
    e = whole_e.whole()

    order.done(e, held, *got)
    share_got = steps(order, mlp_share)
    means_two, dbranch, dctx = branch_back(order(e), middle, stats_two, upstream, output_weight)
    order.done(dctx)
    held = next(mlp_sum)
    order.done(held)
    dq, dk, dv, sums = attend_back(heads, lse, context, order(dctx), tables, with_rows)
    held = next(mlp_sum)
    order.done(dq, held, *share_got)
    delta_heads = (dq, dk, dv)
    sum_rows = 2 * t // width
    below = jnp.pad(sums[:2].reshape(sum_rows, width), ((2, EXTRA - 2 - sum_rows), (0, 0)))
    back = lambda owners, dq: project_back(owners, dq, dk, dv, project_w, x, stats_one, below)
    first = back(owners[:1], order(dq))
    rest = back(owners[1:], after(dq, first))
    order.done(first)
    delta_one = Scatter(first, rest)
    got = steps(order, delta_one)
    order.done(rest)
    attention_grads = lambda which, name: gradients(
        which, [(normed_one, [order(dq), dk, dv]), (dbranch, [context])], name, join=2
    )
    attention_given = attention_grads(1 - core, "attention_given")
    attention_sum = sum_over_dp(attention_given, order)
    next(attention_sum)
    order.done(*attention_given)
    attention_kept = attention_grads(core, "attention_kept")
    order.done(*attention_kept, *got)
    got = steps(order, delta_one)
    held = attention_sum.send(attention_kept)
    order.done(held)
    held = next(mlp_sum)
    order.done(held, *got)
    got = finish(order, delta_one)
    held = next(attention_sum)
    order.done(held)
    held = next(attention_sum)
    order.done(held, *got)
    if lax.axis_size("dp") > 8:
        for _ in range(2):
            order.done(next(mlp_sum))
            order.done(next(attention_sum))
    held = next(attention_sum)
    order.done(held)
    mlp_halves = next(mlp_sum)
    gate_up_grad = gate_up_out(core, [order(mlp_halves[0][0]), mlp_halves[0][1]], mlp_halves[1][:2])
    order.done(gate_up_grad)
    delta_one = delta_one.total(order)
    bias_grad = [jnp.sum(a, axis=0, dtype=F32) for a in delta_heads]
    small = jnp.stack([delta_one[t], delta_one[t + 1], *two_grads, *bias_grad])
    small = small + swap(small, 0)
    order.done(small)
    held = next(attention_sum)
    order.done(held)
    finish(order, mlp_share)
    devices = lax.axis_size("dp")
    others = [lax.ppermute(order(small), "dp", [(i, i ^ k) for i in range(devices)]) for k in range(2, devices, 2)]
    down_grad = down_out(core, [order(mlp_halves[0][2])], mlp_halves[1][2:])
    order.done(down_grad)
    result = (middle_share + mlp_share.total(order)).astype(BF)
    sums = (delta_one[t + 2 : t + 2 + sum_rows] / D).reshape(2, t).T
    unit_one = (tokens.astype(F32) - stats_one[:, 0:1]) * stats_one[:, 1:2]
    dmid = cotangent.astype(F32) + stats_two[:, 1:2] * (e_own - means_two[:, 0:1] - unit_two * means_two[:, 1:2])
    tokens_grad = order(dmid) + stats_one[:, 1:2] * (
        delta_one[:t] * norm_one_gain.astype(F32) - sums[:, 0:1] - unit_one * sums[:, 1:2]
    )
    small = sum((order(other) for other in others), small)
    order.done(tokens_grad, small, result)
    attention_halves = next(attention_sum)
    project_grad, output_grad = attention_out(
        core, [order(attention_halves[0][0]), *attention_halves[0][1:]], attention_halves[1]
    )
    return (
        result,
        tokens_grad,
        small[0],
        small[1],
        project_grad.transpose(1, 0, 2),
        small[4:7],
        output_grad,
        small[2],
        small[3],
        gate_up_grad,
        down_grad,
    )


def solution(mesh):
    return jax.shard_map(
        per_device,
        mesh=mesh,
        in_specs=(
            P("dp", "tensor"),
            P("tensor"),
            P("tensor"),
            P(None, None, "tensor"),
            P(None, "tensor"),
            P("tensor", None),
            P("tensor"),
            P("tensor"),
            P(None, None, "tensor"),
            P("tensor", None),
            P("dp", "tensor"),
        ),
        out_specs=(
            P("dp", "tensor"),
            P("dp", "tensor"),
            P("tensor"),
            P("tensor"),
            P(None, None, "tensor"),
            P(None, "tensor"),
            P("tensor", None),
            P("tensor"),
            P("tensor"),
            P(None, None, "tensor"),
            P("tensor", None),
        ),
        check_vma=False,
    )
```

```python
import functools

import jax
import jax.numpy as jnp
from jax import lax
from jax.experimental import pallas as pl
from jax.experimental.pallas import tpu as pltpu
from jax.sharding import PartitionSpec as P

D = 2048
HEAD_DIM = 64
ROT = 16
SEQ = 1024
PAIR = 2 * HEAD_DIM
CHUNKS = 1
SUB = 256
WEIGHTS = {"mlp_kept": 30, "mlp_out": 10, "attend_back": 20, "attention_kept": 40}
EXTRA = 16

EPSILON = 1e-05
ROPE_BASE = 10000.0
BF = jnp.bfloat16
F32 = jnp.float32
NT = (((1,), (1,)), ((), ()))
TN = (((0,), (0,)), ((), ()))
ANY = pl.BlockSpec(memory_space=pl.ANY)


def dot(a, b, dims=(((1,), (0,)), ((), ()))):
    return lax.dot_general(a, b, dims, preferred_element_type=F32)


def params(mib):
    return pltpu.CompilerParams(vmem_limit_bytes=mib << 20)


def cost(name):
    return pl.CostEstimate(flops=int(WEIGHTS.get(name, 0) * 1e9), bytes_accessed=0, transcendentals=0)


def after(value, *others):
    return lax.optimization_barrier((value, *others))[0]


def kernel_call(body, grid, ins, in_specs, outs, out_specs, previous=(), scratch=(), mib=56, name=None):
    given = len(ins)
    previous = dict(previous)
    aliases = {given + i: out for i, out in enumerate(previous)}

    def run(*refs):
        body(*refs[:given], *refs[given + len(previous) :])

    return pl.pallas_call(
        run,
        grid=grid,
        in_specs=list(in_specs) + [ANY] * len(previous),
        out_specs=list(out_specs),
        out_shape=list(outs),
        input_output_aliases=aliases,
        scratch_shapes=list(scratch),
        compiler_params=params(mib),
        cost_estimate=cost(name),
        name=name,
    )(*ins, *previous.values())


def still(block, index):
    return pl.BlockSpec(block, index, pipeline_mode=pl.Buffered(1))


def sds(shape, dtype):
    return jax.ShapeDtypeStruct(shape, dtype)


def prefetched(body, scalars, grid, ins, in_specs, outs, out_specs, mib=56, name=None):
    return pl.pallas_call(
        body,
        grid_spec=pltpu.PrefetchScalarGridSpec(
            num_scalar_prefetch=1, grid=grid, in_specs=in_specs, out_specs=out_specs
        ),
        out_shape=outs,
        compiler_params=params(mib),
        cost_estimate=cost(name),
        name=name,
    )(jnp.stack(scalars).astype(jnp.int32), *ins)


def norm_rows(x_ref, gain, shift, normed_ref, stats_ref, rows=64):
    def step(i, carry):
        at = pl.ds(pl.multiple_of(i * rows, rows), rows)
        x = x_ref[at, :].astype(F32)
        mean = jnp.mean(x, axis=-1, keepdims=True)
        centered = x - mean
        inverse = lax.rsqrt(jnp.mean(centered * centered, axis=-1, keepdims=True) + EPSILON)
        normed_ref[at, :] = (centered * inverse * gain + shift).astype(BF)
        lane = lax.broadcasted_iota(jnp.int32, (rows, 128), 1)
        stats_ref[at, :] = jnp.where(lane == 0, mean, inverse)
        return carry

    lax.fori_loop(0, x_ref.shape[0] // rows, step, 0)


def rope_tables():
    lane = jnp.arange(PAIR, dtype=jnp.int32)[None, :] % HEAD_DIM
    half = ROT // 2
    index = (lane % half).astype(F32)
    angles = jnp.arange(SEQ, dtype=F32)[:, None] * ROPE_BASE ** (-(index * (2.0 / ROT)))
    turned = lane < ROT
    cosine = jnp.where(turned, jnp.cos(angles), 1.0)
    low = jnp.where(turned & (lane >= half), jnp.sin(angles), 0.0)
    high = jnp.where(lane < half, -jnp.sin(angles), 0.0)
    return jnp.stack([cosine, low, high])


def turn(values, table):
    half = ROT // 2
    return (
        values * table[0]
        + pltpu.roll(values, half, 1) * table[1]
        + pltpu.roll(values, values.shape[1] - half, 1) * table[2]
    )


def turn_back(values, table):
    half = ROT // 2
    return (
        values * table[0]
        - pltpu.roll(values, half, 1) * table[1]
        - pltpu.roll(values, values.shape[1] - half, 1) * table[2]
    )


def project_body(x_ref, small_ref, weight_ref, bias_ref, table_ref, normed_ref, stats_ref, heads_ref):
    part = pl.program_id(0)

    @pl.when(part == 0)
    def _():
        gain, shift = (small_ref[k : k + 1, :].astype(F32) for k in (0, 1))
        norm_rows(x_ref, gain, shift, normed_ref, stats_ref)

    out = dot(normed_ref[...], weight_ref[0]) + bias_ref[0]
    width = out.shape[1]

    @pl.when(part < 2)
    def _():
        table = table_ref[...]
        for p in range(width // PAIR):
            heads_ref[0, :, p * PAIR : (p + 1) * PAIR] = turn(out[:, p * PAIR : (p + 1) * PAIR], table).astype(BF)

    @pl.when(part == 2)
    def _():
        heads_ref[0] = out.astype(BF)


def project(c, x, weight, bias, tables, previous):
    t, width = x.shape[0] - EXTRA, weight.shape[2]
    total = t * CHUNKS
    one = lambda k: (0, 0)
    return kernel_call(
        project_body,
        (3,),
        [x, x, weight, bias, tables],
        [
            still((t, D), one),
            pl.BlockSpec((EXTRA, D), lambda k: (t // EXTRA, 0)),
            pl.BlockSpec((1, D, width), lambda k: (k, 0, 0)),
            pl.BlockSpec((1, 1, width), lambda k: (k, 0, 0)),
            still((3, t, PAIR), lambda k: (0, c, 0)),
        ],
        [sds((total, D), BF), sds((total, 128), F32), sds((3, total, width), BF)],
        [
            pl.BlockSpec((t, D), lambda k: (c, 0)),
            pl.BlockSpec((t, 128), lambda k: (c, 0)),
            pl.BlockSpec((1, t, width), lambda k: (k, c, 0)),
        ],
        previous,
        mib=34,
        name="project",
    )


def lane_of(rows):
    return lax.broadcasted_iota(jnp.int32, (rows, PAIR), 1) < HEAD_DIM


def attend_body(c, owners_ref, q_ref, k_ref, v_ref, out_weight_ref, first_ref, rest_ref, ctx_ref, lse_ref):
    pair = pl.program_id(0)
    t = q_ref.shape[1]
    scale = HEAD_DIM ** (-0.5)
    low = lane_of(SUB)
    for r in range(t // SUB):
        start = c * t + r * SUB
        extent = start + SUB
        q = q_ref[0, r * SUB : (r + 1) * SUB, :].astype(F32) * scale
        keys = k_ref[0, :extent, :]
        values = v_ref[0, :extent, :]
        row = start + lax.broadcasted_iota(jnp.int32, (SUB, extent), 0)
        seen = lax.broadcasted_iota(jnp.int32, (SUB, extent), 1) <= row
        contexts, sums = [], []
        for h in range(2):
            own = jnp.where(low if h == 0 else ~low, q, 0.0).astype(BF)
            scores = jnp.where(seen, dot(own, keys, NT), -1000000000.0)
            top = jnp.max(scores, axis=-1, keepdims=True)
            raised = jnp.exp(scores - top)
            total = jnp.sum(raised, axis=-1, keepdims=True)
            contexts.append(dot(raised.astype(BF), values) / total)
            sums.append(top + jnp.log(total))
        at = pl.ds(pl.multiple_of(pair * PAIR, PAIR), PAIR)
        ctx_ref[r * SUB : (r + 1) * SUB, at] = jnp.where(low, contexts[0], contexts[1]).astype(BF)
        lse_ref[r * SUB : (r + 1) * SUB, :] = jnp.where(low, sums[0], sums[1])

    @pl.when(pair == pl.num_programs(0) - 1)
    def _():
        wide = first_ref.shape[1]
        for j in range(D // wide):
            at = pl.ds(pl.multiple_of(owners_ref[j] * wide, wide), wide)
            out = dot(ctx_ref[...], out_weight_ref[:, at]).astype(BF)
            if j == 0:
                first_ref[...] = out
            else:
                rest_ref[:, (j - 1) * wide : j * wide] = out


def attend(owners, heads, out_weight):
    t, width = heads.shape[1], heads.shape[2]
    here = lambda p, owners: (0, p)
    fixed = lambda p, owners: (0, 0)
    return prefetched(
        functools.partial(attend_body, 0),
        owners,
        (width // PAIR,),
        [heads, heads, heads, out_weight],
        [pl.BlockSpec((1, t, PAIR), lambda p, owners, k=k: (k, 0, p)) for k in range(3)]
        + [still((width, D), fixed)],
        [sds((t, width), BF), sds((t, D - width), BF), sds((t, width), BF), sds((t, width), F32)],
        [
            pl.BlockSpec((t, width), fixed),
            pl.BlockSpec((t, D - width), fixed),
            pl.BlockSpec((t, width), fixed),
            pl.BlockSpec((t, PAIR), here),
        ],
        mib=30,
        name="attend",
    )


def attend_back_body(c, *refs):
    q_ref, k_ref, v_ref, lse_ref, ctx_ref, dctx_ref, table_ref, with_ref, dq_ref, dk_ref, dv_ref, sums_ref, dk_sum, dv_sum = refs
    t = q_ref.shape[1]

    @pl.when(pl.program_id(0) == 0)
    def _():
        sums_ref[...] = jnp.zeros_like(sums_ref)

    def row_sums(k, gradient, values, at):
        first = gradient * with_ref[0, k : k + 1, :]
        second = gradient * (values - with_ref[1, k : k + 1, :])
        sums_ref[0:1, at] += jnp.sum(first.T, axis=0, keepdims=True)
        sums_ref[1:2, at] += jnp.sum(second.T, axis=0, keepdims=True)

    scale = HEAD_DIM ** (-0.5)
    low = lane_of(SUB)
    dk_sum[...] = jnp.zeros_like(dk_sum)
    dv_sum[...] = jnp.zeros_like(dv_sum)
    for r in range(t // SUB):
        here = slice(r * SUB, (r + 1) * SUB)
        start = c * t + r * SUB
        extent = start + SUB
        q = q_ref[0, here, :].astype(F32) * scale
        keys = k_ref[0, :extent, :]
        values = v_ref[0, :extent, :]
        dctx = dctx_ref[here, :]
        lse_t = lse_ref[here, :].T
        product_t = (ctx_ref[here, :].astype(F32) * dctx.astype(F32)).T
        low_keys = lane_of(extent)
        column = start + lax.broadcasted_iota(jnp.int32, (extent, SUB), 1)
        seen = lax.broadcasted_iota(jnp.int32, (extent, SUB), 0) <= column
        dq = jnp.zeros((SUB, PAIR), F32)
        for h in range(2):
            own = low if h == 0 else ~low
            q_own = jnp.where(own, q, 0.0).astype(BF)
            dctx_own = jnp.where(own, dctx, jnp.zeros_like(dctx))
            rows = slice(h * HEAD_DIM, (h + 1) * HEAD_DIM)
            row_dot = jnp.sum(product_t[rows, :], axis=0, keepdims=True)
            scores = dot(keys, q_own, NT) - lse_t[h * HEAD_DIM : h * HEAD_DIM + 1, :]
            probs = jnp.where(seen, jnp.exp(scores), 0.0)
            delta_probs = dot(values, dctx_own, NT)
            delta_scores = (probs * (delta_probs - row_dot)).astype(BF)
            dv_sum[:extent, :] += dot(probs.astype(BF), dctx_own)
            dk_sum[:extent, :] += dot(delta_scores, q_own)
            keys_own = jnp.where(low_keys if h == 0 else ~low_keys, keys, jnp.zeros_like(keys))
            dq = dq + dot(delta_scores, keys_own, TN)
        table = table_ref[:, start:extent, :]
        dq = turn_back(dq * scale, table)
        dq_ref[here, :] = dq.astype(BF)
        row_sums(0, dq, turn_back(q_ref[0, here, :].astype(F32), table), here)
    for r in range(t // SUB):
        here = slice(r * SUB, (r + 1) * SUB)
        table = table_ref[:, here, :]
        dk = turn_back(dk_sum[here, :], table)
        dk_ref[here, :] = dk.astype(BF)
        row_sums(1, dk, turn_back(k_ref[0, here, :].astype(F32), table), here)
        dv = dv_sum[here, :]
        dv_ref[here, :] = dv.astype(BF)
        row_sums(2, dv, v_ref[0, here, :].astype(F32), here)


def attend_back(heads, lse, ctx, dctx, tables, with_rows):
    t, width = heads.shape[1], heads.shape[2]
    own = pl.BlockSpec((t, PAIR), lambda p: (0, p))
    return kernel_call(
        functools.partial(attend_back_body, 0),
        (width // PAIR,),
        [heads, heads, heads, lse, ctx, dctx, tables, with_rows],
        [pl.BlockSpec((1, t, PAIR), lambda p, k=k: (k, 0, p)) for k in range(3)]
        + [own, own, own, still((3, t, PAIR), lambda p: (0, 0, 0)), pl.BlockSpec((2, 3, PAIR), lambda p: (0, 0, p))],
        [sds((t, width), BF)] * 3 + [sds((8, t), F32)],
        [own, own, own, pl.BlockSpec((8, t), lambda p: (0, 0))],
        scratch=[pltpu.VMEM((t, PAIR), F32)] * 2,
        mib=28,
        name="attend_back",
    )


def mlp_body(mid_ref, up_ref, gain_ref, shift_ref, gate_w_ref, up_w_ref, down_w_ref, normed_ref, stats_ref, hidden_ref, dgate_ref, dup_ref):
    @pl.when(pl.program_id(0) == 0)
    def _():
        norm_rows(mid_ref, gain_ref[...], shift_ref[...], normed_ref, stats_ref)

    normed = normed_ref[...]
    gate = dot(normed, gate_w_ref[...])
    upward = dot(normed, up_w_ref[...])
    delta_hidden = dot(up_ref[...], down_w_ref[...], NT)
    sigmoid = jax.nn.sigmoid(gate)
    silu = gate * sigmoid
    hidden_ref[...] = (silu * upward).astype(BF)
    dgate_ref[...] = (delta_hidden * upward * (sigmoid + silu * (1.0 - sigmoid))).astype(BF)
    dup_ref[...] = (delta_hidden * silu).astype(BF)


def mlp(c, mid, upstream, gain, shift, gate_w, up_w, down_w, previous):
    t, units = mid.shape[0], gate_w.shape[1]
    total = t * CHUNKS
    tile = 256
    one = lambda j: (0, 0)
    own = lambda j: (c, 0)
    column = pl.BlockSpec((t, tile), lambda j: (c, j))
    return kernel_call(
        mlp_body,
        (pl.cdiv(units, tile),),
        [mid, upstream, gain, shift, gate_w, up_w, down_w],
        [
            still((t, D), one),
            still((t, D), own),
            pl.BlockSpec((1, D), one),
            pl.BlockSpec((1, D), one),
            pl.BlockSpec((D, tile), lambda j: (0, j)),
            pl.BlockSpec((D, tile), lambda j: (0, j)),
            pl.BlockSpec((tile, D), lambda j: (j, 0)),
        ],
        [sds((total, D), BF), sds((total, 128), F32)] + [sds((total, units), BF)] * 3,
        [pl.BlockSpec((t, D), own), pl.BlockSpec((t, 128), own), column, column, column],
        previous,
        mib=46,
        name="mlp",
    )


def mlp_back_body(owners_ref, dgate_ref, dup_ref, gate_w_ref, up_w_ref, out_ref):
    out_ref[...] = (dot(dgate_ref[...], gate_w_ref[...], NT) + dot(dup_ref[...], up_w_ref[...], NT)).astype(BF)


def mlp_back(owners, width, dgate, dup, gate_w, up_w):
    t, units = dgate.shape
    whole = still((t, units), lambda j, owners: (0, 0))
    weight = pl.BlockSpec((width, units), lambda j, owners: (owners[j], 0))
    return prefetched(
        mlp_back_body,
        owners,
        (len(owners),),
        [dgate, dup, gate_w, up_w],
        [whole, whole, weight, weight],
        [sds((t, len(owners) * width), BF)],
        [pl.BlockSpec((t, width), lambda j, owners: (0, j))],
        mib=56,
        name="mlp_back",
    )[0]


def branch_back_body(e_ref, mid_ref, stats_ref, up_ref, weight_ref, means_ref, dbranch_ref, dctx_ref):
    rows = 64

    def step(i, carry):
        at = pl.ds(pl.multiple_of(i * rows, rows), rows)
        e = e_ref[at, :].astype(F32)
        mean, inverse = stats_ref[at, 0:1], stats_ref[at, 1:2]
        unit = (mid_ref[at, :].astype(F32) - mean) * inverse
        first = jnp.mean(e, axis=-1, keepdims=True)
        second = jnp.mean(e * unit, axis=-1, keepdims=True)
        dbranch_ref[at, :] = (up_ref[at, :].astype(F32) + inverse * (e - first - unit * second)).astype(BF)
        lane = lax.broadcasted_iota(jnp.int32, (rows, 128), 1)
        means_ref[at, :] = jnp.where(lane == 0, first, second)
        return carry

    lax.fori_loop(0, e_ref.shape[0] // rows, step, 0)
    dctx_ref[...] = dot(dbranch_ref[...], weight_ref[...], NT).astype(BF)


def branch_back(e, mid, stats, upstream, weight):
    t, width = e.shape[0], weight.shape[0]
    tile = SUB
    row = lambda i: (i, 0)
    return kernel_call(
        branch_back_body,
        (t // tile,),
        [e, mid, stats, upstream, weight],
        [
            pl.BlockSpec((tile, D), row),
            pl.BlockSpec((tile, D), row),
            pl.BlockSpec((tile, 128), row),
            pl.BlockSpec((tile, D), row),
            still((width, D), lambda i: (0, 0)),
        ],
        [sds((t, 128), F32), sds((t, D), BF), sds((t, width), BF)],
        [pl.BlockSpec((tile, 128), row), pl.BlockSpec((tile, D), row), pl.BlockSpec((tile, width), row)],
        mib=24,
        name="branch_back",
    )


def project_back_body(owners_ref, dq_ref, dk_ref, dv_ref, weight_ref, x_ref, stats_ref, below_ref, out_ref):
    n = dot(dq_ref[...], weight_ref[0], NT) + dot(dk_ref[...], weight_ref[1], NT) + dot(dv_ref[...], weight_ref[2], NT)
    out_ref[: n.shape[0], :] = n.astype(BF)
    unit = (x_ref[...].astype(F32) - stats_ref[:, 0:1]) * stats_ref[:, 1:2]
    with_unit = n * unit
    row = lax.broadcasted_iota(jnp.int32, (EXTRA, n.shape[1]), 0)
    gain_grad = jnp.sum(with_unit, axis=0, keepdims=True)
    shift_grad = jnp.sum(n, axis=0, keepdims=True)
    out_ref[n.shape[0] :, :] = jnp.where(row == 0, gain_grad, jnp.where(row == 1, shift_grad, below_ref[...])).astype(BF)


def project_back(owners, dq, dk, dv, weight, x, stats, below):
    t, width = dq.shape
    count = len(owners)
    whole = still((t, width), lambda j, owners: (0, 0))
    return prefetched(
        project_back_body,
        owners,
        (count,),
        [dq, dk, dv, weight, x, stats, below],
        [
            whole,
            whole,
            whole,
            pl.BlockSpec((3, width, width), lambda j, owners: (0, owners[j], 0)),
            pl.BlockSpec((t, width), lambda j, owners: (0, owners[j])),
            still((t, 128), lambda j, owners: (0, 0)),
            still((EXTRA, width), lambda j, owners: (0, 0)),
        ],
        [sds((t + EXTRA, count * width), BF)],
        [pl.BlockSpec((t + EXTRA, width), lambda j, owners: (0, j))],
        mib=34,
        name="project_back",
    )[0]


def add(a, b):
    return (a.astype(F32) + b.astype(F32)).astype(BF)


class Order:
    def __init__(self):
        self.before = ()

    def __call__(self, value):
        return after(value, *self.before) if self.before else value

    def done(self, *values):
        self.before = tuple(values)


class Gather:
    def __init__(self, share):
        self.n = lax.axis_size("tensor")
        self.pieces = [share]
        self.held = {(i, i): 0 for i in range(self.n)}
        self.steps = 0

    def send(self, piece, pairs, order):
        self.pieces.append(lax.ppermute(order(self.pieces[piece]), "tensor", pairs))

    def step(self, order):
        n, s = self.n, self.steps
        self.steps += 1
        before = len(self.pieces)
        if n == 4:
            outer, inner, out = [(0, 1), (1, 0), (2, 3), (3, 2)], [(1, 2), (2, 1)], [(1, 0), (2, 3)]
            for piece, pairs in (((0, outer), (0, inner)), ((2, out), (1, inner)), ((4, out),))[s]:
                self.send(piece, pairs, order)
            owners = ((1, None, 2, None, 3), (0, 2, None, 3, None), (3, 1, None, 0, None), (2, None, 1, None, 0))
            self.held = {(i, i): 0 for i in range(n)} | {
                (i, owner): 1 + k for i, row in enumerate(owners) for k, owner in enumerate(row) if owner is not None
            }
        else:
            up, down = (0, 0) if s == 0 else (before - 2, before - 1)
            self.held.update({(i + 1, i - s): before for i in range(s, n - 1)})
            self.held.update({(i, i + 1 + s): before + 1 for i in range(n - 1 - s)})
            self.send(up, [(i, i + 1) for i in range(s, n - 1)], order)
            self.send(down, [(i + 1, i) for i in range(n - 1 - s)], order)
        return self.pieces[before:]

    def last(self, order):
        got = self.step(order)
        while self.steps < self.n - 1:
            got = self.step(order)
        return got

    def whole(self):
        share = self.pieces[0]
        t, width = share.shape
        return prefetched(
            functools.partial(assemble_body, self.held),
            [lax.axis_index("tensor")],
            (self.n,),
            self.pieces,
            [still((t, width), lambda j, me: (0, 0))] * len(self.pieces),
            [sds((t, self.n * width), share.dtype)],
            [pl.BlockSpec((t, width), lambda j, me: (0, j))],
            mib=14,
            name="assemble",
        )[0]


def steps(order, *ops):
    return [got for op in ops if op.steps < op.n - 1 for got in op.step(order)]


def finish(order, *ops):
    got = steps(order, *ops)
    while any(op.steps < op.n - 1 for op in ops):
        got = steps(order, *ops)
    return got


def scatter_order(n):
    me = lax.axis_index("tensor")
    first = jnp.where(me < n // 2, n - 1, 0)
    return [(first + k) % n for k in range(n)]


class Scatter:
    def __init__(self, first, rest):
        self.n, self.me = lax.axis_size("tensor"), lax.axis_index("tensor")
        self.first, self.rest, self.steps, self.got = first, rest, 0, {}
        self.width = first.shape[1]

    def part(self, owner, *got):
        place = (owner - jnp.where(self.me < self.n // 2, self.n - 1, 0) - 1) % self.n
        place = jnp.clip(place, 0, self.n - 2)
        value = lax.dynamic_slice_in_dim(self.rest, place * self.width, self.width, 1)
        return functools.reduce(add, got, value)

    def any(self, owner, *got):
        first = jnp.where(self.me < self.n // 2, self.n - 1, 0)
        value = jnp.where(owner % self.n == first, self.first, self.part(owner % self.n))
        return functools.reduce(add, got, value)

    def send(self, name, value, pairs, order):
        self.got[name] = lax.ppermute(order(value), "tensor", pairs)

    def step(self, order):
        n, me, s = self.n, self.me, self.steps
        self.got = got = {name: order(value) for name, value in self.got.items()}
        self.steps += 1
        if n == 4:
            inward, inner, outer = [(0, 1), (3, 2)], [(1, 2), (2, 1)], [(0, 1), (1, 0), (2, 3), (3, 2)]
            if s == 0:
                self.send("far", self.first, inward, order)
                return [got["far"]]
            if s == 1:
                self.send("far", add(self.first, got["far"]), inner, order)
                self.send("next", self.part(jnp.where(me == 0, 2, 1)), inward, order)
            else:
                self.send("far", self.part(me ^ 1, got["far"]), outer, order)
                self.send("next", self.part(3 - me, got["next"]), inner, order)
            return [got["far"], got["next"]]
        up, down = ((got["up"],), (got["down"],)) if s else ((), ())
        self.send("up", self.any(me + n - 1 - s, *up), [(i, i + 1) for i in range(s + 1)], order)
        self.send("down", self.any(me - n + 1 + s, *down), [(i + 1, i) for i in range(n - 2 - s, n - 1)], order)
        return [got["up"], got["down"]]

    def last(self, order):
        got = self.step(order)
        while self.steps < self.n - 1:
            got = self.step(order)
        return got

    def total(self, order):
        self.got = {name: order(value) for name, value in self.got.items()}
        own = self.any(self.me) if self.n != 4 else self.part(self.me)
        return sum((g.astype(F32) for g in self.got.values()), own.astype(F32))


def assemble_body(held, me_ref, *refs):
    out_ref, owner, me = refs[-1], pl.program_id(0), me_ref[0]
    for k, ref in enumerate(refs[:-1]):
        places = [(device, o) for (device, o), at in held.items() if at == k]
        here = functools.reduce(jnp.logical_or, [(me == device) & (owner == o) for device, o in places])

        @pl.when(here)
        def _(ref=ref):
            out_ref[...] = ref[...]


def gradients_body(groups, join, which_ref, *refs):
    lefts, rest = refs[: len(groups)], refs[len(groups) :]
    rights, outs = rest[: sum(groups)], rest[sum(groups) :]
    k = 0
    for left, count in zip(lefts, groups):
        turned = left[...].T
        for right in rights[k : k + count]:
            wide = right.shape[1]
            at = k % join * wide
            outs[k // join][:, at : at + wide] = dot(turned, right[...]).astype(BF)
            k += 1


def gradients(which, pairs, name, join=1):
    t = pairs[0][0].shape[0]
    block = 256
    nb = D // 2 // block
    lefts, rights = [left for left, _ in pairs], [right for _, some in pairs for right in some]
    wide = join * rights[0].shape[1]
    return prefetched(
        functools.partial(gradients_body, [len(some) for _, some in pairs], join),
        [which],
        (nb,),
        lefts + rights,
        [pl.BlockSpec((t, block), lambda i, which: (0, which[0] * nb + i))] * len(lefts)
        + [still(right.shape, lambda i, which: (0, 0)) for right in rights],
        [sds((D // 2, wide), BF)] * (len(rights) // join),
        [pl.BlockSpec((block, wide), lambda i, which: (i, 0))] * (len(rights) // join),
        mib=30 if join > 1 else 56,
        name=name,
    )


def mlp_out_body(owners_ref, hidden_ref, weight_ref, first_ref, rest_ref):
    out = dot(hidden_ref[...], weight_ref[...]).astype(BF)

    @pl.when(pl.program_id(0) == 0)
    def _():
        first_ref[...] = out

    @pl.when(pl.program_id(0) > 0)
    def _():
        rest_ref[...] = out


def mlp_out(owners, width, hidden, weight):
    t, units = hidden.shape
    return prefetched(
        mlp_out_body,
        owners,
        (len(owners),),
        [hidden, weight],
        [
            still((t, units), lambda j, owners: (0, 0)),
            pl.BlockSpec((units, width), lambda j, owners: (0, owners[j])),
        ],
        [sds((t, width), BF), sds((t, D - width), BF)],
        [
            pl.BlockSpec((t, width), lambda j, owners: (0, 0)),
            pl.BlockSpec((t, width), lambda j, owners: (0, jnp.maximum(j - 1, 0))),
        ],
        mib=22,
        name="mlp_out",
    )


def swap(value, bit, axis="dp"):
    n = lax.axis_size(axis)
    return lax.ppermute(value, axis, [(i, i ^ (1 << bit)) for i in range(n)])


def split_body(groups, bits_ref, *refs):
    parts, outs = refs[: 4 * groups], refs[4 * groups :]
    for part in range(2):
        for phase in range(2):

            @pl.when(pl.program_id(0) == phase)
            def _(part=part, phase=phase):
                at = 0
                for g in range(groups):
                    keep, got = parts[2 * (part * groups + g)], parts[2 * (part * groups + g) + 1]
                    wide = keep.shape[1]
                    outs[2 * part + phase][:, at : at + wide] = add(keep[...], got[...])
                    at += wide


def split(upper, lower, bits, joined):
    groups = len(upper)
    rows = upper[0][0].shape[0] // (4 if joined else 2)
    block = min(128, rows)
    nb = rows // block
    columns = sum(keep.shape[1] for keep, _ in upper)
    ins, in_specs = [], []
    for part, pairs in enumerate((upper, lower)):
        first = 2 * nb * part if joined else 0

        def index(phase, j, bits, part=part, first=first):
            half = jnp.where(phase == 0, 1 - bits[part], bits[part])
            return (first + half * nb + j, 0)

        for pair in pairs:
            for array in pair:
                ins.append(array)
                in_specs.append(pl.BlockSpec((block, array.shape[1]), index))
    given = pl.BlockSpec((block, columns), lambda phase, j, bits: (jnp.where(phase == 0, j, nb - 1), 0))
    kept = pl.BlockSpec((block, columns), lambda phase, j, bits: (jnp.where(phase == 0, 0, j), 0))
    return prefetched(
        functools.partial(split_body, groups),
        bits,
        (2, nb),
        ins,
        in_specs,
        [sds((rows, columns), BF)] * 4,
        [given, kept] * 2,
        mib=56 if groups > 2 else 28,
        name="split",
    )


def merge_body(widths, bits_ref, *refs):
    for part in range(2):
        for which in range(2):

            @pl.when((pl.program_id(0) == bits_ref[part]) == (which == 0))
            def _(part=part, which=which):
                value = refs[2 * part + which][...]
                if widths:
                    at = 0
                    for out, wide in zip(refs[4:], widths):
                        out[part] = value[:, at : at + wide]
                        at += wide
                else:
                    refs[4 + part][...] = value


def merge(upper, lower, bits, widths=()):
    rows, columns = upper[0].shape
    block = min(128, rows)
    nb = rows // block

    def spec(part, which):
        def index(i, j, bits):
            half = bits[part] if which == 0 else 1 - bits[part]
            return (jnp.where(i == half, j, jnp.where(i < half, 0, nb - 1)), 0)

        return pl.BlockSpec((block, columns), index)

    if widths:
        outs = [sds((2, 2 * rows, wide), BF) for wide in widths]
        out_specs = [pl.BlockSpec((2, block, wide), lambda i, j, bits: (0, i * nb + j, 0)) for wide in widths]
    else:
        outs = [sds((2 * rows, columns), BF)] * 2
        out_specs = [pl.BlockSpec((block, columns), lambda i, j, bits: (i * nb + j, 0))] * 2
    return prefetched(
        functools.partial(merge_body, widths),
        bits,
        (2, nb),
        [*upper, *lower],
        [spec(part, which) for part in range(2) for which in range(2)],
        outs,
        out_specs,
        mib=56,
        name="merge",
    )


def sum_over_dp(given, order):
    me, n = lax.axis_index("dp"), lax.axis_size("dp")
    count = n.bit_length() - 1
    bit = lambda b: (me >> b) & 1
    orders = [list(range(1, count)), list(range(count - 1, 0, -1))]
    got = [swap(g, 0) for g in given]
    kept = yield got
    upper = lower = [(order(k), g) for k, g in zip(kept, got)]
    for s in range(count - 1):
        a, b = orders[0][s], orders[1][s]
        p_give, p_keep, q_give, q_keep = split(upper, lower, [bit(a), bit(b)], s == 0)
        upper, lower = [(p_keep, swap(p_give, a))], [(q_keep, swap(q_give, b))]
        yield p_keep
        upper, lower = [(order(upper[0][0]), upper[0][1])], [(order(lower[0][0]), lower[0][1])]
    p, q = add(*upper[0]), add(*lower[0])
    for s in reversed(range(count - 1)):
        a, b = orders[0][s], orders[1][s]
        p, q = lax.optimization_barrier((p, q))
        got = swap(p, a), swap(q, b)
        yield p
        out = merge([order(p), got[0]], [q, got[1]], [bit(a), bit(b)], () if s else [g.shape[1] for g in given])
        if s:
            p, q = out
    own = [array.reshape(-1, array.shape[2]) for array in out]
    other = [swap(array, 0) for array in own]
    yield own[0]
    yield own, other


def finish_sum(steps_left):
    *_, last = steps_left
    return last


def halves(core, own, other, nb):
    def index(mine):
        def of(i, bits):
            half = bits[0] if mine else 1 - bits[0]
            return (jnp.clip(i - half * nb, 0, nb - 1), 0)

        return of

    return index(True), index(False)


def halves_body(store, core_ref, *refs):
    half = pl.program_id(0) // (pl.num_programs(0) // 2)
    groups = store.groups
    own, other, outs = refs[:groups], refs[groups : 2 * groups], refs[2 * groups :]
    for arrays, mine in ((own, True), (other, False)):

        @pl.when((half == core_ref[0]) == mine)
        def _(arrays=arrays):
            store(arrays, outs)


def from_halves(store, core, own, other, outs, out_specs, block, mib, name):
    store.groups = len(own)
    nb = own[0].shape[0] // block
    return prefetched(
        functools.partial(halves_body, store),
        [core],
        (2 * nb,),
        [*own, *other],
        [
            pl.BlockSpec((block, array.shape[1]), index)
            for arrays, index in zip((own, other), halves(core, own, other, nb))
            for array in arrays
        ],
        outs,
        out_specs,
        mib=mib,
        name=name,
    )


def gate_up_out(core, own, other):
    def store(arrays, outs):
        for k in range(2):
            outs[0][:, k, :] = arrays[k][...].astype(F32)

    units, block = own[0].shape[1], 128
    outs, spec = [sds((D, 2, units), F32)], [pl.BlockSpec((block, 2, units), lambda i, c: (i, 0, 0))]
    return from_halves(store, core, own, other, outs, spec, block, 56, "gate_up_out")[0]


def down_out(core, own, other):
    def store(arrays, outs):
        outs[0][...] = arrays[0][...].astype(F32).T

    units, block = own[0].shape[1], 128
    outs, spec = [sds((units, D), F32)], [pl.BlockSpec((units, block), lambda i, c: (0, i))]
    return from_halves(store, core, own, other, outs, spec, block, 56, "down_out")[0]


def attention_out(core, own, other):
    def store(arrays, outs):
        for k in range(3):
            outs[0][k] = arrays[0][:, k * width : (k + 1) * width].astype(F32)
        outs[1][...] = arrays[0][:, 3 * width :].astype(F32).T

    width, block = own[0].shape[1] // 4, 256
    outs = [sds((3, D, width), F32), sds((width, D), F32)]
    specs = [
        pl.BlockSpec((3, block, width), lambda i, c: (0, i, 0)),
        pl.BlockSpec((width, block), lambda i, c: (0, i)),
    ]
    return from_halves(store, core, own, other, outs, specs, block, 22, "attention_out")


def per_device(
    tokens,
    norm_one_gain,
    norm_one_shift,
    project_weight,
    project_bias,
    output_weight,
    norm_two_gain,
    norm_two_shift,
    gate_up_weight,
    down_weight,
    cotangent,
):
    width = tokens.shape[1]
    t = tokens.shape[0] // CHUNKS
    offset = lax.axis_index("tensor") * width
    core = lax.axis_index("dp") & 1
    mine = lambda full: lax.dynamic_slice_in_dim(full, offset, width, full.ndim - 1)
    half_of = lambda array, which: lax.dynamic_slice_in_dim(array, which * (D // 2), D // 2, 1)
    order = Order()

    small = jnp.stack([norm_one_gain, norm_one_shift, norm_two_gain, norm_two_shift])
    whole_x = Gather(jnp.concatenate([tokens, jnp.pad(small, ((0, EXTRA - 4), (0, 0)))]))
    whole_up = Gather(cotangent)
    got = whole_x.step(order)
    gate_w = order(gate_up_weight)[:, 0]
    order.done(*got, gate_w)
    got = whole_x.step(order)
    up_w = order(gate_up_weight)[:, 1]
    tables = rope_tables()
    order.done(*got, up_w, tables)
    whole_x.last(order)
    x = whole_x.whole()
    gain_one, gain_two, shift_two = (x[t + i : t + i + 1].astype(F32) for i in (0, 2, 3))
    project_w = project_weight.transpose(1, 0, 2)
    bias = project_bias.astype(F32)[:, None, :]

    through = lambda row: jnp.einsum("d,kdc->kc", row[0].astype(BF), project_w, preferred_element_type=F32)
    with_rows = jnp.stack([through(gain_one), through(x[t + 1 : t + 2]) + bias[:, 0]])

    order.done(x)
    got = whole_up.step(order)
    normed_one, stats_one, heads = project(0, x, project_w, bias, tables, ())
    order.done(*got, stats_one)
    owners = scatter_order(whole_up.n)
    first, rest, context, lse = attend(owners, order(heads), output_weight)
    order.done(lse)
    branch = Scatter(first, rest)
    for _ in range(2):
        order.done(*whole_up.step(order), *branch.step(order), with_rows)
    if whole_up.n > 4:
        whole_up.last(order)
    branch.last(order)
    upstream = whole_up.whole()
    middle_share = tokens.astype(F32) + branch.total(order)
    middle_sent = (middle_share - stats_one[:, 0:1]).astype(BF)
    order.done(middle_sent)
    whole_middle = Gather(middle_sent)
    while whole_middle.steps < whole_middle.n - 1:
        whole_middle.step(order)
    middle = whole_middle.whole()

    normed_two, stats_two, hidden, dgate, dup = mlp(
        0, middle, upstream, gain_two, shift_two, gate_w, up_w, down_weight, ()
    )
    first = mlp_back(owners[:1], width, dgate, dup, gate_w, up_w)
    rest = mlp_back(owners[1:], width, after(dgate, first), dup, gate_w, up_w)
    order.done(first)
    delta_two = Scatter(first, rest)
    got = steps(order, delta_two)
    order.done(rest, *got)
    got = steps(order, delta_two)
    mlp_grads = lambda which, name: gradients(
        which, [(normed_two, [order(dgate), dup]), (upstream, [hidden])], name
    )
    mlp_given = mlp_grads(1 - core, "mlp_given")
    mlp_sum = sum_over_dp(mlp_given, order)
    next(mlp_sum)
    order.done(*got, *mlp_given)
    got = finish(order, delta_two)
    mlp_kept = mlp_grads(core, "mlp_kept")
    order.done(*got, *mlp_kept)
    delta_two = delta_two.total(order)
    unit_two = (mine(middle).astype(F32) - stats_two[:, 0:1]) * stats_two[:, 1:2]
    two_grads = [jnp.sum(delta_two * unit_two, axis=0), jnp.sum(delta_two, axis=0)]
    e_own = delta_two * norm_two_gain.astype(F32)
    e_sent = e_own.astype(BF)
    order.done(e_sent)
    whole_e = Gather(e_sent)
    got = steps(order, whole_e)
    held = mlp_sum.send(mlp_kept)
    order.done(*got, held)
    got = steps(order, whole_e)
    mlp_share = Scatter(*mlp_out(owners, width, order(hidden), down_weight))
    order.done(*got, mlp_share.rest)
    got = finish(order, whole_e) + steps(order, mlp_share)
    held = next(mlp_sum)
    e = whole_e.whole()

    order.done(e, held, *got)
    share_got = steps(order, mlp_share)
    means_two, dbranch, dctx = branch_back(order(e), middle, stats_two, upstream, output_weight)
    order.done(dctx)
    held = next(mlp_sum)
    order.done(held)
    dq, dk, dv, sums = attend_back(heads, lse, context, order(dctx), tables, with_rows)
    held = next(mlp_sum)
    order.done(dq, held, *share_got)
    delta_heads = (dq, dk, dv)
    sum_rows = 2 * t // width
    below = jnp.pad(sums[:2].reshape(sum_rows, width), ((2, EXTRA - 2 - sum_rows), (0, 0)))
    back = lambda owners, dq: project_back(owners, dq, dk, dv, project_w, x, stats_one, below)
    first = back(owners[:1], order(dq))
    rest = back(owners[1:], after(dq, first))
    order.done(first)
    delta_one = Scatter(first, rest)
    got = steps(order, delta_one)
    order.done(rest)
    attention_grads = lambda which, name: gradients(
        which, [(normed_one, [order(dq), dk, dv]), (dbranch, [context])], name, join=4
    )
    attention_given = attention_grads(1 - core, "attention_given")
    attention_sum = sum_over_dp(attention_given, order)
    next(attention_sum)
    order.done(*attention_given, *got)
    got = steps(order, delta_one)
    attention_kept = attention_grads(core, "attention_kept")
    order.done(*attention_kept)
    held = attention_sum.send(attention_kept)
    order.done(held)
    held = next(mlp_sum)
    order.done(held, *got)
    got = finish(order, delta_one)
    held = next(attention_sum)
    order.done(held)
    held = next(attention_sum)
    order.done(held, *got)
    if lax.axis_size("dp") > 8:
        for _ in range(2):
            order.done(next(mlp_sum))
            order.done(next(attention_sum))
    held = next(attention_sum)
    order.done(held)
    share_got = finish(order, mlp_share)
    mlp_halves = next(mlp_sum)
    gate_up_grad = gate_up_out(core, [order(mlp_halves[0][0]), mlp_halves[0][1]], mlp_halves[1][:2])
    order.done(gate_up_grad)
    delta_one = delta_one.total(order)
    bias_grad = [jnp.sum(a, axis=0, dtype=F32) for a in delta_heads]
    small = jnp.stack([delta_one[t], delta_one[t + 1], *two_grads, *bias_grad])
    small = small + swap(small, 0)
    sums = (delta_one[t + 2 : t + 2 + sum_rows] / D).reshape(2, t).T
    unit_one = (tokens.astype(F32) - stats_one[:, 0:1]) * stats_one[:, 1:2]
    dmid = cotangent.astype(F32) + stats_two[:, 1:2] * (e_own - means_two[:, 0:1] - unit_two * means_two[:, 1:2])
    tokens_grad = order(dmid) + stats_one[:, 1:2] * (
        delta_one[:t] * norm_one_gain.astype(F32) - sums[:, 0:1] - unit_one * sums[:, 1:2]
    )
    order.done(small, tokens_grad, *share_got)
    held = next(attention_sum)
    order.done(held)
    devices = lax.axis_size("dp")
    others = [lax.ppermute(order(small), "dp", [(i, i ^ k) for i in range(devices)]) for k in range(2, devices, 2)]
    down_grad = down_out(core, [order(mlp_halves[0][2])], mlp_halves[1][2:])
    order.done(down_grad)
    result = (middle_share + mlp_share.total(order)).astype(BF)
    small = sum((order(other) for other in others), small)
    order.done(tokens_grad, small, result)
    attention_halves = next(attention_sum)
    project_grad, output_grad = attention_out(
        core, [order(attention_halves[0][0]), *attention_halves[0][1:]], attention_halves[1]
    )
    return (
        result,
        tokens_grad,
        small[0],
        small[1],
        project_grad.transpose(1, 0, 2),
        small[4:7],
        output_grad,
        small[2],
        small[3],
        gate_up_grad,
        down_grad,
    )


def solution(mesh):
    return jax.shard_map(
        per_device,
        mesh=mesh,
        in_specs=(
            P("dp", "tensor"),
            P("tensor"),
            P("tensor"),
            P(None, None, "tensor"),
            P(None, "tensor"),
            P("tensor", None),
            P("tensor"),
            P("tensor"),
            P(None, None, "tensor"),
            P("tensor", None),
            P("dp", "tensor"),
        ),
        out_specs=(
            P("dp", "tensor"),
            P("dp", "tensor"),
            P("tensor"),
            P("tensor"),
            P(None, None, "tensor"),
            P(None, "tensor"),
            P("tensor", None),
            P("tensor"),
            P("tensor"),
            P(None, None, "tensor"),
            P("tensor", None),
        ),
        check_vma=False,
    )
```

```python
import functools

import jax
import jax.numpy as jnp
from jax import lax
from jax.experimental import pallas as pl
from jax.experimental.pallas import tpu as pltpu
from jax.sharding import PartitionSpec as P

D = 2048
HEAD_DIM = 64
ROT = 16
SEQ = 1024
PAIR = 2 * HEAD_DIM
CHUNKS = 1
SUB = 256
WEIGHTS = {"mlp_kept": 30, "mlp_out": 10, "attend_back": 20, "merge": 15, "attention_kept": 40}
EXTRA = 16

EPSILON = 1e-05
ROPE_BASE = 10000.0
BF = jnp.bfloat16
F32 = jnp.float32
NT = (((1,), (1,)), ((), ()))
TN = (((0,), (0,)), ((), ()))
ANY = pl.BlockSpec(memory_space=pl.ANY)


def dot(a, b, dims=(((1,), (0,)), ((), ()))):
    return lax.dot_general(a, b, dims, preferred_element_type=F32)


def params(mib):
    return pltpu.CompilerParams(vmem_limit_bytes=mib << 20)


def cost(name):
    return pl.CostEstimate(flops=int(WEIGHTS.get(name, 0) * 1e9), bytes_accessed=0, transcendentals=0)


def after(value, *others):
    return lax.optimization_barrier((value, *others))[0]


def kernel_call(body, grid, ins, in_specs, outs, out_specs, previous=(), scratch=(), mib=56, name=None):
    given = len(ins)
    previous = dict(previous)
    aliases = {given + i: out for i, out in enumerate(previous)}

    def run(*refs):
        body(*refs[:given], *refs[given + len(previous) :])

    return pl.pallas_call(
        run,
        grid=grid,
        in_specs=list(in_specs) + [ANY] * len(previous),
        out_specs=list(out_specs),
        out_shape=list(outs),
        input_output_aliases=aliases,
        scratch_shapes=list(scratch),
        compiler_params=params(mib),
        cost_estimate=cost(name),
        name=name,
    )(*ins, *previous.values())


def still(block, index):
    return pl.BlockSpec(block, index, pipeline_mode=pl.Buffered(1))


def sds(shape, dtype):
    return jax.ShapeDtypeStruct(shape, dtype)


def prefetched(body, scalars, grid, ins, in_specs, outs, out_specs, mib=56, name=None):
    return pl.pallas_call(
        body,
        grid_spec=pltpu.PrefetchScalarGridSpec(
            num_scalar_prefetch=1, grid=grid, in_specs=in_specs, out_specs=out_specs
        ),
        out_shape=outs,
        compiler_params=params(mib),
        cost_estimate=cost(name),
        name=name,
    )(jnp.stack(scalars).astype(jnp.int32), *ins)


def norm_rows(x_ref, gain, shift, normed_ref, stats_ref, rows=64):
    def step(i, carry):
        at = pl.ds(pl.multiple_of(i * rows, rows), rows)
        x = x_ref[at, :].astype(F32)
        mean = jnp.mean(x, axis=-1, keepdims=True)
        centered = x - mean
        inverse = lax.rsqrt(jnp.mean(centered * centered, axis=-1, keepdims=True) + EPSILON)
        normed_ref[at, :] = (centered * inverse * gain + shift).astype(BF)
        lane = lax.broadcasted_iota(jnp.int32, (rows, 128), 1)
        stats_ref[at, :] = jnp.where(lane == 0, mean, inverse)
        return carry

    lax.fori_loop(0, x_ref.shape[0] // rows, step, 0)


def rope_tables():
    lane = jnp.arange(PAIR, dtype=jnp.int32)[None, :] % HEAD_DIM
    half = ROT // 2
    index = (lane % half).astype(F32)
    angles = jnp.arange(SEQ, dtype=F32)[:, None] * ROPE_BASE ** (-(index * (2.0 / ROT)))
    turned = lane < ROT
    cosine = jnp.where(turned, jnp.cos(angles), 1.0)
    low = jnp.where(turned & (lane >= half), jnp.sin(angles), 0.0)
    high = jnp.where(lane < half, -jnp.sin(angles), 0.0)
    return jnp.stack([cosine, low, high])


def turn(values, table):
    half = ROT // 2
    return (
        values * table[0]
        + pltpu.roll(values, half, 1) * table[1]
        + pltpu.roll(values, values.shape[1] - half, 1) * table[2]
    )


def turn_back(values, table):
    half = ROT // 2
    return (
        values * table[0]
        - pltpu.roll(values, half, 1) * table[1]
        - pltpu.roll(values, values.shape[1] - half, 1) * table[2]
    )


def project_body(x_ref, small_ref, weight_ref, bias_ref, table_ref, normed_ref, stats_ref, heads_ref):
    part = pl.program_id(0)

    @pl.when(part == 0)
    def _():
        gain, shift = (small_ref[k : k + 1, :].astype(F32) for k in (0, 1))
        norm_rows(x_ref, gain, shift, normed_ref, stats_ref)

    out = dot(normed_ref[...], weight_ref[0]) + bias_ref[0]
    width = out.shape[1]

    @pl.when(part < 2)
    def _():
        table = table_ref[...]
        for p in range(width // PAIR):
            heads_ref[0, :, p * PAIR : (p + 1) * PAIR] = turn(out[:, p * PAIR : (p + 1) * PAIR], table).astype(BF)

    @pl.when(part == 2)
    def _():
        heads_ref[0] = out.astype(BF)


def project(c, x, weight, bias, tables, previous):
    t, width = x.shape[0] - EXTRA, weight.shape[2]
    total = t * CHUNKS
    one = lambda k: (0, 0)
    return kernel_call(
        project_body,
        (3,),
        [x, x, weight, bias, tables],
        [
            still((t, D), one),
            pl.BlockSpec((EXTRA, D), lambda k: (t // EXTRA, 0)),
            pl.BlockSpec((1, D, width), lambda k: (k, 0, 0)),
            pl.BlockSpec((1, 1, width), lambda k: (k, 0, 0)),
            still((3, t, PAIR), lambda k: (0, c, 0)),
        ],
        [sds((total, D), BF), sds((total, 128), F32), sds((3, total, width), BF)],
        [
            pl.BlockSpec((t, D), lambda k: (c, 0)),
            pl.BlockSpec((t, 128), lambda k: (c, 0)),
            pl.BlockSpec((1, t, width), lambda k: (k, c, 0)),
        ],
        previous,
        mib=34,
        name="project",
    )


def lane_of(rows):
    return lax.broadcasted_iota(jnp.int32, (rows, PAIR), 1) < HEAD_DIM


def attend_body(c, owners_ref, q_ref, k_ref, v_ref, out_weight_ref, first_ref, rest_ref, ctx_ref, lse_ref):
    pair = pl.program_id(0)
    t = q_ref.shape[1]
    scale = HEAD_DIM ** (-0.5)
    low = lane_of(SUB)
    for r in range(t // SUB):
        start = c * t + r * SUB
        extent = start + SUB
        q = q_ref[0, r * SUB : (r + 1) * SUB, :].astype(F32) * scale
        keys = k_ref[0, :extent, :]
        values = v_ref[0, :extent, :]
        row = start + lax.broadcasted_iota(jnp.int32, (SUB, extent), 0)
        seen = lax.broadcasted_iota(jnp.int32, (SUB, extent), 1) <= row
        contexts, sums = [], []
        for h in range(2):
            own = jnp.where(low if h == 0 else ~low, q, 0.0).astype(BF)
            scores = jnp.where(seen, dot(own, keys, NT), -1000000000.0)
            top = jnp.max(scores, axis=-1, keepdims=True)
            raised = jnp.exp(scores - top)
            total = jnp.sum(raised, axis=-1, keepdims=True)
            contexts.append(dot(raised.astype(BF), values) / total)
            sums.append(top + jnp.log(total))
        at = pl.ds(pl.multiple_of(pair * PAIR, PAIR), PAIR)
        ctx_ref[r * SUB : (r + 1) * SUB, at] = jnp.where(low, contexts[0], contexts[1]).astype(BF)
        lse_ref[r * SUB : (r + 1) * SUB, :] = jnp.where(low, sums[0], sums[1])

    @pl.when(pair == pl.num_programs(0) - 1)
    def _():
        wide = first_ref.shape[1]
        for j in range(D // wide):
            at = pl.ds(pl.multiple_of(owners_ref[j] * wide, wide), wide)
            out = dot(ctx_ref[...], out_weight_ref[:, at]).astype(BF)
            if j == 0:
                first_ref[...] = out
            else:
                rest_ref[:, (j - 1) * wide : j * wide] = out


def attend(owners, heads, out_weight):
    t, width = heads.shape[1], heads.shape[2]
    here = lambda p, owners: (0, p)
    fixed = lambda p, owners: (0, 0)
    return prefetched(
        functools.partial(attend_body, 0),
        owners,
        (width // PAIR,),
        [heads, heads, heads, out_weight],
        [pl.BlockSpec((1, t, PAIR), lambda p, owners, k=k: (k, 0, p)) for k in range(3)]
        + [still((width, D), fixed)],
        [sds((t, width), BF), sds((t, D - width), BF), sds((t, width), BF), sds((t, width), F32)],
        [
            pl.BlockSpec((t, width), fixed),
            pl.BlockSpec((t, D - width), fixed),
            pl.BlockSpec((t, width), fixed),
            pl.BlockSpec((t, PAIR), here),
        ],
        mib=30,
        name="attend",
    )


def attend_back_body(c, *refs):
    q_ref, k_ref, v_ref, lse_ref, ctx_ref, dctx_ref, table_ref, with_ref, dq_ref, dk_ref, dv_ref, sums_ref, dk_sum, dv_sum = refs
    t = q_ref.shape[1]

    @pl.when(pl.program_id(0) == 0)
    def _():
        sums_ref[...] = jnp.zeros_like(sums_ref)

    def row_sums(k, gradient, values, at):
        first = gradient * with_ref[0, k : k + 1, :]
        second = gradient * (values - with_ref[1, k : k + 1, :])
        sums_ref[0:1, at] += jnp.sum(first.T, axis=0, keepdims=True)
        sums_ref[1:2, at] += jnp.sum(second.T, axis=0, keepdims=True)

    scale = HEAD_DIM ** (-0.5)
    low = lane_of(SUB)
    dk_sum[...] = jnp.zeros_like(dk_sum)
    dv_sum[...] = jnp.zeros_like(dv_sum)
    for r in range(t // SUB):
        here = slice(r * SUB, (r + 1) * SUB)
        start = c * t + r * SUB
        extent = start + SUB
        q = q_ref[0, here, :].astype(F32) * scale
        keys = k_ref[0, :extent, :]
        values = v_ref[0, :extent, :]
        dctx = dctx_ref[here, :]
        lse_t = lse_ref[here, :].T
        product_t = (ctx_ref[here, :].astype(F32) * dctx.astype(F32)).T
        low_keys = lane_of(extent)
        column = start + lax.broadcasted_iota(jnp.int32, (extent, SUB), 1)
        seen = lax.broadcasted_iota(jnp.int32, (extent, SUB), 0) <= column
        dq = jnp.zeros((SUB, PAIR), F32)
        for h in range(2):
            own = low if h == 0 else ~low
            q_own = jnp.where(own, q, 0.0).astype(BF)
            dctx_own = jnp.where(own, dctx, jnp.zeros_like(dctx))
            rows = slice(h * HEAD_DIM, (h + 1) * HEAD_DIM)
            row_dot = jnp.sum(product_t[rows, :], axis=0, keepdims=True)
            scores = dot(keys, q_own, NT) - lse_t[h * HEAD_DIM : h * HEAD_DIM + 1, :]
            probs = jnp.where(seen, jnp.exp(scores), 0.0)
            delta_probs = dot(values, dctx_own, NT)
            delta_scores = (probs * (delta_probs - row_dot)).astype(BF)
            dv_sum[:extent, :] += dot(probs.astype(BF), dctx_own)
            dk_sum[:extent, :] += dot(delta_scores, q_own)
            keys_own = jnp.where(low_keys if h == 0 else ~low_keys, keys, jnp.zeros_like(keys))
            dq = dq + dot(delta_scores, keys_own, TN)
        table = table_ref[:, start:extent, :]
        dq = turn_back(dq * scale, table)
        dq_ref[here, :] = dq.astype(BF)
        row_sums(0, dq, turn_back(q_ref[0, here, :].astype(F32), table), here)
    for r in range(t // SUB):
        here = slice(r * SUB, (r + 1) * SUB)
        table = table_ref[:, here, :]
        dk = turn_back(dk_sum[here, :], table)
        dk_ref[here, :] = dk.astype(BF)
        row_sums(1, dk, turn_back(k_ref[0, here, :].astype(F32), table), here)
        dv = dv_sum[here, :]
        dv_ref[here, :] = dv.astype(BF)
        row_sums(2, dv, v_ref[0, here, :].astype(F32), here)


def attend_back(heads, lse, ctx, dctx, tables, with_rows):
    t, width = heads.shape[1], heads.shape[2]
    own = pl.BlockSpec((t, PAIR), lambda p: (0, p))
    return kernel_call(
        functools.partial(attend_back_body, 0),
        (width // PAIR,),
        [heads, heads, heads, lse, ctx, dctx, tables, with_rows],
        [pl.BlockSpec((1, t, PAIR), lambda p, k=k: (k, 0, p)) for k in range(3)]
        + [own, own, own, still((3, t, PAIR), lambda p: (0, 0, 0)), pl.BlockSpec((2, 3, PAIR), lambda p: (0, 0, p))],
        [sds((t, width), BF)] * 3 + [sds((8, t), F32)],
        [own, own, own, pl.BlockSpec((8, t), lambda p: (0, 0))],
        scratch=[pltpu.VMEM((t, PAIR), F32)] * 2,
        mib=28,
        name="attend_back",
    )


def mlp_body(mid_ref, up_ref, gain_ref, shift_ref, gate_w_ref, up_w_ref, down_w_ref, normed_ref, stats_ref, hidden_ref, dgate_ref, dup_ref):
    @pl.when(pl.program_id(0) == 0)
    def _():
        norm_rows(mid_ref, gain_ref[...], shift_ref[...], normed_ref, stats_ref)

    normed = normed_ref[...]
    gate = dot(normed, gate_w_ref[...])
    upward = dot(normed, up_w_ref[...])
    delta_hidden = dot(up_ref[...], down_w_ref[...], NT)
    sigmoid = jax.nn.sigmoid(gate)
    silu = gate * sigmoid
    hidden_ref[...] = (silu * upward).astype(BF)
    dgate_ref[...] = (delta_hidden * upward * (sigmoid + silu * (1.0 - sigmoid))).astype(BF)
    dup_ref[...] = (delta_hidden * silu).astype(BF)


def mlp(c, mid, upstream, gain, shift, gate_w, up_w, down_w, previous):
    t, units = mid.shape[0], gate_w.shape[1]
    total = t * CHUNKS
    tile = 256
    one = lambda j: (0, 0)
    own = lambda j: (c, 0)
    column = pl.BlockSpec((t, tile), lambda j: (c, j))
    return kernel_call(
        mlp_body,
        (pl.cdiv(units, tile),),
        [mid, upstream, gain, shift, gate_w, up_w, down_w],
        [
            still((t, D), one),
            still((t, D), own),
            pl.BlockSpec((1, D), one),
            pl.BlockSpec((1, D), one),
            pl.BlockSpec((D, tile), lambda j: (0, j)),
            pl.BlockSpec((D, tile), lambda j: (0, j)),
            pl.BlockSpec((tile, D), lambda j: (j, 0)),
        ],
        [sds((total, D), BF), sds((total, 128), F32)] + [sds((total, units), BF)] * 3,
        [pl.BlockSpec((t, D), own), pl.BlockSpec((t, 128), own), column, column, column],
        previous,
        mib=46,
        name="mlp",
    )


def mlp_back_body(owners_ref, dgate_ref, dup_ref, gate_w_ref, up_w_ref, out_ref):
    out_ref[...] = (dot(dgate_ref[...], gate_w_ref[...], NT) + dot(dup_ref[...], up_w_ref[...], NT)).astype(BF)


def mlp_back(owners, width, dgate, dup, gate_w, up_w):
    t, units = dgate.shape
    whole = still((t, units), lambda j, owners: (0, 0))
    weight = pl.BlockSpec((width, units), lambda j, owners: (owners[j], 0))
    return prefetched(
        mlp_back_body,
        owners,
        (len(owners),),
        [dgate, dup, gate_w, up_w],
        [whole, whole, weight, weight],
        [sds((t, len(owners) * width), BF)],
        [pl.BlockSpec((t, width), lambda j, owners: (0, j))],
        mib=56,
        name="mlp_back",
    )[0]


def branch_back_body(e_ref, mid_ref, stats_ref, up_ref, weight_ref, means_ref, dbranch_ref, dctx_ref):
    rows = 64

    def step(i, carry):
        at = pl.ds(pl.multiple_of(i * rows, rows), rows)
        e = e_ref[at, :].astype(F32)
        mean, inverse = stats_ref[at, 0:1], stats_ref[at, 1:2]
        unit = (mid_ref[at, :].astype(F32) - mean) * inverse
        first = jnp.mean(e, axis=-1, keepdims=True)
        second = jnp.mean(e * unit, axis=-1, keepdims=True)
        dbranch_ref[at, :] = (up_ref[at, :].astype(F32) + inverse * (e - first - unit * second)).astype(BF)
        lane = lax.broadcasted_iota(jnp.int32, (rows, 128), 1)
        means_ref[at, :] = jnp.where(lane == 0, first, second)
        return carry

    lax.fori_loop(0, e_ref.shape[0] // rows, step, 0)
    dctx_ref[...] = dot(dbranch_ref[...], weight_ref[...], NT).astype(BF)


def branch_back(e, mid, stats, upstream, weight):
    t, width = e.shape[0], weight.shape[0]
    tile = SUB
    row = lambda i: (i, 0)
    return kernel_call(
        branch_back_body,
        (t // tile,),
        [e, mid, stats, upstream, weight],
        [
            pl.BlockSpec((tile, D), row),
            pl.BlockSpec((tile, D), row),
            pl.BlockSpec((tile, 128), row),
            pl.BlockSpec((tile, D), row),
            still((width, D), lambda i: (0, 0)),
        ],
        [sds((t, 128), F32), sds((t, D), BF), sds((t, width), BF)],
        [pl.BlockSpec((tile, 128), row), pl.BlockSpec((tile, D), row), pl.BlockSpec((tile, width), row)],
        mib=24,
        name="branch_back",
    )


def project_back_body(owners_ref, dq_ref, dk_ref, dv_ref, weight_ref, x_ref, stats_ref, below_ref, out_ref):
    n = dot(dq_ref[...], weight_ref[0], NT) + dot(dk_ref[...], weight_ref[1], NT) + dot(dv_ref[...], weight_ref[2], NT)
    out_ref[: n.shape[0], :] = n.astype(BF)
    unit = (x_ref[...].astype(F32) - stats_ref[:, 0:1]) * stats_ref[:, 1:2]
    with_unit = n * unit
    row = lax.broadcasted_iota(jnp.int32, (EXTRA, n.shape[1]), 0)
    gain_grad = jnp.sum(with_unit, axis=0, keepdims=True)
    shift_grad = jnp.sum(n, axis=0, keepdims=True)
    out_ref[n.shape[0] :, :] = jnp.where(row == 0, gain_grad, jnp.where(row == 1, shift_grad, below_ref[...])).astype(BF)


def project_back(owners, dq, dk, dv, weight, x, stats, below):
    t, width = dq.shape
    count = len(owners)
    whole = still((t, width), lambda j, owners: (0, 0))
    return prefetched(
        project_back_body,
        owners,
        (count,),
        [dq, dk, dv, weight, x, stats, below],
        [
            whole,
            whole,
            whole,
            pl.BlockSpec((3, width, width), lambda j, owners: (0, owners[j], 0)),
            pl.BlockSpec((t, width), lambda j, owners: (0, owners[j])),
            still((t, 128), lambda j, owners: (0, 0)),
            still((EXTRA, width), lambda j, owners: (0, 0)),
        ],
        [sds((t + EXTRA, count * width), BF)],
        [pl.BlockSpec((t + EXTRA, width), lambda j, owners: (0, j))],
        mib=34,
        name="project_back",
    )[0]


def add(a, b):
    return (a.astype(F32) + b.astype(F32)).astype(BF)


class Order:
    def __init__(self):
        self.before = ()

    def __call__(self, value):
        return after(value, *self.before) if self.before else value

    def done(self, *values):
        self.before = tuple(values)


class Gather:
    def __init__(self, share):
        self.n = lax.axis_size("tensor")
        self.pieces = [share]
        self.held = {(i, i): 0 for i in range(self.n)}
        self.steps = 0

    def send(self, piece, pairs, order):
        self.pieces.append(lax.ppermute(order(self.pieces[piece]), "tensor", pairs))

    def step(self, order):
        n, s = self.n, self.steps
        self.steps += 1
        before = len(self.pieces)
        if n == 4:
            outer, inner, out = [(0, 1), (1, 0), (2, 3), (3, 2)], [(1, 2), (2, 1)], [(1, 0), (2, 3)]
            for piece, pairs in (((0, outer), (0, inner)), ((2, out), (1, inner)), ((4, out),))[s]:
                self.send(piece, pairs, order)
            owners = ((1, None, 2, None, 3), (0, 2, None, 3, None), (3, 1, None, 0, None), (2, None, 1, None, 0))
            self.held = {(i, i): 0 for i in range(n)} | {
                (i, owner): 1 + k for i, row in enumerate(owners) for k, owner in enumerate(row) if owner is not None
            }
        else:
            up, down = (0, 0) if s == 0 else (before - 2, before - 1)
            self.held.update({(i + 1, i - s): before for i in range(s, n - 1)})
            self.held.update({(i, i + 1 + s): before + 1 for i in range(n - 1 - s)})
            self.send(up, [(i, i + 1) for i in range(s, n - 1)], order)
            self.send(down, [(i + 1, i) for i in range(n - 1 - s)], order)
        return self.pieces[before:]

    def last(self, order):
        got = self.step(order)
        while self.steps < self.n - 1:
            got = self.step(order)
        return got

    def whole(self):
        share = self.pieces[0]
        t, width = share.shape
        return prefetched(
            functools.partial(assemble_body, self.held),
            [lax.axis_index("tensor")],
            (self.n,),
            self.pieces,
            [still((t, width), lambda j, me: (0, 0))] * len(self.pieces),
            [sds((t, self.n * width), share.dtype)],
            [pl.BlockSpec((t, width), lambda j, me: (0, j))],
            mib=14,
            name="assemble",
        )[0]


def steps(order, *ops):
    return [got for op in ops if op.steps < op.n - 1 for got in op.step(order)]


def finish(order, *ops):
    got = steps(order, *ops)
    while any(op.steps < op.n - 1 for op in ops):
        got = steps(order, *ops)
    return got


def scatter_order(n):
    me = lax.axis_index("tensor")
    first = jnp.where(me < n // 2, n - 1, 0)
    return [(first + k) % n for k in range(n)]


class Scatter:
    def __init__(self, first, rest):
        self.n, self.me = lax.axis_size("tensor"), lax.axis_index("tensor")
        self.first, self.rest, self.steps, self.got = first, rest, 0, {}
        self.width = first.shape[1]

    def part(self, owner, *got):
        place = (owner - jnp.where(self.me < self.n // 2, self.n - 1, 0) - 1) % self.n
        place = jnp.clip(place, 0, self.n - 2)
        value = lax.dynamic_slice_in_dim(self.rest, place * self.width, self.width, 1)
        return functools.reduce(add, got, value)

    def any(self, owner, *got):
        first = jnp.where(self.me < self.n // 2, self.n - 1, 0)
        value = jnp.where(owner % self.n == first, self.first, self.part(owner % self.n))
        return functools.reduce(add, got, value)

    def send(self, name, value, pairs, order):
        self.got[name] = lax.ppermute(order(value), "tensor", pairs)

    def step(self, order):
        n, me, s = self.n, self.me, self.steps
        self.got = got = {name: order(value) for name, value in self.got.items()}
        self.steps += 1
        if n == 4:
            inward, inner, outer = [(0, 1), (3, 2)], [(1, 2), (2, 1)], [(0, 1), (1, 0), (2, 3), (3, 2)]
            if s == 0:
                self.send("far", self.first, inward, order)
                return [got["far"]]
            if s == 1:
                self.send("far", add(self.first, got["far"]), inner, order)
                self.send("next", self.part(jnp.where(me == 0, 2, 1)), inward, order)
            else:
                self.send("far", self.part(me ^ 1, got["far"]), outer, order)
                self.send("next", self.part(3 - me, got["next"]), inner, order)
            return [got["far"], got["next"]]
        up, down = ((got["up"],), (got["down"],)) if s else ((), ())
        self.send("up", self.any(me + n - 1 - s, *up), [(i, i + 1) for i in range(s + 1)], order)
        self.send("down", self.any(me - n + 1 + s, *down), [(i + 1, i) for i in range(n - 2 - s, n - 1)], order)
        return [got["up"], got["down"]]

    def last(self, order):
        got = self.step(order)
        while self.steps < self.n - 1:
            got = self.step(order)
        return got

    def total(self, order):
        self.got = {name: order(value) for name, value in self.got.items()}
        own = self.any(self.me) if self.n != 4 else self.part(self.me)
        return sum((g.astype(F32) for g in self.got.values()), own.astype(F32))


def assemble_body(held, me_ref, *refs):
    out_ref, owner, me = refs[-1], pl.program_id(0), me_ref[0]
    for k, ref in enumerate(refs[:-1]):
        places = [(device, o) for (device, o), at in held.items() if at == k]
        here = functools.reduce(jnp.logical_or, [(me == device) & (owner == o) for device, o in places])

        @pl.when(here)
        def _(ref=ref):
            out_ref[...] = ref[...]


def gradients_body(groups, join, which_ref, *refs):
    lefts, rest = refs[: len(groups)], refs[len(groups) :]
    rights, outs = rest[: sum(groups)], rest[sum(groups) :]
    k = 0
    for left, count in zip(lefts, groups):
        turned = left[...].T
        for right in rights[k : k + count]:
            wide = right.shape[1]
            at = k % join * wide
            outs[k // join][:, at : at + wide] = dot(turned, right[...]).astype(BF)
            k += 1


def gradients(which, pairs, name, join=1):
    t = pairs[0][0].shape[0]
    block = 256
    nb = D // 2 // block
    lefts, rights = [left for left, _ in pairs], [right for _, some in pairs for right in some]
    wide = join * rights[0].shape[1]
    return prefetched(
        functools.partial(gradients_body, [len(some) for _, some in pairs], join),
        [which],
        (nb,),
        lefts + rights,
        [pl.BlockSpec((t, block), lambda i, which: (0, which[0] * nb + i))] * len(lefts)
        + [still(right.shape, lambda i, which: (0, 0)) for right in rights],
        [sds((D // 2, wide), BF)] * (len(rights) // join),
        [pl.BlockSpec((block, wide), lambda i, which: (i, 0))] * (len(rights) // join),
        mib=30 if join > 1 else 56,
        name=name,
    )


def mlp_out_body(owners_ref, hidden_ref, weight_ref, first_ref, rest_ref):
    out = dot(hidden_ref[...], weight_ref[...]).astype(BF)

    @pl.when(pl.program_id(0) == 0)
    def _():
        first_ref[...] = out

    @pl.when(pl.program_id(0) > 0)
    def _():
        rest_ref[...] = out


def mlp_out(owners, width, hidden, weight):
    t, units = hidden.shape
    return prefetched(
        mlp_out_body,
        owners,
        (len(owners),),
        [hidden, weight],
        [
            still((t, units), lambda j, owners: (0, 0)),
            pl.BlockSpec((units, width), lambda j, owners: (0, owners[j])),
        ],
        [sds((t, width), BF), sds((t, D - width), BF)],
        [
            pl.BlockSpec((t, width), lambda j, owners: (0, 0)),
            pl.BlockSpec((t, width), lambda j, owners: (0, jnp.maximum(j - 1, 0))),
        ],
        mib=22,
        name="mlp_out",
    )


def swap(value, bit, axis="dp"):
    n = lax.axis_size(axis)
    return lax.ppermute(value, axis, [(i, i ^ (1 << bit)) for i in range(n)])


def split_body(groups, bits_ref, *refs):
    parts, outs = refs[: 4 * groups], refs[4 * groups :]
    for part in range(2):
        for phase in range(2):

            @pl.when(pl.program_id(0) == phase)
            def _(part=part, phase=phase):
                at = 0
                for g in range(groups):
                    keep, got = parts[2 * (part * groups + g)], parts[2 * (part * groups + g) + 1]
                    wide = keep.shape[1]
                    outs[2 * part + phase][:, at : at + wide] = add(keep[...], got[...])
                    at += wide


def split(upper, lower, bits, joined):
    groups = len(upper)
    rows = upper[0][0].shape[0] // (4 if joined else 2)
    block = min(128, rows)
    nb = rows // block
    columns = sum(keep.shape[1] for keep, _ in upper)
    ins, in_specs = [], []
    for part, pairs in enumerate((upper, lower)):
        first = 2 * nb * part if joined else 0

        def index(phase, j, bits, part=part, first=first):
            half = jnp.where(phase == 0, 1 - bits[part], bits[part])
            return (first + half * nb + j, 0)

        for pair in pairs:
            for array in pair:
                ins.append(array)
                in_specs.append(pl.BlockSpec((block, array.shape[1]), index))
    given = pl.BlockSpec((block, columns), lambda phase, j, bits: (jnp.where(phase == 0, j, nb - 1), 0))
    kept = pl.BlockSpec((block, columns), lambda phase, j, bits: (jnp.where(phase == 0, 0, j), 0))
    return prefetched(
        functools.partial(split_body, groups),
        bits,
        (2, nb),
        ins,
        in_specs,
        [sds((rows, columns), BF)] * 4,
        [given, kept] * 2,
        mib=56 if groups > 2 else 28,
        name="split",
    )


def merge_body(widths, bits_ref, *refs):
    for part in range(2):
        for which in range(2):

            @pl.when((pl.program_id(0) == bits_ref[part]) == (which == 0))
            def _(part=part, which=which):
                value = refs[2 * part + which][...]
                if widths:
                    at = 0
                    for out, wide in zip(refs[4:], widths):
                        out[part] = value[:, at : at + wide]
                        at += wide
                else:
                    refs[4 + part][...] = value


def merge(upper, lower, bits, widths=()):
    rows, columns = upper[0].shape
    block = min(128, rows)
    nb = rows // block

    def spec(part, which):
        def index(i, j, bits):
            half = bits[part] if which == 0 else 1 - bits[part]
            return (jnp.where(i == half, j, jnp.where(i < half, 0, nb - 1)), 0)

        return pl.BlockSpec((block, columns), index)

    if widths:
        outs = [sds((2, 2 * rows, wide), BF) for wide in widths]
        out_specs = [pl.BlockSpec((2, block, wide), lambda i, j, bits: (0, i * nb + j, 0)) for wide in widths]
    else:
        outs = [sds((2 * rows, columns), BF)] * 2
        out_specs = [pl.BlockSpec((block, columns), lambda i, j, bits: (i * nb + j, 0))] * 2
    return prefetched(
        functools.partial(merge_body, widths),
        bits,
        (2, nb),
        [*upper, *lower],
        [spec(part, which) for part in range(2) for which in range(2)],
        outs,
        out_specs,
        mib=56 if widths and columns > D else 22,
        name="merge",
    )


def sum_over_dp(given, order):
    me, n = lax.axis_index("dp"), lax.axis_size("dp")
    count = n.bit_length() - 1
    bit = lambda b: (me >> b) & 1
    orders = [list(range(1, count)), list(range(count - 1, 0, -1))]
    got = [swap(g, 0) for g in given]
    kept = yield got
    upper = lower = [(order(k), g) for k, g in zip(kept, got)]
    for s in range(count - 1):
        a, b = orders[0][s], orders[1][s]
        p_give, p_keep, q_give, q_keep = split(upper, lower, [bit(a), bit(b)], s == 0)
        upper, lower = [(p_keep, swap(p_give, a))], [(q_keep, swap(q_give, b))]
        yield p_keep
        upper, lower = [(order(upper[0][0]), upper[0][1])], [(order(lower[0][0]), lower[0][1])]
    p, q = add(*upper[0]), add(*lower[0])
    for s in reversed(range(count - 1)):
        a, b = orders[0][s], orders[1][s]
        p, q = lax.optimization_barrier((p, q))
        got = swap(p, a), swap(q, b)
        yield p
        out = merge([order(p), got[0]], [q, got[1]], [bit(a), bit(b)], () if s else [g.shape[1] for g in given])
        if s:
            p, q = out
    own = [array.reshape(-1, array.shape[2]) for array in out]
    other = [swap(array, 0) for array in own]
    yield own[0]
    yield own, other


def finish_sum(steps_left):
    *_, last = steps_left
    return last


def halves(core, own, other, nb):
    def index(mine):
        def of(i, bits):
            half = bits[0] if mine else 1 - bits[0]
            return (jnp.clip(i - half * nb, 0, nb - 1), 0)

        return of

    return index(True), index(False)


def halves_body(store, core_ref, *refs):
    half = pl.program_id(0) // (pl.num_programs(0) // 2)
    groups = store.groups
    own, other, outs = refs[:groups], refs[groups : 2 * groups], refs[2 * groups :]
    for arrays, mine in ((own, True), (other, False)):

        @pl.when((half == core_ref[0]) == mine)
        def _(arrays=arrays):
            store(arrays, outs)


def from_halves(store, core, own, other, outs, out_specs, block, mib, name):
    store.groups = len(own)
    nb = own[0].shape[0] // block
    return prefetched(
        functools.partial(halves_body, store),
        [core],
        (2 * nb,),
        [*own, *other],
        [
            pl.BlockSpec((block, array.shape[1]), index)
            for arrays, index in zip((own, other), halves(core, own, other, nb))
            for array in arrays
        ],
        outs,
        out_specs,
        mib=mib,
        name=name,
    )


def gate_up_out(core, own, other):
    def store(arrays, outs):
        for k in range(2):
            outs[0][:, k, :] = arrays[k][...].astype(F32)

    units, block = own[0].shape[1], 128
    outs, spec = [sds((D, 2, units), F32)], [pl.BlockSpec((block, 2, units), lambda i, c: (i, 0, 0))]
    return from_halves(store, core, own, other, outs, spec, block, 56, "gate_up_out")[0]


def down_out(core, own, other):
    def store(arrays, outs):
        outs[0][...] = arrays[0][...].astype(F32).T

    units, block = own[0].shape[1], 128
    outs, spec = [sds((units, D), F32)], [pl.BlockSpec((units, block), lambda i, c: (0, i))]
    return from_halves(store, core, own, other, outs, spec, block, 56, "down_out")[0]


def attention_out(core, own, other):
    def store(arrays, outs):
        for k in range(3):
            outs[0][k] = arrays[0][:, k * width : (k + 1) * width].astype(F32)
        outs[1][...] = arrays[0][:, 3 * width :].astype(F32).T

    width, block = own[0].shape[1] // 4, 256
    outs = [sds((3, D, width), F32), sds((width, D), F32)]
    specs = [
        pl.BlockSpec((3, block, width), lambda i, c: (0, i, 0)),
        pl.BlockSpec((width, block), lambda i, c: (0, i)),
    ]
    return from_halves(store, core, own, other, outs, specs, block, 22, "attention_out")


def per_device(
    tokens,
    norm_one_gain,
    norm_one_shift,
    project_weight,
    project_bias,
    output_weight,
    norm_two_gain,
    norm_two_shift,
    gate_up_weight,
    down_weight,
    cotangent,
):
    width = tokens.shape[1]
    t = tokens.shape[0] // CHUNKS
    offset = lax.axis_index("tensor") * width
    core = lax.axis_index("dp") & 1
    mine = lambda full: lax.dynamic_slice_in_dim(full, offset, width, full.ndim - 1)
    half_of = lambda array, which: lax.dynamic_slice_in_dim(array, which * (D // 2), D // 2, 1)
    order = Order()

    small = jnp.stack([norm_one_gain, norm_one_shift, norm_two_gain, norm_two_shift])
    whole_x = Gather(jnp.concatenate([tokens, jnp.pad(small, ((0, EXTRA - 4), (0, 0)))]))
    whole_up = Gather(cotangent)
    got = whole_x.step(order)
    gate_w = order(gate_up_weight)[:, 0]
    order.done(*got, gate_w)
    got = whole_x.step(order)
    up_w = order(gate_up_weight)[:, 1]
    tables = rope_tables()
    order.done(*got, up_w, tables)
    whole_x.last(order)
    x = whole_x.whole()
    gain_one, gain_two, shift_two = (x[t + i : t + i + 1].astype(F32) for i in (0, 2, 3))
    project_w = project_weight.transpose(1, 0, 2)
    bias = project_bias.astype(F32)[:, None, :]

    through = lambda row: jnp.einsum("d,kdc->kc", row[0].astype(BF), project_w, preferred_element_type=F32)
    with_rows = jnp.stack([through(gain_one), through(x[t + 1 : t + 2]) + bias[:, 0]])

    order.done(x)
    got = whole_up.step(order)
    normed_one, stats_one, heads = project(0, x, project_w, bias, tables, ())
    order.done(*got, stats_one)
    owners = scatter_order(whole_up.n)
    first, rest, context, lse = attend(owners, order(heads), output_weight)
    order.done(lse)
    branch = Scatter(first, rest)
    for _ in range(2):
        order.done(*whole_up.step(order), *branch.step(order), with_rows)
    if whole_up.n > 4:
        whole_up.last(order)
    branch.last(order)
    upstream = whole_up.whole()
    middle_share = tokens.astype(F32) + branch.total(order)
    middle_sent = (middle_share - stats_one[:, 0:1]).astype(BF)
    order.done(middle_sent)
    whole_middle = Gather(middle_sent)
    while whole_middle.steps < whole_middle.n - 1:
        whole_middle.step(order)
    middle = whole_middle.whole()

    normed_two, stats_two, hidden, dgate, dup = mlp(
        0, middle, upstream, gain_two, shift_two, gate_w, up_w, down_weight, ()
    )
    first = mlp_back(owners[:1], width, dgate, dup, gate_w, up_w)
    rest = mlp_back(owners[1:], width, after(dgate, first), dup, gate_w, up_w)
    order.done(first)
    delta_two = Scatter(first, rest)
    got = steps(order, delta_two)
    order.done(rest, *got)
    got = steps(order, delta_two)
    mlp_grads = lambda which, name: gradients(
        which, [(normed_two, [order(dgate), dup]), (upstream, [hidden])], name
    )
    mlp_given = mlp_grads(1 - core, "mlp_given")
    mlp_sum = sum_over_dp(mlp_given, order)
    next(mlp_sum)
    order.done(*got, *mlp_given)
    got = finish(order, delta_two)
    mlp_kept = mlp_grads(core, "mlp_kept")
    order.done(*got, *mlp_kept)
    delta_two = delta_two.total(order)
    unit_two = (mine(middle).astype(F32) - stats_two[:, 0:1]) * stats_two[:, 1:2]
    two_grads = [jnp.sum(delta_two * unit_two, axis=0), jnp.sum(delta_two, axis=0)]
    e_own = delta_two * norm_two_gain.astype(F32)
    e_sent = e_own.astype(BF)
    order.done(e_sent)
    whole_e = Gather(e_sent)
    got = steps(order, whole_e)
    held = mlp_sum.send(mlp_kept)
    order.done(*got, held)
    got = steps(order, whole_e)
    mlp_share = Scatter(*mlp_out(owners, width, order(hidden), down_weight))
    order.done(*got, mlp_share.rest)
    got = finish(order, whole_e) + steps(order, mlp_share)
    held = next(mlp_sum)
    e = whole_e.whole()

    order.done(e, held, *got)
    share_got = steps(order, mlp_share)
    means_two, dbranch, dctx = branch_back(order(e), middle, stats_two, upstream, output_weight)
    order.done(dctx)
    held = next(mlp_sum)
    order.done(held)
    dq, dk, dv, sums = attend_back(heads, lse, context, order(dctx), tables, with_rows)
    held = next(mlp_sum)
    order.done(dq, held, *share_got)
    delta_heads = (dq, dk, dv)
    sum_rows = 2 * t // width
    below = jnp.pad(sums[:2].reshape(sum_rows, width), ((2, EXTRA - 2 - sum_rows), (0, 0)))
    back = lambda owners, dq: project_back(owners, dq, dk, dv, project_w, x, stats_one, below)
    first = back(owners[:1], order(dq))
    rest = back(owners[1:], after(dq, first))
    order.done(first)
    delta_one = Scatter(first, rest)
    got = steps(order, delta_one)
    order.done(rest)
    attention_grads = lambda which, name: gradients(
        which, [(normed_one, [order(dq), dk, dv]), (dbranch, [context])], name, join=4
    )
    attention_given = attention_grads(1 - core, "attention_given")
    attention_sum = sum_over_dp(attention_given, order)
    next(attention_sum)
    order.done(*attention_given, *got)
    got = steps(order, delta_one)
    attention_kept = attention_grads(core, "attention_kept")
    order.done(*attention_kept)
    held = attention_sum.send(attention_kept)
    order.done(held, *got)
    got = finish(order, delta_one)
    held = next(mlp_sum)
    order.done(held)
    held = next(attention_sum)
    order.done(held, *got)
    held = next(attention_sum)
    order.done(held)
    if lax.axis_size("dp") > 8:
        for _ in range(2):
            order.done(next(mlp_sum))
            order.done(next(attention_sum))
    mlp_halves = next(mlp_sum)
    down_grad = down_out(core, [order(mlp_halves[0][2])], mlp_halves[1][2:])
    order.done(down_grad, *got)
    held = next(attention_sum)
    order.done(held)
    share_got = finish(order, mlp_share)
    gate_up_grad = gate_up_out(core, [order(mlp_halves[0][0]), mlp_halves[0][1]], mlp_halves[1][:2])
    order.done(gate_up_grad)
    delta_one = delta_one.total(order)
    bias_grad = [jnp.sum(a, axis=0, dtype=F32) for a in delta_heads]
    small = jnp.stack([delta_one[t], delta_one[t + 1], *two_grads, *bias_grad])
    small = small + swap(small, 0)
    sums = (delta_one[t + 2 : t + 2 + sum_rows] / D).reshape(2, t).T
    unit_one = (tokens.astype(F32) - stats_one[:, 0:1]) * stats_one[:, 1:2]
    dmid = cotangent.astype(F32) + stats_two[:, 1:2] * (e_own - means_two[:, 0:1] - unit_two * means_two[:, 1:2])
    tokens_grad = order(dmid) + stats_one[:, 1:2] * (
        delta_one[:t] * norm_one_gain.astype(F32) - sums[:, 0:1] - unit_one * sums[:, 1:2]
    )
    order.done(small, tokens_grad, *share_got)
    held = next(attention_sum)
    order.done(held)
    devices = lax.axis_size("dp")
    others = [lax.ppermute(order(small), "dp", [(i, i ^ k) for i in range(devices)]) for k in range(2, devices, 2)]
    result = (middle_share + mlp_share.total(order)).astype(BF)
    small = sum((order(other) for other in others), small)
    order.done(tokens_grad, small, result)
    attention_halves = next(attention_sum)
    project_grad, output_grad = attention_out(
        core, [order(attention_halves[0][0]), *attention_halves[0][1:]], attention_halves[1]
    )
    return (
        result,
        tokens_grad,
        small[0],
        small[1],
        project_grad.transpose(1, 0, 2),
        small[4:7],
        output_grad,
        small[2],
        small[3],
        gate_up_grad,
        down_grad,
    )


def solution(mesh):
    return jax.shard_map(
        per_device,
        mesh=mesh,
        in_specs=(
            P("dp", "tensor"),
            P("tensor"),
            P("tensor"),
            P(None, None, "tensor"),
            P(None, "tensor"),
            P("tensor", None),
            P("tensor"),
            P("tensor"),
            P(None, None, "tensor"),
            P("tensor", None),
            P("dp", "tensor"),
        ),
        out_specs=(
            P("dp", "tensor"),
            P("dp", "tensor"),
            P("tensor"),
            P("tensor"),
            P(None, None, "tensor"),
            P(None, "tensor"),
            P("tensor", None),
            P("tensor"),
            P("tensor"),
            P(None, None, "tensor"),
            P("tensor", None),
        ),
        check_vma=False,
    )
```

```python
import functools

import jax
import jax.numpy as jnp
from jax import lax
from jax.experimental import pallas as pl
from jax.experimental.pallas import tpu as pltpu
from jax.sharding import PartitionSpec as P

D = 2048
HEAD_DIM = 64
ROT = 16
SEQ = 1024
PAIR = 2 * HEAD_DIM
CHUNKS = 1
SUB = 256
WEIGHTS = {"mlp_kept": 30, "mlp_out": 10, "attend_back": 20, "merge": 15, "attention_kept": 40}
EXTRA = 16

EPSILON = 1e-05
ROPE_BASE = 10000.0
BF = jnp.bfloat16
F32 = jnp.float32
NT = (((1,), (1,)), ((), ()))
TN = (((0,), (0,)), ((), ()))
ANY = pl.BlockSpec(memory_space=pl.ANY)


def dot(a, b, dims=(((1,), (0,)), ((), ()))):
    return lax.dot_general(a, b, dims, preferred_element_type=F32)


def params(mib):
    return pltpu.CompilerParams(vmem_limit_bytes=mib << 20)


def cost(name):
    return pl.CostEstimate(flops=int(WEIGHTS.get(name, 0) * 1e9), bytes_accessed=0, transcendentals=0)


def after(value, *others):
    return lax.optimization_barrier((value, *others))[0]


def kernel_call(body, grid, ins, in_specs, outs, out_specs, previous=(), scratch=(), mib=56, name=None):
    given = len(ins)
    previous = dict(previous)
    aliases = {given + i: out for i, out in enumerate(previous)}

    def run(*refs):
        body(*refs[:given], *refs[given + len(previous) :])

    return pl.pallas_call(
        run,
        grid=grid,
        in_specs=list(in_specs) + [ANY] * len(previous),
        out_specs=list(out_specs),
        out_shape=list(outs),
        input_output_aliases=aliases,
        scratch_shapes=list(scratch),
        compiler_params=params(mib),
        cost_estimate=cost(name),
        name=name,
    )(*ins, *previous.values())


def still(block, index):
    return pl.BlockSpec(block, index, pipeline_mode=pl.Buffered(1))


def sds(shape, dtype):
    return jax.ShapeDtypeStruct(shape, dtype)


def prefetched(body, scalars, grid, ins, in_specs, outs, out_specs, mib=56, name=None):
    return pl.pallas_call(
        body,
        grid_spec=pltpu.PrefetchScalarGridSpec(
            num_scalar_prefetch=1, grid=grid, in_specs=in_specs, out_specs=out_specs
        ),
        out_shape=outs,
        compiler_params=params(mib),
        cost_estimate=cost(name),
        name=name,
    )(jnp.stack(scalars).astype(jnp.int32), *ins)


def norm_rows(x_ref, gain, shift, normed_ref, stats_ref, rows=64):
    def step(i, carry):
        at = pl.ds(pl.multiple_of(i * rows, rows), rows)
        x = x_ref[at, :].astype(F32)
        mean = jnp.mean(x, axis=-1, keepdims=True)
        centered = x - mean
        inverse = lax.rsqrt(jnp.mean(centered * centered, axis=-1, keepdims=True) + EPSILON)
        normed_ref[at, :] = (centered * inverse * gain + shift).astype(BF)
        lane = lax.broadcasted_iota(jnp.int32, (rows, 128), 1)
        stats_ref[at, :] = jnp.where(lane == 0, mean, inverse)
        return carry

    lax.fori_loop(0, x_ref.shape[0] // rows, step, 0)


def rope_tables():
    lane = jnp.arange(PAIR, dtype=jnp.int32)[None, :] % HEAD_DIM
    half = ROT // 2
    index = (lane % half).astype(F32)
    angles = jnp.arange(SEQ, dtype=F32)[:, None] * ROPE_BASE ** (-(index * (2.0 / ROT)))
    turned = lane < ROT
    cosine = jnp.where(turned, jnp.cos(angles), 1.0)
    low = jnp.where(turned & (lane >= half), jnp.sin(angles), 0.0)
    high = jnp.where(lane < half, -jnp.sin(angles), 0.0)
    return jnp.stack([cosine, low, high])


def turn(values, table):
    half = ROT // 2
    return (
        values * table[0]
        + pltpu.roll(values, half, 1) * table[1]
        + pltpu.roll(values, values.shape[1] - half, 1) * table[2]
    )


def turn_back(values, table):
    half = ROT // 2
    return (
        values * table[0]
        - pltpu.roll(values, half, 1) * table[1]
        - pltpu.roll(values, values.shape[1] - half, 1) * table[2]
    )


def project_body(x_ref, small_ref, weight_ref, bias_ref, table_ref, normed_ref, stats_ref, heads_ref):
    part = pl.program_id(0)

    @pl.when(part == 0)
    def _():
        gain, shift = (small_ref[k : k + 1, :].astype(F32) for k in (0, 1))
        norm_rows(x_ref, gain, shift, normed_ref, stats_ref)

    out = dot(normed_ref[...], weight_ref[0]) + bias_ref[0]
    width = out.shape[1]

    @pl.when(part < 2)
    def _():
        table = table_ref[...]
        for p in range(width // PAIR):
            heads_ref[0, :, p * PAIR : (p + 1) * PAIR] = turn(out[:, p * PAIR : (p + 1) * PAIR], table).astype(BF)

    @pl.when(part == 2)
    def _():
        heads_ref[0] = out.astype(BF)


def project(c, x, weight, bias, tables, previous):
    t, width = x.shape[0] - EXTRA, weight.shape[2]
    total = t * CHUNKS
    one = lambda k: (0, 0)
    return kernel_call(
        project_body,
        (3,),
        [x, x, weight, bias, tables],
        [
            still((t, D), one),
            pl.BlockSpec((EXTRA, D), lambda k: (t // EXTRA, 0)),
            pl.BlockSpec((1, D, width), lambda k: (k, 0, 0)),
            pl.BlockSpec((1, 1, width), lambda k: (k, 0, 0)),
            still((3, t, PAIR), lambda k: (0, c, 0)),
        ],
        [sds((total, D), BF), sds((total, 128), F32), sds((3, total, width), BF)],
        [
            pl.BlockSpec((t, D), lambda k: (c, 0)),
            pl.BlockSpec((t, 128), lambda k: (c, 0)),
            pl.BlockSpec((1, t, width), lambda k: (k, c, 0)),
        ],
        previous,
        mib=56,
        name="project",
    )


def lane_of(rows):
    return lax.broadcasted_iota(jnp.int32, (rows, PAIR), 1) < HEAD_DIM


def attend_body(c, owners_ref, q_ref, k_ref, v_ref, out_weight_ref, first_ref, rest_ref, ctx_ref, lse_ref):
    pair = pl.program_id(0)
    t = q_ref.shape[1]
    scale = HEAD_DIM ** (-0.5)
    low = lane_of(SUB)
    for r in range(t // SUB):
        start = c * t + r * SUB
        extent = start + SUB
        q = q_ref[0, r * SUB : (r + 1) * SUB, :].astype(F32) * scale
        keys = k_ref[0, :extent, :]
        values = v_ref[0, :extent, :]
        row = start + lax.broadcasted_iota(jnp.int32, (SUB, extent), 0)
        seen = lax.broadcasted_iota(jnp.int32, (SUB, extent), 1) <= row
        contexts, sums = [], []
        for h in range(2):
            own = jnp.where(low if h == 0 else ~low, q, 0.0).astype(BF)
            scores = jnp.where(seen, dot(own, keys, NT), -1000000000.0)
            top = jnp.max(scores, axis=-1, keepdims=True)
            raised = jnp.exp(scores - top)
            total = jnp.sum(raised, axis=-1, keepdims=True)
            contexts.append(dot(raised.astype(BF), values) / total)
            sums.append(top + jnp.log(total))
        at = pl.ds(pl.multiple_of(pair * PAIR, PAIR), PAIR)
        ctx_ref[r * SUB : (r + 1) * SUB, at] = jnp.where(low, contexts[0], contexts[1]).astype(BF)
        lse_ref[r * SUB : (r + 1) * SUB, :] = jnp.where(low, sums[0], sums[1])

    @pl.when(pair == pl.num_programs(0) - 1)
    def _():
        wide = first_ref.shape[1]
        for j in range(D // wide):
            at = pl.ds(pl.multiple_of(owners_ref[j] * wide, wide), wide)
            out = dot(ctx_ref[...], out_weight_ref[:, at]).astype(BF)
            if j == 0:
                first_ref[...] = out
            else:
                rest_ref[:, (j - 1) * wide : j * wide] = out


def attend(owners, heads, out_weight):
    t, width = heads.shape[1], heads.shape[2]
    here = lambda p, owners: (0, p)
    fixed = lambda p, owners: (0, 0)
    return prefetched(
        functools.partial(attend_body, 0),
        owners,
        (width // PAIR,),
        [heads, heads, heads, out_weight],
        [pl.BlockSpec((1, t, PAIR), lambda p, owners, k=k: (k, 0, p)) for k in range(3)]
        + [still((width, D), fixed)],
        [sds((t, width), BF), sds((t, D - width), BF), sds((t, width), BF), sds((t, width), F32)],
        [
            pl.BlockSpec((t, width), fixed),
            pl.BlockSpec((t, D - width), fixed),
            pl.BlockSpec((t, width), fixed),
            pl.BlockSpec((t, PAIR), here),
        ],
        mib=30,
        name="attend",
    )


def attend_back_body(c, *refs):
    q_ref, k_ref, v_ref, lse_ref, ctx_ref, dctx_ref, table_ref, with_ref, dq_ref, dk_ref, dv_ref, sums_ref, dk_sum, dv_sum = refs
    t = q_ref.shape[1]

    @pl.when(pl.program_id(0) == 0)
    def _():
        sums_ref[...] = jnp.zeros_like(sums_ref)

    def row_sums(k, gradient, values, at):
        first = gradient * with_ref[0, k : k + 1, :]
        second = gradient * (values - with_ref[1, k : k + 1, :])
        sums_ref[0:1, at] += jnp.sum(first.T, axis=0, keepdims=True)
        sums_ref[1:2, at] += jnp.sum(second.T, axis=0, keepdims=True)

    scale = HEAD_DIM ** (-0.5)
    low = lane_of(SUB)
    dk_sum[...] = jnp.zeros_like(dk_sum)
    dv_sum[...] = jnp.zeros_like(dv_sum)
    for r in range(t // SUB):
        here = slice(r * SUB, (r + 1) * SUB)
        start = c * t + r * SUB
        extent = start + SUB
        q = q_ref[0, here, :].astype(F32) * scale
        keys = k_ref[0, :extent, :]
        values = v_ref[0, :extent, :]
        dctx = dctx_ref[here, :]
        lse_t = lse_ref[here, :].T
        product_t = (ctx_ref[here, :].astype(F32) * dctx.astype(F32)).T
        low_keys = lane_of(extent)
        column = start + lax.broadcasted_iota(jnp.int32, (extent, SUB), 1)
        seen = lax.broadcasted_iota(jnp.int32, (extent, SUB), 0) <= column
        dq = jnp.zeros((SUB, PAIR), F32)
        for h in range(2):
            own = low if h == 0 else ~low
            q_own = jnp.where(own, q, 0.0).astype(BF)
            dctx_own = jnp.where(own, dctx, jnp.zeros_like(dctx))
            rows = slice(h * HEAD_DIM, (h + 1) * HEAD_DIM)
            row_dot = jnp.sum(product_t[rows, :], axis=0, keepdims=True)
            scores = dot(keys, q_own, NT) - lse_t[h * HEAD_DIM : h * HEAD_DIM + 1, :]
            probs = jnp.where(seen, jnp.exp(scores), 0.0)
            delta_probs = dot(values, dctx_own, NT)
            delta_scores = (probs * (delta_probs - row_dot)).astype(BF)
            dv_sum[:extent, :] += dot(probs.astype(BF), dctx_own)
            dk_sum[:extent, :] += dot(delta_scores, q_own)
            keys_own = jnp.where(low_keys if h == 0 else ~low_keys, keys, jnp.zeros_like(keys))
            dq = dq + dot(delta_scores, keys_own, TN)
        table = table_ref[:, start:extent, :]
        dq = turn_back(dq * scale, table)
        dq_ref[here, :] = dq.astype(BF)
        row_sums(0, dq, turn_back(q_ref[0, here, :].astype(F32), table), here)
    for r in range(t // SUB):
        here = slice(r * SUB, (r + 1) * SUB)
        table = table_ref[:, here, :]
        dk = turn_back(dk_sum[here, :], table)
        dk_ref[here, :] = dk.astype(BF)
        row_sums(1, dk, turn_back(k_ref[0, here, :].astype(F32), table), here)
        dv = dv_sum[here, :]
        dv_ref[here, :] = dv.astype(BF)
        row_sums(2, dv, v_ref[0, here, :].astype(F32), here)


def attend_back(heads, lse, ctx, dctx, tables, with_rows):
    t, width = heads.shape[1], heads.shape[2]
    own = pl.BlockSpec((t, PAIR), lambda p: (0, p))
    return kernel_call(
        functools.partial(attend_back_body, 0),
        (width // PAIR,),
        [heads, heads, heads, lse, ctx, dctx, tables, with_rows],
        [pl.BlockSpec((1, t, PAIR), lambda p, k=k: (k, 0, p)) for k in range(3)]
        + [own, own, own, still((3, t, PAIR), lambda p: (0, 0, 0)), pl.BlockSpec((2, 3, PAIR), lambda p: (0, 0, p))],
        [sds((t, width), BF)] * 3 + [sds((8, t), F32)],
        [own, own, own, pl.BlockSpec((8, t), lambda p: (0, 0))],
        scratch=[pltpu.VMEM((t, PAIR), F32)] * 2,
        mib=28,
        name="attend_back",
    )


def mlp_body(mid_ref, up_ref, gain_ref, shift_ref, gate_w_ref, up_w_ref, down_w_ref, normed_ref, stats_ref, hidden_ref, dgate_ref, dup_ref):
    @pl.when(pl.program_id(0) == 0)
    def _():
        norm_rows(mid_ref, gain_ref[...], shift_ref[...], normed_ref, stats_ref)

    normed = normed_ref[...]
    gate = dot(normed, gate_w_ref[...])
    upward = dot(normed, up_w_ref[...])
    delta_hidden = dot(up_ref[...], down_w_ref[...], NT)
    sigmoid = jax.nn.sigmoid(gate)
    silu = gate * sigmoid
    hidden_ref[...] = (silu * upward).astype(BF)
    dgate_ref[...] = (delta_hidden * upward * (sigmoid + silu * (1.0 - sigmoid))).astype(BF)
    dup_ref[...] = (delta_hidden * silu).astype(BF)


def mlp(c, mid, upstream, gain, shift, gate_w, up_w, down_w, previous):
    t, units = mid.shape[0], gate_w.shape[1]
    total = t * CHUNKS
    tile = 256
    one = lambda j: (0, 0)
    own = lambda j: (c, 0)
    column = pl.BlockSpec((t, tile), lambda j: (c, j))
    return kernel_call(
        mlp_body,
        (pl.cdiv(units, tile),),
        [mid, upstream, gain, shift, gate_w, up_w, down_w],
        [
            still((t, D), one),
            still((t, D), own),
            pl.BlockSpec((1, D), one),
            pl.BlockSpec((1, D), one),
            pl.BlockSpec((D, tile), lambda j: (0, j)),
            pl.BlockSpec((D, tile), lambda j: (0, j)),
            pl.BlockSpec((tile, D), lambda j: (j, 0)),
        ],
        [sds((total, D), BF), sds((total, 128), F32)] + [sds((total, units), BF)] * 3,
        [pl.BlockSpec((t, D), own), pl.BlockSpec((t, 128), own), column, column, column],
        previous,
        mib=46,
        name="mlp",
    )


def mlp_back_body(owners_ref, dgate_ref, dup_ref, gate_w_ref, up_w_ref, out_ref):
    out_ref[...] = (dot(dgate_ref[...], gate_w_ref[...], NT) + dot(dup_ref[...], up_w_ref[...], NT)).astype(BF)


def mlp_back(owners, width, dgate, dup, gate_w, up_w):
    t, units = dgate.shape
    whole = still((t, units), lambda j, owners: (0, 0))
    weight = pl.BlockSpec((width, units), lambda j, owners: (owners[j], 0))
    return prefetched(
        mlp_back_body,
        owners,
        (len(owners),),
        [dgate, dup, gate_w, up_w],
        [whole, whole, weight, weight],
        [sds((t, len(owners) * width), BF)],
        [pl.BlockSpec((t, width), lambda j, owners: (0, j))],
        mib=56,
        name="mlp_back",
    )[0]


def branch_back_body(e_ref, mid_ref, stats_ref, up_ref, weight_ref, means_ref, dbranch_ref, dctx_ref):
    rows = 64

    def step(i, carry):
        at = pl.ds(pl.multiple_of(i * rows, rows), rows)
        e = e_ref[at, :].astype(F32)
        mean, inverse = stats_ref[at, 0:1], stats_ref[at, 1:2]
        unit = (mid_ref[at, :].astype(F32) - mean) * inverse
        first = jnp.mean(e, axis=-1, keepdims=True)
        second = jnp.mean(e * unit, axis=-1, keepdims=True)
        dbranch_ref[at, :] = (up_ref[at, :].astype(F32) + inverse * (e - first - unit * second)).astype(BF)
        lane = lax.broadcasted_iota(jnp.int32, (rows, 128), 1)
        means_ref[at, :] = jnp.where(lane == 0, first, second)
        return carry

    lax.fori_loop(0, e_ref.shape[0] // rows, step, 0)
    dctx_ref[...] = dot(dbranch_ref[...], weight_ref[...], NT).astype(BF)


def branch_back(e, mid, stats, upstream, weight):
    t, width = e.shape[0], weight.shape[0]
    tile = SUB
    row = lambda i: (i, 0)
    return kernel_call(
        branch_back_body,
        (t // tile,),
        [e, mid, stats, upstream, weight],
        [
            pl.BlockSpec((tile, D), row),
            pl.BlockSpec((tile, D), row),
            pl.BlockSpec((tile, 128), row),
            pl.BlockSpec((tile, D), row),
            still((width, D), lambda i: (0, 0)),
        ],
        [sds((t, 128), F32), sds((t, D), BF), sds((t, width), BF)],
        [pl.BlockSpec((tile, 128), row), pl.BlockSpec((tile, D), row), pl.BlockSpec((tile, width), row)],
        mib=24,
        name="branch_back",
    )


def project_back_body(owners_ref, dq_ref, dk_ref, dv_ref, weight_ref, x_ref, stats_ref, below_ref, out_ref):
    n = dot(dq_ref[...], weight_ref[0], NT) + dot(dk_ref[...], weight_ref[1], NT) + dot(dv_ref[...], weight_ref[2], NT)
    out_ref[: n.shape[0], :] = n.astype(BF)
    unit = (x_ref[...].astype(F32) - stats_ref[:, 0:1]) * stats_ref[:, 1:2]
    with_unit = n * unit
    row = lax.broadcasted_iota(jnp.int32, (EXTRA, n.shape[1]), 0)
    gain_grad = jnp.sum(with_unit, axis=0, keepdims=True)
    shift_grad = jnp.sum(n, axis=0, keepdims=True)
    out_ref[n.shape[0] :, :] = jnp.where(row == 0, gain_grad, jnp.where(row == 1, shift_grad, below_ref[...])).astype(BF)


def project_back(owners, dq, dk, dv, weight, x, stats, below):
    t, width = dq.shape
    count = len(owners)
    whole = still((t, width), lambda j, owners: (0, 0))
    return prefetched(
        project_back_body,
        owners,
        (count,),
        [dq, dk, dv, weight, x, stats, below],
        [
            whole,
            whole,
            whole,
            pl.BlockSpec((3, width, width), lambda j, owners: (0, owners[j], 0)),
            pl.BlockSpec((t, width), lambda j, owners: (0, owners[j])),
            still((t, 128), lambda j, owners: (0, 0)),
            still((EXTRA, width), lambda j, owners: (0, 0)),
        ],
        [sds((t + EXTRA, count * width), BF)],
        [pl.BlockSpec((t + EXTRA, width), lambda j, owners: (0, j))],
        mib=34,
        name="project_back",
    )[0]


def add(a, b):
    return (a.astype(F32) + b.astype(F32)).astype(BF)


class Order:
    def __init__(self):
        self.before = ()

    def __call__(self, value):
        return after(value, *self.before) if self.before else value

    def done(self, *values):
        self.before = tuple(values)


class Gather:
    def __init__(self, share):
        self.n = lax.axis_size("tensor")
        self.pieces = [share]
        self.held = {(i, i): 0 for i in range(self.n)}
        self.steps = 0

    def send(self, piece, pairs, order):
        self.pieces.append(lax.ppermute(order(self.pieces[piece]), "tensor", pairs))

    def step(self, order):
        n, s = self.n, self.steps
        self.steps += 1
        before = len(self.pieces)
        if n == 4:
            outer, inner, out = [(0, 1), (1, 0), (2, 3), (3, 2)], [(1, 2), (2, 1)], [(1, 0), (2, 3)]
            for piece, pairs in (((0, outer), (0, inner)), ((2, out), (1, inner)), ((4, out),))[s]:
                self.send(piece, pairs, order)
            owners = ((1, None, 2, None, 3), (0, 2, None, 3, None), (3, 1, None, 0, None), (2, None, 1, None, 0))
            self.held = {(i, i): 0 for i in range(n)} | {
                (i, owner): 1 + k for i, row in enumerate(owners) for k, owner in enumerate(row) if owner is not None
            }
        else:
            up, down = (0, 0) if s == 0 else (before - 2, before - 1)
            self.held.update({(i + 1, i - s): before for i in range(s, n - 1)})
            self.held.update({(i, i + 1 + s): before + 1 for i in range(n - 1 - s)})
            self.send(up, [(i, i + 1) for i in range(s, n - 1)], order)
            self.send(down, [(i + 1, i) for i in range(n - 1 - s)], order)
        return self.pieces[before:]

    def last(self, order):
        got = self.step(order)
        while self.steps < self.n - 1:
            got = self.step(order)
        return got

    def whole(self, mib=14):
        share = self.pieces[0]
        t, width = share.shape
        return prefetched(
            functools.partial(assemble_body, self.held),
            [lax.axis_index("tensor")],
            (self.n,),
            self.pieces,
            [still((t, width), lambda j, me: (0, 0))] * len(self.pieces),
            [sds((t, self.n * width), share.dtype)],
            [pl.BlockSpec((t, width), lambda j, me: (0, j))],
            mib=mib,
            name="assemble",
        )[0]


def steps(order, *ops):
    return [got for op in ops if op.steps < op.n - 1 for got in op.step(order)]


def finish(order, *ops):
    got = steps(order, *ops)
    while any(op.steps < op.n - 1 for op in ops):
        got = steps(order, *ops)
    return got


def scatter_order(n):
    me = lax.axis_index("tensor")
    first = jnp.where(me < n // 2, n - 1, 0)
    return [(first + k) % n for k in range(n)]


class Scatter:
    def __init__(self, first, rest):
        self.n, self.me = lax.axis_size("tensor"), lax.axis_index("tensor")
        self.first, self.rest, self.steps, self.got = first, rest, 0, {}
        self.width = first.shape[1]

    def part(self, owner, *got):
        place = (owner - jnp.where(self.me < self.n // 2, self.n - 1, 0) - 1) % self.n
        place = jnp.clip(place, 0, self.n - 2)
        value = lax.dynamic_slice_in_dim(self.rest, place * self.width, self.width, 1)
        return functools.reduce(add, got, value)

    def any(self, owner, *got):
        first = jnp.where(self.me < self.n // 2, self.n - 1, 0)
        value = jnp.where(owner % self.n == first, self.first, self.part(owner % self.n))
        return functools.reduce(add, got, value)

    def send(self, name, value, pairs, order):
        self.got[name] = lax.ppermute(order(value), "tensor", pairs)

    def step(self, order):
        n, me, s = self.n, self.me, self.steps
        self.got = got = {name: order(value) for name, value in self.got.items()}
        self.steps += 1
        if n == 4:
            inward, inner, outer = [(0, 1), (3, 2)], [(1, 2), (2, 1)], [(0, 1), (1, 0), (2, 3), (3, 2)]
            if s == 0:
                self.send("far", self.first, inward, order)
                return [got["far"]]
            if s == 1:
                self.send("far", add(self.first, got["far"]), inner, order)
                self.send("next", self.part(jnp.where(me == 0, 2, 1)), inward, order)
            else:
                self.send("far", self.part(me ^ 1, got["far"]), outer, order)
                self.send("next", self.part(3 - me, got["next"]), inner, order)
            return [got["far"], got["next"]]
        up, down = ((got["up"],), (got["down"],)) if s else ((), ())
        self.send("up", self.any(me + n - 1 - s, *up), [(i, i + 1) for i in range(s + 1)], order)
        self.send("down", self.any(me - n + 1 + s, *down), [(i + 1, i) for i in range(n - 2 - s, n - 1)], order)
        return [got["up"], got["down"]]

    def last(self, order):
        got = self.step(order)
        while self.steps < self.n - 1:
            got = self.step(order)
        return got

    def total(self, order):
        self.got = {name: order(value) for name, value in self.got.items()}
        own = self.any(self.me) if self.n != 4 else self.part(self.me)
        return sum((g.astype(F32) for g in self.got.values()), own.astype(F32))


def assemble_body(held, me_ref, *refs):
    out_ref, owner, me = refs[-1], pl.program_id(0), me_ref[0]
    for k, ref in enumerate(refs[:-1]):
        places = [(device, o) for (device, o), at in held.items() if at == k]
        here = functools.reduce(jnp.logical_or, [(me == device) & (owner == o) for device, o in places])

        @pl.when(here)
        def _(ref=ref):
            out_ref[...] = ref[...]


def gradients_body(groups, join, which_ref, *refs):
    lefts, rest = refs[: len(groups)], refs[len(groups) :]
    rights, outs = rest[: sum(groups)], rest[sum(groups) :]
    k = 0
    for left, count in zip(lefts, groups):
        turned = left[...].T
        for right in rights[k : k + count]:
            wide = right.shape[1]
            at = k % join * wide
            outs[k // join][:, at : at + wide] = dot(turned, right[...]).astype(BF)
            k += 1


def gradients(which, pairs, name, join=1):
    t = pairs[0][0].shape[0]
    block = 256
    nb = D // 2 // block
    lefts, rights = [left for left, _ in pairs], [right for _, some in pairs for right in some]
    wide = join * rights[0].shape[1]
    return prefetched(
        functools.partial(gradients_body, [len(some) for _, some in pairs], join),
        [which],
        (nb,),
        lefts + rights,
        [pl.BlockSpec((t, block), lambda i, which: (0, which[0] * nb + i))] * len(lefts)
        + [still(right.shape, lambda i, which: (0, 0)) for right in rights],
        [sds((D // 2, wide), BF)] * (len(rights) // join),
        [pl.BlockSpec((block, wide), lambda i, which: (i, 0))] * (len(rights) // join),
        mib=30 if join > 1 else 56,
        name=name,
    )


def mlp_out_body(owners_ref, hidden_ref, weight_ref, first_ref, rest_ref):
    out = dot(hidden_ref[...], weight_ref[...]).astype(BF)

    @pl.when(pl.program_id(0) == 0)
    def _():
        first_ref[...] = out

    @pl.when(pl.program_id(0) > 0)
    def _():
        rest_ref[...] = out


def mlp_out(owners, width, hidden, weight):
    t, units = hidden.shape
    return prefetched(
        mlp_out_body,
        owners,
        (len(owners),),
        [hidden, weight],
        [
            still((t, units), lambda j, owners: (0, 0)),
            pl.BlockSpec((units, width), lambda j, owners: (0, owners[j])),
        ],
        [sds((t, width), BF), sds((t, D - width), BF)],
        [
            pl.BlockSpec((t, width), lambda j, owners: (0, 0)),
            pl.BlockSpec((t, width), lambda j, owners: (0, jnp.maximum(j - 1, 0))),
        ],
        mib=22,
        name="mlp_out",
    )


def swap(value, bit, axis="dp"):
    n = lax.axis_size(axis)
    return lax.ppermute(value, axis, [(i, i ^ (1 << bit)) for i in range(n)])


def split_body(groups, bits_ref, *refs):
    parts, outs = refs[: 4 * groups], refs[4 * groups :]
    for part in range(2):
        for phase in range(2):

            @pl.when(pl.program_id(0) == phase)
            def _(part=part, phase=phase):
                at = 0
                for g in range(groups):
                    keep, got = parts[2 * (part * groups + g)], parts[2 * (part * groups + g) + 1]
                    wide = keep.shape[1]
                    outs[2 * part + phase][:, at : at + wide] = add(keep[...], got[...])
                    at += wide


def split(upper, lower, bits, joined):
    groups = len(upper)
    rows = upper[0][0].shape[0] // (4 if joined else 2)
    block = min(128, rows)
    nb = rows // block
    columns = sum(keep.shape[1] for keep, _ in upper)
    ins, in_specs = [], []
    for part, pairs in enumerate((upper, lower)):
        first = 2 * nb * part if joined else 0

        def index(phase, j, bits, part=part, first=first):
            half = jnp.where(phase == 0, 1 - bits[part], bits[part])
            return (first + half * nb + j, 0)

        for pair in pairs:
            for array in pair:
                ins.append(array)
                in_specs.append(pl.BlockSpec((block, array.shape[1]), index))
    given = pl.BlockSpec((block, columns), lambda phase, j, bits: (jnp.where(phase == 0, j, nb - 1), 0))
    kept = pl.BlockSpec((block, columns), lambda phase, j, bits: (jnp.where(phase == 0, 0, j), 0))
    return prefetched(
        functools.partial(split_body, groups),
        bits,
        (2, nb),
        ins,
        in_specs,
        [sds((rows, columns), BF)] * 4,
        [given, kept] * 2,
        mib=56 if groups > 2 else 28,
        name="split",
    )


def merge_body(widths, bits_ref, *refs):
    for part in range(2):
        for which in range(2):

            @pl.when((pl.program_id(0) == bits_ref[part]) == (which == 0))
            def _(part=part, which=which):
                value = refs[2 * part + which][...]
                if widths:
                    at = 0
                    for out, wide in zip(refs[4:], widths):
                        out[part] = value[:, at : at + wide]
                        at += wide
                else:
                    refs[4 + part][...] = value


def merge(upper, lower, bits, widths=()):
    rows, columns = upper[0].shape
    block = min(128, rows)
    nb = rows // block

    def spec(part, which):
        def index(i, j, bits):
            half = bits[part] if which == 0 else 1 - bits[part]
            return (jnp.where(i == half, j, jnp.where(i < half, 0, nb - 1)), 0)

        return pl.BlockSpec((block, columns), index)

    if widths:
        outs = [sds((2, 2 * rows, wide), BF) for wide in widths]
        out_specs = [pl.BlockSpec((2, block, wide), lambda i, j, bits: (0, i * nb + j, 0)) for wide in widths]
    else:
        outs = [sds((2 * rows, columns), BF)] * 2
        out_specs = [pl.BlockSpec((block, columns), lambda i, j, bits: (i * nb + j, 0))] * 2
    return prefetched(
        functools.partial(merge_body, widths),
        bits,
        (2, nb),
        [*upper, *lower],
        [spec(part, which) for part in range(2) for which in range(2)],
        outs,
        out_specs,
        mib=56 if widths and columns > D else 22,
        name="merge",
    )


def sum_over_dp(given, order):
    me, n = lax.axis_index("dp"), lax.axis_size("dp")
    count = n.bit_length() - 1
    bit = lambda b: (me >> b) & 1
    orders = [list(range(1, count)), list(range(count - 1, 0, -1))]
    got = [swap(g, 0) for g in given]
    kept = yield got
    upper = lower = [(order(k), g) for k, g in zip(kept, got)]
    for s in range(count - 1):
        a, b = orders[0][s], orders[1][s]
        p_give, p_keep, q_give, q_keep = split(upper, lower, [bit(a), bit(b)], s == 0)
        upper, lower = [(p_keep, swap(p_give, a))], [(q_keep, swap(q_give, b))]
        yield p_keep
        upper, lower = [(order(upper[0][0]), upper[0][1])], [(order(lower[0][0]), lower[0][1])]
    p, q = add(*upper[0]), add(*lower[0])
    for s in reversed(range(count - 1)):
        a, b = orders[0][s], orders[1][s]
        p, q = lax.optimization_barrier((p, q))
        got = swap(p, a), swap(q, b)
        yield p
        out = merge([order(p), got[0]], [q, got[1]], [bit(a), bit(b)], () if s else [g.shape[1] for g in given])
        if s:
            p, q = out
    own = [array.reshape(-1, array.shape[2]) for array in out]
    other = [swap(array, 0) for array in own]
    yield own[0]
    yield own, other


def finish_sum(steps_left):
    *_, last = steps_left
    return last


def halves(core, own, other, nb):
    def index(mine):
        def of(i, bits):
            half = bits[0] if mine else 1 - bits[0]
            return (jnp.clip(i - half * nb, 0, nb - 1), 0)

        return of

    return index(True), index(False)


def halves_body(store, core_ref, *refs):
    half = pl.program_id(0) // (pl.num_programs(0) // 2)
    groups = store.groups
    own, other, outs = refs[:groups], refs[groups : 2 * groups], refs[2 * groups :]
    for arrays, mine in ((own, True), (other, False)):

        @pl.when((half == core_ref[0]) == mine)
        def _(arrays=arrays):
            store(arrays, outs)


def from_halves(store, core, own, other, outs, out_specs, block, mib, name):
    store.groups = len(own)
    nb = own[0].shape[0] // block
    return prefetched(
        functools.partial(halves_body, store),
        [core],
        (2 * nb,),
        [*own, *other],
        [
            pl.BlockSpec((block, array.shape[1]), index)
            for arrays, index in zip((own, other), halves(core, own, other, nb))
            for array in arrays
        ],
        outs,
        out_specs,
        mib=mib,
        name=name,
    )


def gate_up_out(core, own, other):
    def store(arrays, outs):
        for k in range(2):
            outs[0][:, k, :] = arrays[k][...].astype(F32)

    units, block = own[0].shape[1], 256
    outs, spec = [sds((D, 2, units), F32)], [pl.BlockSpec((block, 2, units), lambda i, c: (i, 0, 0))]
    return from_halves(store, core, own, other, outs, spec, block, 56, "gate_up_out")[0]


def down_out(core, own, other):
    def store(arrays, outs):
        outs[0][...] = arrays[0][...].astype(F32).T

    units, block = own[0].shape[1], 256
    outs, spec = [sds((units, D), F32)], [pl.BlockSpec((units, block), lambda i, c: (0, i))]
    return from_halves(store, core, own, other, outs, spec, block, 56, "down_out")[0]


def attention_out(core, own, other):
    def store(arrays, outs):
        for k in range(3):
            outs[0][k] = arrays[0][:, k * width : (k + 1) * width].astype(F32)
        outs[1][...] = arrays[0][:, 3 * width :].astype(F32).T

    width, block = own[0].shape[1] // 4, 256
    outs = [sds((3, D, width), F32), sds((width, D), F32)]
    specs = [
        pl.BlockSpec((3, block, width), lambda i, c: (0, i, 0)),
        pl.BlockSpec((width, block), lambda i, c: (0, i)),
    ]
    return from_halves(store, core, own, other, outs, specs, block, 22, "attention_out")


def per_device(
    tokens,
    norm_one_gain,
    norm_one_shift,
    project_weight,
    project_bias,
    output_weight,
    norm_two_gain,
    norm_two_shift,
    gate_up_weight,
    down_weight,
    cotangent,
):
    width = tokens.shape[1]
    t = tokens.shape[0] // CHUNKS
    offset = lax.axis_index("tensor") * width
    core = lax.axis_index("dp") & 1
    mine = lambda full: lax.dynamic_slice_in_dim(full, offset, width, full.ndim - 1)
    half_of = lambda array, which: lax.dynamic_slice_in_dim(array, which * (D // 2), D // 2, 1)
    order = Order()

    small = jnp.stack([norm_one_gain, norm_one_shift, norm_two_gain, norm_two_shift])
    whole_x = Gather(jnp.concatenate([tokens, jnp.pad(small, ((0, EXTRA - 4), (0, 0)))]))
    whole_up = Gather(cotangent)
    got = whole_x.step(order)
    gate_w = order(gate_up_weight)[:, 0]
    order.done(*got, gate_w)
    got = whole_x.step(order)
    up_w = order(gate_up_weight)[:, 1]
    tables = rope_tables()
    order.done(*got, up_w, tables)
    whole_x.last(order)
    x = whole_x.whole(56)
    gain_one, gain_two, shift_two = (x[t + i : t + i + 1].astype(F32) for i in (0, 2, 3))
    project_w = project_weight.transpose(1, 0, 2)
    bias = project_bias.astype(F32)[:, None, :]

    through = lambda row: jnp.einsum("d,kdc->kc", row[0].astype(BF), project_w, preferred_element_type=F32)
    with_rows = jnp.stack([through(gain_one), through(x[t + 1 : t + 2]) + bias[:, 0]])

    order.done(x)
    got = whole_up.step(order)
    normed_one, stats_one, heads = project(0, x, project_w, bias, tables, ())
    order.done(*got, stats_one)
    owners = scatter_order(whole_up.n)
    first, rest, context, lse = attend(owners, order(heads), output_weight)
    order.done(lse)
    branch = Scatter(first, rest)
    for _ in range(2):
        order.done(*whole_up.step(order), *branch.step(order), with_rows)
    if whole_up.n > 4:
        whole_up.last(order)
    branch.last(order)
    upstream = whole_up.whole()
    middle_share = tokens.astype(F32) + branch.total(order)
    middle_sent = (middle_share - stats_one[:, 0:1]).astype(BF)
    order.done(middle_sent)
    whole_middle = Gather(middle_sent)
    while whole_middle.steps < whole_middle.n - 1:
        whole_middle.step(order)
    middle = whole_middle.whole()

    normed_two, stats_two, hidden, dgate, dup = mlp(
        0, middle, upstream, gain_two, shift_two, gate_w, up_w, down_weight, ()
    )
    first = mlp_back(owners[:1], width, dgate, dup, gate_w, up_w)
    rest = mlp_back(owners[1:], width, after(dgate, first), dup, gate_w, up_w)
    order.done(first)
    delta_two = Scatter(first, rest)
    got = steps(order, delta_two)
    order.done(rest, *got)
    got = steps(order, delta_two)
    mlp_grads = lambda which, name: gradients(
        which, [(normed_two, [order(dgate), dup]), (upstream, [hidden])], name
    )
    mlp_given = mlp_grads(1 - core, "mlp_given")
    mlp_sum = sum_over_dp(mlp_given, order)
    next(mlp_sum)
    order.done(*got, *mlp_given)
    got = finish(order, delta_two)
    mlp_kept = mlp_grads(core, "mlp_kept")
    order.done(*got, *mlp_kept)
    delta_two = delta_two.total(order)
    unit_two = (mine(middle).astype(F32) - stats_two[:, 0:1]) * stats_two[:, 1:2]
    two_grads = [jnp.sum(delta_two * unit_two, axis=0), jnp.sum(delta_two, axis=0)]
    e_own = delta_two * norm_two_gain.astype(F32)
    e_sent = e_own.astype(BF)
    order.done(e_sent)
    whole_e = Gather(e_sent)
    got = steps(order, whole_e)
    held = mlp_sum.send(mlp_kept)
    order.done(*got, held)
    got = steps(order, whole_e)
    mlp_share = Scatter(*mlp_out(owners, width, order(hidden), down_weight))
    order.done(*got, mlp_share.rest)
    got = finish(order, whole_e) + steps(order, mlp_share)
    held = next(mlp_sum)
    e = whole_e.whole()

    order.done(e, held, *got)
    share_got = steps(order, mlp_share)
    means_two, dbranch, dctx = branch_back(order(e), middle, stats_two, upstream, output_weight)
    order.done(dctx)
    held = next(mlp_sum)
    order.done(held)
    dq, dk, dv, sums = attend_back(heads, lse, context, order(dctx), tables, with_rows)
    held = next(mlp_sum)
    order.done(dq, held, *share_got)
    delta_heads = (dq, dk, dv)
    sum_rows = 2 * t // width
    below = jnp.pad(sums[:2].reshape(sum_rows, width), ((2, EXTRA - 2 - sum_rows), (0, 0)))
    back = lambda owners, dq: project_back(owners, dq, dk, dv, project_w, x, stats_one, below)
    first = back(owners[:1], order(dq))
    rest = back(owners[1:], after(dq, first))
    order.done(first)
    delta_one = Scatter(first, rest)
    got = steps(order, delta_one)
    order.done(rest)
    attention_grads = lambda which, name: gradients(
        which, [(normed_one, [order(dq), dk, dv]), (dbranch, [context])], name, join=4
    )
    attention_given = attention_grads(1 - core, "attention_given")
    attention_sum = sum_over_dp(attention_given, order)
    next(attention_sum)
    order.done(*attention_given, *got)
    got = steps(order, delta_one)
    attention_kept = attention_grads(core, "attention_kept")
    order.done(*attention_kept)
    held = attention_sum.send(attention_kept)
    order.done(held, *got)
    got = finish(order, delta_one)
    held = next(mlp_sum)
    order.done(held)
    held = next(attention_sum)
    order.done(held, *got)
    held = next(attention_sum)
    order.done(held)
    if lax.axis_size("dp") > 8:
        for _ in range(2):
            order.done(next(mlp_sum))
            order.done(next(attention_sum))
    mlp_halves = next(mlp_sum)
    down_grad = down_out(core, [order(mlp_halves[0][2])], mlp_halves[1][2:])
    order.done(down_grad, *got)
    held = next(attention_sum)
    order.done(held)
    share_got = finish(order, mlp_share)
    gate_up_grad = gate_up_out(core, [order(mlp_halves[0][0]), mlp_halves[0][1]], mlp_halves[1][:2])
    order.done(gate_up_grad)
    delta_one = delta_one.total(order)
    bias_grad = [jnp.sum(a, axis=0, dtype=F32) for a in delta_heads]
    small = jnp.stack([delta_one[t], delta_one[t + 1], *two_grads, *bias_grad])
    small = small + swap(small, 0)
    sums = (delta_one[t + 2 : t + 2 + sum_rows] / D).reshape(2, t).T
    unit_one = (tokens.astype(F32) - stats_one[:, 0:1]) * stats_one[:, 1:2]
    dmid = cotangent.astype(F32) + stats_two[:, 1:2] * (e_own - means_two[:, 0:1] - unit_two * means_two[:, 1:2])
    tokens_grad = order(dmid) + stats_one[:, 1:2] * (
        delta_one[:t] * norm_one_gain.astype(F32) - sums[:, 0:1] - unit_one * sums[:, 1:2]
    )
    order.done(small, tokens_grad, *share_got)
    held = next(attention_sum)
    order.done(held)
    devices = lax.axis_size("dp")
    others = [lax.ppermute(order(small), "dp", [(i, i ^ k) for i in range(devices)]) for k in range(2, devices, 2)]
    result = (middle_share + mlp_share.total(order)).astype(BF)
    small = sum((order(other) for other in others), small)
    order.done(tokens_grad, small, result)
    attention_halves = next(attention_sum)
    project_grad, output_grad = attention_out(
        core, [order(attention_halves[0][0]), *attention_halves[0][1:]], attention_halves[1]
    )
    return (
        result,
        tokens_grad,
        small[0],
        small[1],
        project_grad.transpose(1, 0, 2),
        small[4:7],
        output_grad,
        small[2],
        small[3],
        gate_up_grad,
        down_grad,
    )


def solution(mesh):
    return jax.shard_map(
        per_device,
        mesh=mesh,
        in_specs=(
            P("dp", "tensor"),
            P("tensor"),
            P("tensor"),
            P(None, None, "tensor"),
            P(None, "tensor"),
            P("tensor", None),
            P("tensor"),
            P("tensor"),
            P(None, None, "tensor"),
            P("tensor", None),
            P("dp", "tensor"),
        ),
        out_specs=(
            P("dp", "tensor"),
            P("dp", "tensor"),
            P("tensor"),
            P("tensor"),
            P(None, None, "tensor"),
            P(None, "tensor"),
            P("tensor", None),
            P("tensor"),
            P("tensor"),
            P(None, None, "tensor"),
            P("tensor", None),
        ),
        check_vma=False,
    )
```

```python
import functools

import jax
import jax.numpy as jnp
from jax import lax
from jax.experimental import pallas as pl
from jax.experimental.pallas import tpu as pltpu
from jax.sharding import PartitionSpec as P

D = 2048
HEAD_DIM = 64
ROT = 16
SEQ = 1024
PAIR = 2 * HEAD_DIM
CHUNKS = 1
SUB = 256
WEIGHTS = {"mlp_kept": 30, "mlp_out": 10, "attend_back": 20, "merge": 15, "attention_kept": 40}
EXTRA = 16

EPSILON = 1e-05
ROPE_BASE = 10000.0
BF = jnp.bfloat16
F32 = jnp.float32
NT = (((1,), (1,)), ((), ()))
TN = (((0,), (0,)), ((), ()))
ANY = pl.BlockSpec(memory_space=pl.ANY)


def dot(a, b, dims=(((1,), (0,)), ((), ()))):
    return lax.dot_general(a, b, dims, preferred_element_type=F32)


def params(mib):
    return pltpu.CompilerParams(vmem_limit_bytes=mib << 20)


def cost(name):
    return pl.CostEstimate(flops=int(WEIGHTS.get(name, 0) * 1e9), bytes_accessed=0, transcendentals=0)


def after(value, *others):
    return lax.optimization_barrier((value, *others))[0]


def kernel_call(body, grid, ins, in_specs, outs, out_specs, previous=(), scratch=(), mib=56, name=None):
    given = len(ins)
    previous = dict(previous)
    aliases = {given + i: out for i, out in enumerate(previous)}

    def run(*refs):
        body(*refs[:given], *refs[given + len(previous) :])

    return pl.pallas_call(
        run,
        grid=grid,
        in_specs=list(in_specs) + [ANY] * len(previous),
        out_specs=list(out_specs),
        out_shape=list(outs),
        input_output_aliases=aliases,
        scratch_shapes=list(scratch),
        compiler_params=params(mib),
        cost_estimate=cost(name),
        name=name,
    )(*ins, *previous.values())


def still(block, index):
    return pl.BlockSpec(block, index, pipeline_mode=pl.Buffered(1))


def sds(shape, dtype):
    return jax.ShapeDtypeStruct(shape, dtype)


def prefetched(body, scalars, grid, ins, in_specs, outs, out_specs, mib=56, name=None):
    return pl.pallas_call(
        body,
        grid_spec=pltpu.PrefetchScalarGridSpec(
            num_scalar_prefetch=1, grid=grid, in_specs=in_specs, out_specs=out_specs
        ),
        out_shape=outs,
        compiler_params=params(mib),
        cost_estimate=cost(name),
        name=name,
    )(jnp.stack(scalars).astype(jnp.int32), *ins)


def norm_rows(x_ref, gain, shift, normed_ref, stats_ref, rows=64):
    def step(i, carry):
        at = pl.ds(pl.multiple_of(i * rows, rows), rows)
        x = x_ref[at, :].astype(F32)
        mean = jnp.mean(x, axis=-1, keepdims=True)
        centered = x - mean
        inverse = lax.rsqrt(jnp.mean(centered * centered, axis=-1, keepdims=True) + EPSILON)
        normed_ref[at, :] = (centered * inverse * gain + shift).astype(BF)
        lane = lax.broadcasted_iota(jnp.int32, (rows, 128), 1)
        stats_ref[at, :] = jnp.where(lane == 0, mean, inverse)
        return carry

    lax.fori_loop(0, x_ref.shape[0] // rows, step, 0)


def rope_tables():
    lane = jnp.arange(PAIR, dtype=jnp.int32)[None, :] % HEAD_DIM
    half = ROT // 2
    index = (lane % half).astype(F32)
    angles = jnp.arange(SEQ, dtype=F32)[:, None] * ROPE_BASE ** (-(index * (2.0 / ROT)))
    turned = lane < ROT
    cosine = jnp.where(turned, jnp.cos(angles), 1.0)
    low = jnp.where(turned & (lane >= half), jnp.sin(angles), 0.0)
    high = jnp.where(lane < half, -jnp.sin(angles), 0.0)
    return jnp.stack([cosine, low, high])


def turn(values, table):
    half = ROT // 2
    return (
        values * table[0]
        + pltpu.roll(values, half, 1) * table[1]
        + pltpu.roll(values, values.shape[1] - half, 1) * table[2]
    )


def turn_back(values, table):
    half = ROT // 2
    return (
        values * table[0]
        - pltpu.roll(values, half, 1) * table[1]
        - pltpu.roll(values, values.shape[1] - half, 1) * table[2]
    )


def project_body(x_ref, small_ref, weight_ref, bias_ref, table_ref, normed_ref, stats_ref, heads_ref):
    part = pl.program_id(0)

    @pl.when(part == 0)
    def _():
        gain, shift = (small_ref[k : k + 1, :].astype(F32) for k in (0, 1))
        norm_rows(x_ref, gain, shift, normed_ref, stats_ref)

    out = dot(normed_ref[...], weight_ref[0]) + bias_ref[0]
    width = out.shape[1]

    @pl.when(part < 2)
    def _():
        table = table_ref[...]
        for p in range(width // PAIR):
            heads_ref[0, :, p * PAIR : (p + 1) * PAIR] = turn(out[:, p * PAIR : (p + 1) * PAIR], table).astype(BF)

    @pl.when(part == 2)
    def _():
        heads_ref[0] = out.astype(BF)


def project(c, x, weight, bias, tables, previous):
    t, width = x.shape[0] - EXTRA, weight.shape[2]
    total = t * CHUNKS
    one = lambda k: (0, 0)
    return kernel_call(
        project_body,
        (3,),
        [x, x, weight, bias, tables],
        [
            still((t, D), one),
            pl.BlockSpec((EXTRA, D), lambda k: (t // EXTRA, 0)),
            pl.BlockSpec((1, D, width), lambda k: (k, 0, 0)),
            pl.BlockSpec((1, 1, width), lambda k: (k, 0, 0)),
            still((3, t, PAIR), lambda k: (0, c, 0)),
        ],
        [sds((total, D), BF), sds((total, 128), F32), sds((3, total, width), BF)],
        [
            pl.BlockSpec((t, D), lambda k: (c, 0)),
            pl.BlockSpec((t, 128), lambda k: (c, 0)),
            pl.BlockSpec((1, t, width), lambda k: (k, c, 0)),
        ],
        previous,
        mib=34,
        name="project",
    )


def lane_of(rows):
    return lax.broadcasted_iota(jnp.int32, (rows, PAIR), 1) < HEAD_DIM


def attend_body(c, owners_ref, q_ref, k_ref, v_ref, out_weight_ref, first_ref, rest_ref, ctx_ref, lse_ref):
    pair = pl.program_id(0)
    t = q_ref.shape[1]
    scale = HEAD_DIM ** (-0.5)
    low = lane_of(SUB)
    for r in range(t // SUB):
        start = c * t + r * SUB
        extent = start + SUB
        q = q_ref[0, r * SUB : (r + 1) * SUB, :].astype(F32) * scale
        keys = k_ref[0, :extent, :]
        values = v_ref[0, :extent, :]
        row = start + lax.broadcasted_iota(jnp.int32, (SUB, extent), 0)
        seen = lax.broadcasted_iota(jnp.int32, (SUB, extent), 1) <= row
        contexts, sums = [], []
        for h in range(2):
            own = jnp.where(low if h == 0 else ~low, q, 0.0).astype(BF)
            scores = jnp.where(seen, dot(own, keys, NT), -1000000000.0)
            top = jnp.max(scores, axis=-1, keepdims=True)
            raised = jnp.exp(scores - top)
            total = jnp.sum(raised, axis=-1, keepdims=True)
            contexts.append(dot(raised.astype(BF), values) / total)
            sums.append(top + jnp.log(total))
        at = pl.ds(pl.multiple_of(pair * PAIR, PAIR), PAIR)
        ctx_ref[r * SUB : (r + 1) * SUB, at] = jnp.where(low, contexts[0], contexts[1]).astype(BF)
        lse_ref[r * SUB : (r + 1) * SUB, :] = jnp.where(low, sums[0], sums[1])

    @pl.when(pair == pl.num_programs(0) - 1)
    def _():
        wide = first_ref.shape[1]
        for j in range(D // wide):
            at = pl.ds(pl.multiple_of(owners_ref[j] * wide, wide), wide)
            out = dot(ctx_ref[...], out_weight_ref[:, at]).astype(BF)
            if j == 0:
                first_ref[...] = out
            else:
                rest_ref[:, (j - 1) * wide : j * wide] = out


def attend(owners, heads, out_weight):
    t, width = heads.shape[1], heads.shape[2]
    here = lambda p, owners: (0, p)
    fixed = lambda p, owners: (0, 0)
    return prefetched(
        functools.partial(attend_body, 0),
        owners,
        (width // PAIR,),
        [heads, heads, heads, out_weight],
        [pl.BlockSpec((1, t, PAIR), lambda p, owners, k=k: (k, 0, p)) for k in range(3)]
        + [still((width, D), fixed)],
        [sds((t, width), BF), sds((t, D - width), BF), sds((t, width), BF), sds((t, width), F32)],
        [
            pl.BlockSpec((t, width), fixed),
            pl.BlockSpec((t, D - width), fixed),
            pl.BlockSpec((t, width), fixed),
            pl.BlockSpec((t, PAIR), here),
        ],
        mib=30,
        name="attend",
    )


def attend_back_body(c, *refs):
    q_ref, k_ref, v_ref, lse_ref, ctx_ref, dctx_ref, table_ref, with_ref, dq_ref, dk_ref, dv_ref, sums_ref, dk_sum, dv_sum = refs
    t = q_ref.shape[1]

    @pl.when(pl.program_id(0) == 0)
    def _():
        sums_ref[...] = jnp.zeros_like(sums_ref)

    def row_sums(k, gradient, values, at):
        first = gradient * with_ref[0, k : k + 1, :]
        second = gradient * (values - with_ref[1, k : k + 1, :])
        sums_ref[0:1, at] += jnp.sum(first.T, axis=0, keepdims=True)
        sums_ref[1:2, at] += jnp.sum(second.T, axis=0, keepdims=True)

    scale = HEAD_DIM ** (-0.5)
    low = lane_of(SUB)
    dk_sum[...] = jnp.zeros_like(dk_sum)
    dv_sum[...] = jnp.zeros_like(dv_sum)
    for r in range(t // SUB):
        here = slice(r * SUB, (r + 1) * SUB)
        start = c * t + r * SUB
        extent = start + SUB
        q = q_ref[0, here, :].astype(F32) * scale
        keys = k_ref[0, :extent, :]
        values = v_ref[0, :extent, :]
        dctx = dctx_ref[here, :]
        lse_t = lse_ref[here, :].T
        product_t = (ctx_ref[here, :].astype(F32) * dctx.astype(F32)).T
        low_keys = lane_of(extent)
        column = start + lax.broadcasted_iota(jnp.int32, (extent, SUB), 1)
        seen = lax.broadcasted_iota(jnp.int32, (extent, SUB), 0) <= column
        dq = jnp.zeros((SUB, PAIR), F32)
        for h in range(2):
            own = low if h == 0 else ~low
            q_own = jnp.where(own, q, 0.0).astype(BF)
            dctx_own = jnp.where(own, dctx, jnp.zeros_like(dctx))
            rows = slice(h * HEAD_DIM, (h + 1) * HEAD_DIM)
            row_dot = jnp.sum(product_t[rows, :], axis=0, keepdims=True)
            scores = dot(keys, q_own, NT) - lse_t[h * HEAD_DIM : h * HEAD_DIM + 1, :]
            probs = jnp.where(seen, jnp.exp(scores), 0.0)
            delta_probs = dot(values, dctx_own, NT)
            delta_scores = (probs * (delta_probs - row_dot)).astype(BF)
            dv_sum[:extent, :] += dot(probs.astype(BF), dctx_own)
            dk_sum[:extent, :] += dot(delta_scores, q_own)
            keys_own = jnp.where(low_keys if h == 0 else ~low_keys, keys, jnp.zeros_like(keys))
            dq = dq + dot(delta_scores, keys_own, TN)
        table = table_ref[:, start:extent, :]
        dq = turn_back(dq * scale, table)
        dq_ref[here, :] = dq.astype(BF)
        row_sums(0, dq, turn_back(q_ref[0, here, :].astype(F32), table), here)
    for r in range(t // SUB):
        here = slice(r * SUB, (r + 1) * SUB)
        table = table_ref[:, here, :]
        dk = turn_back(dk_sum[here, :], table)
        dk_ref[here, :] = dk.astype(BF)
        row_sums(1, dk, turn_back(k_ref[0, here, :].astype(F32), table), here)
        dv = dv_sum[here, :]
        dv_ref[here, :] = dv.astype(BF)
        row_sums(2, dv, v_ref[0, here, :].astype(F32), here)


def attend_back(heads, lse, ctx, dctx, tables, with_rows):
    t, width = heads.shape[1], heads.shape[2]
    own = pl.BlockSpec((t, PAIR), lambda p: (0, p))
    return kernel_call(
        functools.partial(attend_back_body, 0),
        (width // PAIR,),
        [heads, heads, heads, lse, ctx, dctx, tables, with_rows],
        [pl.BlockSpec((1, t, PAIR), lambda p, k=k: (k, 0, p)) for k in range(3)]
        + [own, own, own, still((3, t, PAIR), lambda p: (0, 0, 0)), pl.BlockSpec((2, 3, PAIR), lambda p: (0, 0, p))],
        [sds((t, width), BF)] * 3 + [sds((8, t), F32)],
        [own, own, own, pl.BlockSpec((8, t), lambda p: (0, 0))],
        scratch=[pltpu.VMEM((t, PAIR), F32)] * 2,
        mib=28,
        name="attend_back",
    )


def mlp_body(mid_ref, up_ref, gain_ref, shift_ref, gate_w_ref, up_w_ref, down_w_ref, normed_ref, stats_ref, hidden_ref, dgate_ref, dup_ref):
    @pl.when(pl.program_id(0) == 0)
    def _():
        norm_rows(mid_ref, gain_ref[...], shift_ref[...], normed_ref, stats_ref)

    normed = normed_ref[...]
    gate = dot(normed, gate_w_ref[...])
    upward = dot(normed, up_w_ref[...])
    delta_hidden = dot(up_ref[...], down_w_ref[...], NT)
    sigmoid = jax.nn.sigmoid(gate)
    silu = gate * sigmoid
    hidden_ref[...] = (silu * upward).astype(BF)
    dgate_ref[...] = (delta_hidden * upward * (sigmoid + silu * (1.0 - sigmoid))).astype(BF)
    dup_ref[...] = (delta_hidden * silu).astype(BF)


def mlp(c, mid, upstream, gain, shift, gate_w, up_w, down_w, previous):
    t, units = mid.shape[0], gate_w.shape[1]
    total = t * CHUNKS
    tile = 256
    one = lambda j: (0, 0)
    own = lambda j: (c, 0)
    column = pl.BlockSpec((t, tile), lambda j: (c, j))
    return kernel_call(
        mlp_body,
        (pl.cdiv(units, tile),),
        [mid, upstream, gain, shift, gate_w, up_w, down_w],
        [
            still((t, D), one),
            still((t, D), own),
            pl.BlockSpec((1, D), one),
            pl.BlockSpec((1, D), one),
            pl.BlockSpec((D, tile), lambda j: (0, j)),
            pl.BlockSpec((D, tile), lambda j: (0, j)),
            pl.BlockSpec((tile, D), lambda j: (j, 0)),
        ],
        [sds((total, D), BF), sds((total, 128), F32)] + [sds((total, units), BF)] * 3,
        [pl.BlockSpec((t, D), own), pl.BlockSpec((t, 128), own), column, column, column],
        previous,
        mib=46,
        name="mlp",
    )


def mlp_back_body(owners_ref, dgate_ref, dup_ref, gate_w_ref, up_w_ref, out_ref):
    out_ref[...] = (dot(dgate_ref[...], gate_w_ref[...], NT) + dot(dup_ref[...], up_w_ref[...], NT)).astype(BF)


def mlp_back(owners, width, dgate, dup, gate_w, up_w):
    t, units = dgate.shape
    whole = still((t, units), lambda j, owners: (0, 0))
    weight = pl.BlockSpec((width, units), lambda j, owners: (owners[j], 0))
    return prefetched(
        mlp_back_body,
        owners,
        (len(owners),),
        [dgate, dup, gate_w, up_w],
        [whole, whole, weight, weight],
        [sds((t, len(owners) * width), BF)],
        [pl.BlockSpec((t, width), lambda j, owners: (0, j))],
        mib=56,
        name="mlp_back",
    )[0]


def branch_back_body(e_ref, mid_ref, stats_ref, up_ref, weight_ref, means_ref, dbranch_ref, dctx_ref):
    rows = 64

    def step(i, carry):
        at = pl.ds(pl.multiple_of(i * rows, rows), rows)
        e = e_ref[at, :].astype(F32)
        mean, inverse = stats_ref[at, 0:1], stats_ref[at, 1:2]
        unit = (mid_ref[at, :].astype(F32) - mean) * inverse
        first = jnp.mean(e, axis=-1, keepdims=True)
        second = jnp.mean(e * unit, axis=-1, keepdims=True)
        dbranch_ref[at, :] = (up_ref[at, :].astype(F32) + inverse * (e - first - unit * second)).astype(BF)
        lane = lax.broadcasted_iota(jnp.int32, (rows, 128), 1)
        means_ref[at, :] = jnp.where(lane == 0, first, second)
        return carry

    lax.fori_loop(0, e_ref.shape[0] // rows, step, 0)
    dctx_ref[...] = dot(dbranch_ref[...], weight_ref[...], NT).astype(BF)


def branch_back(e, mid, stats, upstream, weight):
    t, width = e.shape[0], weight.shape[0]
    tile = SUB
    row = lambda i: (i, 0)
    return kernel_call(
        branch_back_body,
        (t // tile,),
        [e, mid, stats, upstream, weight],
        [
            pl.BlockSpec((tile, D), row),
            pl.BlockSpec((tile, D), row),
            pl.BlockSpec((tile, 128), row),
            pl.BlockSpec((tile, D), row),
            still((width, D), lambda i: (0, 0)),
        ],
        [sds((t, 128), F32), sds((t, D), BF), sds((t, width), BF)],
        [pl.BlockSpec((tile, 128), row), pl.BlockSpec((tile, D), row), pl.BlockSpec((tile, width), row)],
        mib=24,
        name="branch_back",
    )


def project_back_body(owners_ref, dq_ref, dk_ref, dv_ref, weight_ref, x_ref, stats_ref, below_ref, out_ref):
    n = dot(dq_ref[...], weight_ref[0], NT) + dot(dk_ref[...], weight_ref[1], NT) + dot(dv_ref[...], weight_ref[2], NT)
    out_ref[: n.shape[0], :] = n.astype(BF)
    unit = (x_ref[...].astype(F32) - stats_ref[:, 0:1]) * stats_ref[:, 1:2]
    with_unit = n * unit
    row = lax.broadcasted_iota(jnp.int32, (EXTRA, n.shape[1]), 0)
    gain_grad = jnp.sum(with_unit, axis=0, keepdims=True)
    shift_grad = jnp.sum(n, axis=0, keepdims=True)
    out_ref[n.shape[0] :, :] = jnp.where(row == 0, gain_grad, jnp.where(row == 1, shift_grad, below_ref[...])).astype(BF)


def project_back(owners, dq, dk, dv, weight, x, stats, below):
    t, width = dq.shape
    count = len(owners)
    whole = still((t, width), lambda j, owners: (0, 0))
    return prefetched(
        project_back_body,
        owners,
        (count,),
        [dq, dk, dv, weight, x, stats, below],
        [
            whole,
            whole,
            whole,
            pl.BlockSpec((3, width, width), lambda j, owners: (0, owners[j], 0)),
            pl.BlockSpec((t, width), lambda j, owners: (0, owners[j])),
            still((t, 128), lambda j, owners: (0, 0)),
            still((EXTRA, width), lambda j, owners: (0, 0)),
        ],
        [sds((t + EXTRA, count * width), BF)],
        [pl.BlockSpec((t + EXTRA, width), lambda j, owners: (0, j))],
        mib=34,
        name="project_back",
    )[0]


def add(a, b):
    return (a.astype(F32) + b.astype(F32)).astype(BF)


class Order:
    def __init__(self):
        self.before = ()

    def __call__(self, value):
        return after(value, *self.before) if self.before else value

    def done(self, *values):
        self.before = tuple(values)


class Gather:
    def __init__(self, share):
        self.n = lax.axis_size("tensor")
        self.pieces = [share]
        self.held = {(i, i): 0 for i in range(self.n)}
        self.steps = 0

    def send(self, piece, pairs, order):
        self.pieces.append(lax.ppermute(order(self.pieces[piece]), "tensor", pairs))

    def step(self, order):
        n, s = self.n, self.steps
        self.steps += 1
        before = len(self.pieces)
        if n == 4:
            outer, inner, out = [(0, 1), (1, 0), (2, 3), (3, 2)], [(1, 2), (2, 1)], [(1, 0), (2, 3)]
            for piece, pairs in (((0, outer), (0, inner)), ((2, out), (1, inner)), ((4, out),))[s]:
                self.send(piece, pairs, order)
            owners = ((1, None, 2, None, 3), (0, 2, None, 3, None), (3, 1, None, 0, None), (2, None, 1, None, 0))
            self.held = {(i, i): 0 for i in range(n)} | {
                (i, owner): 1 + k for i, row in enumerate(owners) for k, owner in enumerate(row) if owner is not None
            }
        else:
            up, down = (0, 0) if s == 0 else (before - 2, before - 1)
            self.held.update({(i + 1, i - s): before for i in range(s, n - 1)})
            self.held.update({(i, i + 1 + s): before + 1 for i in range(n - 1 - s)})
            self.send(up, [(i, i + 1) for i in range(s, n - 1)], order)
            self.send(down, [(i + 1, i) for i in range(n - 1 - s)], order)
        return self.pieces[before:]

    def last(self, order):
        got = self.step(order)
        while self.steps < self.n - 1:
            got = self.step(order)
        return got

    def whole(self, mib=14):
        share = self.pieces[0]
        t, width = share.shape
        return prefetched(
            functools.partial(assemble_body, self.held),
            [lax.axis_index("tensor")],
            (self.n,),
            self.pieces,
            [still((t, width), lambda j, me: (0, 0))] * len(self.pieces),
            [sds((t, self.n * width), share.dtype)],
            [pl.BlockSpec((t, width), lambda j, me: (0, j))],
            mib=mib,
            name="assemble",
        )[0]


def steps(order, *ops):
    return [got for op in ops if op.steps < op.n - 1 for got in op.step(order)]


def finish(order, *ops):
    got = steps(order, *ops)
    while any(op.steps < op.n - 1 for op in ops):
        got = steps(order, *ops)
    return got


def scatter_order(n):
    me = lax.axis_index("tensor")
    first = jnp.where(me < n // 2, n - 1, 0)
    return [(first + k) % n for k in range(n)]


class Scatter:
    def __init__(self, first, rest):
        self.n, self.me = lax.axis_size("tensor"), lax.axis_index("tensor")
        self.first, self.rest, self.steps, self.got = first, rest, 0, {}
        self.width = first.shape[1]

    def part(self, owner, *got):
        place = (owner - jnp.where(self.me < self.n // 2, self.n - 1, 0) - 1) % self.n
        place = jnp.clip(place, 0, self.n - 2)
        value = lax.dynamic_slice_in_dim(self.rest, place * self.width, self.width, 1)
        return functools.reduce(add, got, value)

    def any(self, owner, *got):
        first = jnp.where(self.me < self.n // 2, self.n - 1, 0)
        value = jnp.where(owner % self.n == first, self.first, self.part(owner % self.n))
        return functools.reduce(add, got, value)

    def send(self, name, value, pairs, order):
        self.got[name] = lax.ppermute(order(value), "tensor", pairs)

    def step(self, order):
        n, me, s = self.n, self.me, self.steps
        self.got = got = {name: order(value) for name, value in self.got.items()}
        self.steps += 1
        if n == 4:
            inward, inner, outer = [(0, 1), (3, 2)], [(1, 2), (2, 1)], [(0, 1), (1, 0), (2, 3), (3, 2)]
            if s == 0:
                self.send("far", self.first, inward, order)
                return [got["far"]]
            if s == 1:
                self.send("far", add(self.first, got["far"]), inner, order)
                self.send("next", self.part(jnp.where(me == 0, 2, 1)), inward, order)
            else:
                self.send("far", self.part(me ^ 1, got["far"]), outer, order)
                self.send("next", self.part(3 - me, got["next"]), inner, order)
            return [got["far"], got["next"]]
        up, down = ((got["up"],), (got["down"],)) if s else ((), ())
        self.send("up", self.any(me + n - 1 - s, *up), [(i, i + 1) for i in range(s + 1)], order)
        self.send("down", self.any(me - n + 1 + s, *down), [(i + 1, i) for i in range(n - 2 - s, n - 1)], order)
        return [got["up"], got["down"]]

    def last(self, order):
        got = self.step(order)
        while self.steps < self.n - 1:
            got = self.step(order)
        return got

    def total(self, order):
        self.got = {name: order(value) for name, value in self.got.items()}
        own = self.any(self.me) if self.n != 4 else self.part(self.me)
        return sum((g.astype(F32) for g in self.got.values()), own.astype(F32))


def assemble_body(held, me_ref, *refs):
    out_ref, owner, me = refs[-1], pl.program_id(0), me_ref[0]
    for k, ref in enumerate(refs[:-1]):
        places = [(device, o) for (device, o), at in held.items() if at == k]
        here = functools.reduce(jnp.logical_or, [(me == device) & (owner == o) for device, o in places])

        @pl.when(here)
        def _(ref=ref):
            out_ref[...] = ref[...]


def gradients_body(groups, join, which_ref, *refs):
    lefts, rest = refs[: len(groups)], refs[len(groups) :]
    rights, outs = rest[: sum(groups)], rest[sum(groups) :]
    k = 0
    for left, count in zip(lefts, groups):
        turned = left[...].T
        for right in rights[k : k + count]:
            wide = right.shape[1]
            at = k % join * wide
            outs[k // join][:, at : at + wide] = dot(turned, right[...]).astype(BF)
            k += 1


def gradients(which, pairs, name, join=1):
    t = pairs[0][0].shape[0]
    block = 256
    nb = D // 2 // block
    lefts, rights = [left for left, _ in pairs], [right for _, some in pairs for right in some]
    wide = join * rights[0].shape[1]
    return prefetched(
        functools.partial(gradients_body, [len(some) for _, some in pairs], join),
        [which],
        (nb,),
        lefts + rights,
        [pl.BlockSpec((t, block), lambda i, which: (0, which[0] * nb + i))] * len(lefts)
        + [still(right.shape, lambda i, which: (0, 0)) for right in rights],
        [sds((D // 2, wide), BF)] * (len(rights) // join),
        [pl.BlockSpec((block, wide), lambda i, which: (i, 0))] * (len(rights) // join),
        mib=30 if join > 1 else 56,
        name=name,
    )


def mlp_out_body(owners_ref, hidden_ref, weight_ref, first_ref, rest_ref):
    out = dot(hidden_ref[...], weight_ref[...]).astype(BF)

    @pl.when(pl.program_id(0) == 0)
    def _():
        first_ref[...] = out

    @pl.when(pl.program_id(0) > 0)
    def _():
        rest_ref[...] = out


def mlp_out(owners, width, hidden, weight):
    t, units = hidden.shape
    return prefetched(
        mlp_out_body,
        owners,
        (len(owners),),
        [hidden, weight],
        [
            still((t, units), lambda j, owners: (0, 0)),
            pl.BlockSpec((units, width), lambda j, owners: (0, owners[j])),
        ],
        [sds((t, width), BF), sds((t, D - width), BF)],
        [
            pl.BlockSpec((t, width), lambda j, owners: (0, 0)),
            pl.BlockSpec((t, width), lambda j, owners: (0, jnp.maximum(j - 1, 0))),
        ],
        mib=22,
        name="mlp_out",
    )


def swap(value, bit, axis="dp"):
    n = lax.axis_size(axis)
    return lax.ppermute(value, axis, [(i, i ^ (1 << bit)) for i in range(n)])


def split_body(groups, bits_ref, *refs):
    parts, outs = refs[: 4 * groups], refs[4 * groups :]
    for part in range(2):
        for phase in range(2):

            @pl.when(pl.program_id(0) == phase)
            def _(part=part, phase=phase):
                at = 0
                for g in range(groups):
                    keep, got = parts[2 * (part * groups + g)], parts[2 * (part * groups + g) + 1]
                    wide = keep.shape[1]
                    outs[2 * part + phase][:, at : at + wide] = add(keep[...], got[...])
                    at += wide


def split(upper, lower, bits, joined):
    groups = len(upper)
    rows = upper[0][0].shape[0] // (4 if joined else 2)
    columns = sum(keep.shape[1] for keep, _ in upper)
    block = min(64 if columns > D else 128, rows)
    nb = rows // block
    ins, in_specs = [], []
    for part, pairs in enumerate((upper, lower)):
        first = 2 * nb * part if joined else 0

        def index(phase, j, bits, part=part, first=first):
            half = jnp.where(phase == 0, 1 - bits[part], bits[part])
            return (first + half * nb + j, 0)

        for pair in pairs:
            for array in pair:
                ins.append(array)
                in_specs.append(pl.BlockSpec((block, array.shape[1]), index))
    given = pl.BlockSpec((block, columns), lambda phase, j, bits: (jnp.where(phase == 0, j, nb - 1), 0))
    kept = pl.BlockSpec((block, columns), lambda phase, j, bits: (jnp.where(phase == 0, 0, j), 0))
    return prefetched(
        functools.partial(split_body, groups),
        bits,
        (2, nb),
        ins,
        in_specs,
        [sds((rows, columns), BF)] * 4,
        [given, kept] * 2,
        mib=56 if groups > 2 else 28,
        name="split",
    )


def merge_body(widths, bits_ref, *refs):
    for part in range(2):
        for which in range(2):

            @pl.when((pl.program_id(0) == bits_ref[part]) == (which == 0))
            def _(part=part, which=which):
                value = refs[2 * part + which][...]
                if widths:
                    at = 0
                    for out, wide in zip(refs[4:], widths):
                        out[part] = value[:, at : at + wide]
                        at += wide
                else:
                    refs[4 + part][...] = value


def merge(upper, lower, bits, widths=()):
    rows, columns = upper[0].shape
    block = min(64 if columns > D else 128, rows)
    nb = rows // block

    def spec(part, which):
        def index(i, j, bits):
            half = bits[part] if which == 0 else 1 - bits[part]
            return (jnp.where(i == half, j, jnp.where(i < half, 0, nb - 1)), 0)

        return pl.BlockSpec((block, columns), index)

    if widths:
        outs = [sds((2, 2 * rows, wide), BF) for wide in widths]
        out_specs = [pl.BlockSpec((2, block, wide), lambda i, j, bits: (0, i * nb + j, 0)) for wide in widths]
    else:
        outs = [sds((2 * rows, columns), BF)] * 2
        out_specs = [pl.BlockSpec((block, columns), lambda i, j, bits: (i * nb + j, 0))] * 2
    return prefetched(
        functools.partial(merge_body, widths),
        bits,
        (2, nb),
        [*upper, *lower],
        [spec(part, which) for part in range(2) for which in range(2)],
        outs,
        out_specs,
        mib=56 if widths and columns > D else 22,
        name="merge",
    )


def sum_over_dp(given, order):
    me, n = lax.axis_index("dp"), lax.axis_size("dp")
    count = n.bit_length() - 1
    bit = lambda b: (me >> b) & 1
    orders = [list(range(1, count)), list(range(count - 1, 0, -1))]
    got = [swap(g, 0) for g in given]
    kept = yield got
    upper = lower = [(order(k), g) for k, g in zip(kept, got)]
    for s in range(count - 1):
        a, b = orders[0][s], orders[1][s]
        p_give, p_keep, q_give, q_keep = split(upper, lower, [bit(a), bit(b)], s == 0)
        upper, lower = [(p_keep, swap(p_give, a))], [(q_keep, swap(q_give, b))]
        yield p_keep
        upper, lower = [(order(upper[0][0]), upper[0][1])], [(order(lower[0][0]), lower[0][1])]
    p, q = add(*upper[0]), add(*lower[0])
    for s in reversed(range(count - 1)):
        a, b = orders[0][s], orders[1][s]
        p, q = lax.optimization_barrier((p, q))
        got = swap(p, a), swap(q, b)
        yield p
        out = merge([order(p), got[0]], [q, got[1]], [bit(a), bit(b)], () if s else [g.shape[1] for g in given])
        if s:
            p, q = out
    own = [array.reshape(-1, array.shape[2]) for array in out]
    other = [swap(array, 0) for array in own]
    yield own[0]
    yield own, other


def finish_sum(steps_left):
    *_, last = steps_left
    return last


def halves(core, own, other, nb):
    def index(mine):
        def of(i, bits):
            half = bits[0] if mine else 1 - bits[0]
            return (jnp.clip(i - half * nb, 0, nb - 1), 0)

        return of

    return index(True), index(False)


def halves_body(store, core_ref, *refs):
    half = pl.program_id(0) // (pl.num_programs(0) // 2)
    groups = store.groups
    own, other, outs = refs[:groups], refs[groups : 2 * groups], refs[2 * groups :]
    for arrays, mine in ((own, True), (other, False)):

        @pl.when((half == core_ref[0]) == mine)
        def _(arrays=arrays):
            store(arrays, outs)


def from_halves(store, core, own, other, outs, out_specs, block, mib, name):
    store.groups = len(own)
    nb = own[0].shape[0] // block
    return prefetched(
        functools.partial(halves_body, store),
        [core],
        (2 * nb,),
        [*own, *other],
        [
            pl.BlockSpec((block, array.shape[1]), index)
            for arrays, index in zip((own, other), halves(core, own, other, nb))
            for array in arrays
        ],
        outs,
        out_specs,
        mib=mib,
        name=name,
    )


def gate_up_out(core, own, other):
    def store(arrays, outs):
        for k in range(2):
            outs[0][:, k, :] = arrays[k][...].astype(F32)

    units, block = own[0].shape[1], 256
    outs, spec = [sds((D, 2, units), F32)], [pl.BlockSpec((block, 2, units), lambda i, c: (i, 0, 0))]
    return from_halves(store, core, own, other, outs, spec, block, 56, "gate_up_out")[0]


def down_out(core, own, other):
    def store(arrays, outs):
        outs[0][...] = arrays[0][...].astype(F32).T

    units, block = own[0].shape[1], 256
    outs, spec = [sds((units, D), F32)], [pl.BlockSpec((units, block), lambda i, c: (0, i))]
    return from_halves(store, core, own, other, outs, spec, block, 56, "down_out")[0]


def attention_out(core, own, other):
    def store(arrays, outs):
        for k in range(3):
            outs[0][k] = arrays[0][:, k * width : (k + 1) * width].astype(F32)
        outs[1][...] = arrays[0][:, 3 * width :].astype(F32).T

    width, block = own[0].shape[1] // 4, 256
    outs = [sds((3, D, width), F32), sds((width, D), F32)]
    specs = [
        pl.BlockSpec((3, block, width), lambda i, c: (0, i, 0)),
        pl.BlockSpec((width, block), lambda i, c: (0, i)),
    ]
    return from_halves(store, core, own, other, outs, specs, block, 22, "attention_out")


def per_device(
    tokens,
    norm_one_gain,
    norm_one_shift,
    project_weight,
    project_bias,
    output_weight,
    norm_two_gain,
    norm_two_shift,
    gate_up_weight,
    down_weight,
    cotangent,
):
    width = tokens.shape[1]
    t = tokens.shape[0] // CHUNKS
    offset = lax.axis_index("tensor") * width
    core = lax.axis_index("dp") & 1
    mine = lambda full: lax.dynamic_slice_in_dim(full, offset, width, full.ndim - 1)
    half_of = lambda array, which: lax.dynamic_slice_in_dim(array, which * (D // 2), D // 2, 1)
    order = Order()

    small = jnp.stack([norm_one_gain, norm_one_shift, norm_two_gain, norm_two_shift])
    whole_x = Gather(jnp.concatenate([tokens, jnp.pad(small, ((0, EXTRA - 4), (0, 0)))]))
    whole_up = Gather(cotangent)
    got = whole_x.step(order)
    gate_w = order(gate_up_weight)[:, 0]
    order.done(*got, gate_w)
    got = whole_x.step(order)
    up_w = order(gate_up_weight)[:, 1]
    tables = rope_tables()
    order.done(*got, up_w, tables)
    whole_x.last(order)
    x = whole_x.whole()
    gain_one, gain_two, shift_two = (x[t + i : t + i + 1].astype(F32) for i in (0, 2, 3))
    project_w = project_weight.transpose(1, 0, 2)
    bias = project_bias.astype(F32)[:, None, :]

    through = lambda row: jnp.einsum("d,kdc->kc", row[0].astype(BF), project_w, preferred_element_type=F32)
    with_rows = jnp.stack([through(gain_one), through(x[t + 1 : t + 2]) + bias[:, 0]])

    order.done(x)
    got = whole_up.step(order)
    normed_one, stats_one, heads = project(0, x, project_w, bias, tables, ())
    order.done(*got, stats_one)
    owners = scatter_order(whole_up.n)
    first, rest, context, lse = attend(owners, order(heads), output_weight)
    order.done(lse)
    branch = Scatter(first, rest)
    for _ in range(2):
        order.done(*whole_up.step(order), *branch.step(order), with_rows)
    if whole_up.n > 4:
        whole_up.last(order)
    branch.last(order)
    upstream = whole_up.whole()
    middle_share = tokens.astype(F32) + branch.total(order)
    middle_sent = (middle_share - stats_one[:, 0:1]).astype(BF)
    order.done(middle_sent)
    whole_middle = Gather(middle_sent)
    while whole_middle.steps < whole_middle.n - 1:
        whole_middle.step(order)
    middle = whole_middle.whole()

    normed_two, stats_two, hidden, dgate, dup = mlp(
        0, middle, upstream, gain_two, shift_two, gate_w, up_w, down_weight, ()
    )
    first = mlp_back(owners[:1], width, dgate, dup, gate_w, up_w)
    rest = mlp_back(owners[1:], width, after(dgate, first), dup, gate_w, up_w)
    order.done(first)
    delta_two = Scatter(first, rest)
    got = steps(order, delta_two)
    order.done(rest, *got)
    got = steps(order, delta_two)
    mlp_grads = lambda which, name: gradients(
        which, [(normed_two, [order(dgate), dup]), (upstream, [hidden])], name
    )
    mlp_given = mlp_grads(1 - core, "mlp_given")
    mlp_sum = sum_over_dp(mlp_given, order)
    next(mlp_sum)
    order.done(*got, *mlp_given)
    got = finish(order, delta_two)
    mlp_kept = mlp_grads(core, "mlp_kept")
    order.done(*got, *mlp_kept)
    delta_two = delta_two.total(order)
    unit_two = (mine(middle).astype(F32) - stats_two[:, 0:1]) * stats_two[:, 1:2]
    two_grads = [jnp.sum(delta_two * unit_two, axis=0), jnp.sum(delta_two, axis=0)]
    e_own = delta_two * norm_two_gain.astype(F32)
    e_sent = e_own.astype(BF)
    order.done(e_sent)
    whole_e = Gather(e_sent)
    got = steps(order, whole_e)
    held = mlp_sum.send(mlp_kept)
    order.done(*got, held)
    got = steps(order, whole_e)
    mlp_share = Scatter(*mlp_out(owners, width, order(hidden), down_weight))
    order.done(*got, mlp_share.rest)
    got = finish(order, whole_e) + steps(order, mlp_share)
    held = next(mlp_sum)
    e = whole_e.whole()

    order.done(e, held, *got)
    share_got = steps(order, mlp_share)
    means_two, dbranch, dctx = branch_back(order(e), middle, stats_two, upstream, output_weight)
    order.done(dctx)
    held = next(mlp_sum)
    order.done(held)
    dq, dk, dv, sums = attend_back(heads, lse, context, order(dctx), tables, with_rows)
    held = next(mlp_sum)
    order.done(dq, held, *share_got)
    delta_heads = (dq, dk, dv)
    sum_rows = 2 * t // width
    below = jnp.pad(sums[:2].reshape(sum_rows, width), ((2, EXTRA - 2 - sum_rows), (0, 0)))
    back = lambda owners, dq: project_back(owners, dq, dk, dv, project_w, x, stats_one, below)
    first = back(owners[:1], order(dq))
    rest = back(owners[1:], after(dq, first))
    order.done(first)
    delta_one = Scatter(first, rest)
    got = steps(order, delta_one)
    order.done(rest)
    attention_grads = lambda which, name: gradients(
        which, [(normed_one, [order(dq), dk, dv]), (dbranch, [context])], name, join=4
    )
    attention_given = attention_grads(1 - core, "attention_given")
    attention_sum = sum_over_dp(attention_given, order)
    next(attention_sum)
    order.done(*attention_given, *got)
    got = steps(order, delta_one)
    attention_kept = attention_grads(core, "attention_kept")
    order.done(*attention_kept)
    held = attention_sum.send(attention_kept)
    order.done(held, *got)
    got = finish(order, delta_one)
    held = next(mlp_sum)
    order.done(held)
    held = next(attention_sum)
    order.done(held, *got)
    held = next(attention_sum)
    order.done(held)
    if lax.axis_size("dp") > 8:
        for _ in range(2):
            order.done(next(mlp_sum))
            order.done(next(attention_sum))
    mlp_halves = next(mlp_sum)
    down_grad = down_out(core, [order(mlp_halves[0][2])], mlp_halves[1][2:])
    order.done(down_grad, *got)
    held = next(attention_sum)
    order.done(held)
    share_got = finish(order, mlp_share)
    gate_up_grad = gate_up_out(core, [order(mlp_halves[0][0]), mlp_halves[0][1]], mlp_halves[1][:2])
    order.done(gate_up_grad)
    delta_one = delta_one.total(order)
    bias_grad = [jnp.sum(a, axis=0, dtype=F32) for a in delta_heads]
    small = jnp.stack([delta_one[t], delta_one[t + 1], *two_grads, *bias_grad])
    small = small + swap(small, 0)
    sums = (delta_one[t + 2 : t + 2 + sum_rows] / D).reshape(2, t).T
    unit_one = (tokens.astype(F32) - stats_one[:, 0:1]) * stats_one[:, 1:2]
    dmid = cotangent.astype(F32) + stats_two[:, 1:2] * (e_own - means_two[:, 0:1] - unit_two * means_two[:, 1:2])
    tokens_grad = order(dmid) + stats_one[:, 1:2] * (
        delta_one[:t] * norm_one_gain.astype(F32) - sums[:, 0:1] - unit_one * sums[:, 1:2]
    )
    order.done(small, tokens_grad, *share_got)
    held = next(attention_sum)
    order.done(held)
    devices = lax.axis_size("dp")
    others = [lax.ppermute(order(small), "dp", [(i, i ^ k) for i in range(devices)]) for k in range(2, devices, 2)]
    result = (middle_share + mlp_share.total(order)).astype(BF)
    small = sum((order(other) for other in others), small)
    order.done(tokens_grad, small, result)
    attention_halves = next(attention_sum)
    project_grad, output_grad = attention_out(
        core, [order(attention_halves[0][0]), *attention_halves[0][1:]], attention_halves[1]
    )
    return (
        result,
        tokens_grad,
        small[0],
        small[1],
        project_grad.transpose(1, 0, 2),
        small[4:7],
        output_grad,
        small[2],
        small[3],
        gate_up_grad,
        down_grad,
    )


def solution(mesh):
    return jax.shard_map(
        per_device,
        mesh=mesh,
        in_specs=(
            P("dp", "tensor"),
            P("tensor"),
            P("tensor"),
            P(None, None, "tensor"),
            P(None, "tensor"),
            P("tensor", None),
            P("tensor"),
            P("tensor"),
            P(None, None, "tensor"),
            P("tensor", None),
            P("dp", "tensor"),
        ),
        out_specs=(
            P("dp", "tensor"),
            P("dp", "tensor"),
            P("tensor"),
            P("tensor"),
            P(None, None, "tensor"),
            P(None, "tensor"),
            P("tensor", None),
            P("tensor"),
            P("tensor"),
            P(None, None, "tensor"),
            P("tensor", None),
        ),
        check_vma=False,
    )
```
